128 devices in a mesh: tile: 8 (over y_lo, z), sub: 16 (over y_hi, x, core).
Axes of the slice: x: 4, y: 4 (y_hi: 2, y_lo: 2; y = y_hi * 2 + y_lo), z: 4, core: 2. Of those that a mesh axis runs over, the one named last changes fastest.
Arguments:
- initial: float32 [64, 128, 4096], P(None, 'tile', 'sub'), may hold values from -6 to 6
- targets: float32 [64, 128, 4096], P(None, 'tile', 'sub'), may hold values from -6 to 6
- diffusivity: float32 [128, 4096], P('tile', 'sub'), may hold values from 0.02 to 0.24
- column_order: int32 [128, 4096], P(('tile', 'sub')), may hold values from 0 to 4095, each once within a row
- send_counts: int32 [128, 128], P(('tile', 'sub')), may hold values from 0 to 64, as said below
- w_first: bfloat16 [16, 64, 192], P('sub'), may hold values from -0.75 to 0.75
- w_inner: bfloat16 [16, 3, 192, 192], P('sub'), may hold values from -0.4375 to 0.4375
- w_last: bfloat16 [16, 192, 64], P('sub'), may hold values from -0.4375 to 0.4375
- b_inner: float32 [16, 4, 192], P('sub'), may hold values from -2 to 2
- b_last: float32 [16, 64], P('sub'), may hold values from -2 to 2
Outputs:
- grad_initial: float32 [64, 128, 4096], P(None, 'tile', 'sub')
- step_first: float32 [16, 64, 192], P('sub')
- step_inner: float32 [16, 3, 192, 192], P('sub')
- step_last: float32 [16, 192, 64], P('sub')
- step_bias_inner: float32 [16, 4, 192], P('sub')
- step_bias_last: float32 [16, 64], P('sub')
The draws below stay inside these ranges and needn't reach their ends.
Inputs may be any that keep to these rules, and one draw needn't show every extreme that they name: `send_counts`: each row sums to 4096. For every pair of destinations d and d plus half of 128 (same sub index, tile indices half the tile axis apart) the two entries of a row sum to 64; some destination receives 64 from every device.
All inputs are finite; a program needn't handle non-finite values.
Results may differ from the reference program's by a relative error of at most 0.0095.
Values may be sent and summed in bfloat16 or wider, within the bound.
A program may use at most 64 MiB of HBM per device.

```python
import math
import jax
import jax.numpy as jnp
from jax import lax

LEV = 64
WIDTH = 192
CX = 16
CY = 256
STEPS = 2
NCOL = 4096
NX = 128
NY = 4096
CAP = 64
EXPERTS = 16
N_TILE = 8
N_SUB = 16
DEVICES = 128


def draw_send_counts(key, part):
    half_count = DEVICES // 2
    first_key, second_key = jax.random.split(jax.random.fold_in(key, 11))
    first_share = jax.random.randint(first_key, (DEVICES, half_count), 0, CAP + 1)
    pair_order = jax.random.permutation(second_key, half_count)
    hot_pairs = pair_order < max(1, DEVICES // 16)
    first_share = jnp.where(hot_pairs[None, :], CAP, first_share)
    return jnp.concatenate([first_share, CAP - first_share], axis=1).astype(jnp.int32)


def steps_of(key, dims, cuts, smallest, high):
    factor_of, own = 1.0, jax.random.fold_in(key, 6)
    for dim, shards_of in cuts:
        draws = jnp.exp(jax.random.uniform(jax.random.fold_in(own, dim), (shards_of,), jnp.float32, smallest / len(cuts), high / len(cuts)))
        factor_of = factor_of * jnp.repeat(draws, dims[dim] // shards_of).reshape([-1 if axis == dim else 1 for axis in range(len(dims))])
    return factor_of


def scatter_about(rng, extent, deviation, reach, cuts=(), kind=jnp.bfloat16):
    array = deviation * jax.random.normal(rng, extent, jnp.float32)
    if cuts:
        array = array * steps_of(rng, extent, cuts, -0.22, 0.18)
    return jnp.clip(array, -reach, reach).astype(kind)


def setup_inputs(seed: int = 0) -> dict:
    key_of = jax.random.split(jax.random.key(seed), 11)
    initial = scatter_about(key_of[0], (LEV, NX, NY), 1.0, 6.0, ((1, 8), (2, 16)), jnp.float32)
    targets = scatter_about(key_of[1], (LEV, NX, NY), 1.0, 6.0, ((1, 8), (2, 16)), jnp.float32)
    diffusivity = jnp.clip(jnp.exp(math.log(0.24) - 2.4849066 * jax.random.uniform(key_of[2], (NX, NY), jnp.float32) ** steps_of(key_of[2], (NX, NY), ((0, 8), (1, 16)), -0.2, 0.2)), 0.02, 0.24)
    column_order = jax.vmap(lambda own: jax.random.permutation(own, NCOL))(jax.random.split(key_of[3], DEVICES)).reshape((DEVICES, NCOL)).astype(jnp.int32)
    send_counts = draw_send_counts(jax.random.fold_in(key_of[10], 71), 0)
    w_first = scatter_about(key_of[5], (EXPERTS, LEV, WIDTH), LEV ** -0.5, 0.75, ((0, 16),))
    w_inner = scatter_about(key_of[6], (EXPERTS, 3, WIDTH, WIDTH), WIDTH ** -0.5, 0.4375, ((0, 16),))
    w_last = scatter_about(key_of[7], (EXPERTS, WIDTH, LEV), WIDTH ** -0.5, 0.4375, ((0, 16),))
    b_inner = scatter_about(key_of[8], (EXPERTS, 4, WIDTH), 0.3, 2.0, ((0, 16),), jnp.float32)
    b_last = scatter_about(key_of[9], (EXPERTS, LEV), 0.3, 2.0, ((0, 16),), jnp.float32)
    return {"initial": initial, "targets": targets, "diffusivity": diffusivity, "column_order": column_order, "send_counts": send_counts, "w_first": w_first, "w_inner": w_inner, "w_last": w_last, "b_inner": b_inner, "b_last": b_last}


def laplace(quantity):
    near = jnp.roll(quantity, 1, 1) + jnp.roll(quantity, -1, 1)
    near = near + jnp.roll(quantity, 1, 2) + jnp.roll(quantity, -1, 2)
    return near - 4.0 * quantity

def silu_slope(preact):
    sigmoid_value = jax.nn.sigmoid(preact)
    return sigmoid_value * (1.0 + preact * (1.0 - sigmoid_value))

def run_network(inputs, misfit, usable, w_first, w_inner, w_last, b_inner, b_last):
    layers = [w_first, w_inner[0], w_inner[1], w_inner[2]]
    feeds = [inputs]
    preacts = []
    current = inputs
    for layer_index in range(4):
        preact = jnp.dot(current, layers[layer_index], preferred_element_type=jnp.float32) + b_inner[layer_index]
        preacts.append(preact)
        current = jax.nn.silu(preact).astype(jnp.bfloat16)
        feeds.append(current)
    output = jnp.dot(current, w_last, preferred_element_type=jnp.float32) + b_last
    residue = (misfit.astype(jnp.float32) + output) * usable[:, None]
    error_bf = residue.astype(jnp.bfloat16)
    grad_last = jnp.dot(current.T, error_bf, preferred_element_type=jnp.float32)
    bias_last = lax.optimization_barrier(jnp.sum(error_bf.astype(jnp.float32), axis=0))
    carried = jnp.dot(error_bf, w_last.T, preferred_element_type=jnp.float32)
    weight_grads = [None, None, None, None]
    bias_grads = [None, None, None, None]
    for layer_index in (3, 2, 1, 0):
        error_bf = (carried * silu_slope(preacts[layer_index])).astype(jnp.bfloat16)
        weight_grads[layer_index] = jnp.dot(feeds[layer_index].T, error_bf, preferred_element_type=jnp.float32)
        bias_grads[layer_index] = lax.optimization_barrier(jnp.sum(error_bf.astype(jnp.float32), axis=0))
        carried = jnp.dot(error_bf, layers[layer_index].T, preferred_element_type=jnp.float32)
    returned_grad = (residue + carried).astype(jnp.bfloat16)
    gradients = (weight_grads[0], jnp.stack(weight_grads[1:]), grad_last, jnp.stack(bias_grads), bias_last)
    return (returned_grad, gradients)

def normalize(gradients):
    total = 0.0
    count = 0
    for member in gradients:
        total = total + lax.optimization_barrier(jnp.sum(member * member, axis=tuple(range(1, member.ndim))))
        count = count + member[0].size
    factor = 1.0 / jnp.sqrt(total / count + 1e-06)
    return tuple((member * factor.reshape((-1,) + (1,) * (member.ndim - 1)) for member in gradients))

def to_columns(grid_field):
    shaped = grid_field.reshape(LEV, N_TILE, CX, N_SUB, CY).transpose(1, 3, 2, 4, 0)
    return shaped.reshape(DEVICES, NCOL, LEV)

def from_columns(column_data):
    shaped = column_data.reshape(N_TILE, N_SUB, CX, CY, LEV).transpose(4, 0, 2, 1, 3)
    return shaped.reshape(LEV, NX, NY)

def reference(initial, targets, diffusivity, column_order, send_counts, w_first, w_inner, w_last, b_inner, b_last):
    grid_field = initial
    for iteration in range(STEPS):
        grid_field = grid_field + diffusivity[None] * laplace(grid_field)
    inputs = to_columns(grid_field).astype(jnp.bfloat16)
    misfit = to_columns(grid_field - targets).astype(jnp.bfloat16)
    packed = jnp.concatenate([inputs, misfit], axis=2)
    ordered = jnp.take_along_axis(packed, column_order.astype(jnp.int32)[:, :, None], axis=1)
    counts = send_counts.astype(jnp.int32)
    starts = (jnp.cumsum(counts, axis=1) - counts).astype(jnp.int32)
    slot_ids = jnp.arange(CAP, dtype=jnp.int32)

    def per_target(target_dev):
        position = starts[:, target_dev][:, None] + slot_ids[None, :]
        usable = slot_ids[None, :] < counts[:, target_dev][:, None]
        clipped = jnp.minimum(position, NCOL - 1).astype(jnp.int32)
        row_data = jnp.take_along_axis(ordered, clipped[:, :, None], axis=1)
        row_data = jnp.where(usable[:, :, None], row_data, jnp.zeros_like(row_data))
        network_id = target_dev % N_SUB
        flat = row_data.reshape(DEVICES * CAP, 2 * LEV)
        returned_grad, gradients = run_network(flat[:, :LEV], flat[:, LEV:], usable.reshape(-1).astype(jnp.float32), w_first[network_id], w_inner[network_id], w_last[network_id], b_inner[network_id], b_last[network_id])
        return (returned_grad.reshape(DEVICES, CAP, LEV), gradients)
    answers, gradients = lax.map(per_target, jnp.arange(DEVICES, dtype=jnp.int32))
    gradients = tuple((member.reshape((N_TILE, N_SUB) + member.shape[1:]).sum(axis=0) for member in gradients))
    steps_out = normalize(gradients)
    position = starts[:, :, None] + slot_ids[None, None, :]
    usable = slot_ids[None, None, :] < counts[:, :, None]
    slot_index = jnp.where(usable, position, NCOL).astype(jnp.int32)
    source_ids = jnp.arange(DEVICES, dtype=jnp.int32)[:, None, None]
    values = answers.transpose(1, 0, 2, 3).astype(jnp.float32)
    ordered_back = jnp.zeros((DEVICES, NCOL + 1, LEV), jnp.float32).at[source_ids, slot_index].set(values)[:, :NCOL]
    column_back = jnp.zeros((DEVICES, NCOL, LEV), jnp.float32).at[jnp.arange(DEVICES, dtype=jnp.int32)[:, None], column_order.astype(jnp.int32)].set(ordered_back)
    cotangent = from_columns(column_back)
    for iteration in range(STEPS):
        cotangent = cotangent + laplace(diffusivity[None] * cotangent)
    return (cotangent, steps_out[0], steps_out[1], steps_out[2], steps_out[3], steps_out[4])
```

```python
import jax
import jax.numpy as jnp
from jax import lax
from jax.sharding import PartitionSpec as P

STEPS = 2


def extended(cells, sides, width):
    for axis, dim in sides:
        count = lax.axis_size(axis)
        head = lax.slice_in_dim(cells, 0, width, axis=dim)
        tail = lax.slice_in_dim(cells, cells.shape[dim] - width, cells.shape[dim], axis=dim)
        cells = jnp.concatenate(
            [
                lax.ppermute(tail, axis, [(i, (i + 1) % count) for i in range(count)]),
                cells,
                lax.ppermute(head, axis, [((i + 1) % count, i) for i in range(count)]),
            ],
            axis=dim,
        )
    return cells


def laplace(quantity):
    padded = extended(quantity, (("tile", 1), ("sub", 2)), 1)
    center = padded[:, 1:-1, 1:-1]
    near = padded[:, 2:, 1:-1] + padded[:, :-2, 1:-1] + padded[:, 1:-1, 2:] + padded[:, 1:-1, :-2]
    return near - 4.0 * center


def silu_slope(preact):
    sigmoid_value = jax.nn.sigmoid(preact)
    return sigmoid_value * (1.0 + preact * (1.0 - sigmoid_value))


def run_network(inputs, misfit, w_first, w_inner, w_last, b_inner, b_last):
    layers = [w_first, w_inner[0], w_inner[1], w_inner[2]]
    feeds = [inputs]
    preacts = []
    current = inputs
    for layer_index in range(4):
        preact = (
            jnp.dot(current, layers[layer_index], preferred_element_type=jnp.float32)
            + b_inner[layer_index]
        )
        preacts.append(preact)
        current = jax.nn.silu(preact).astype(jnp.bfloat16)
        feeds.append(current)
    output = jnp.dot(current, w_last, preferred_element_type=jnp.float32) + b_last
    residue = misfit.astype(jnp.float32) + output
    error_bf = residue.astype(jnp.bfloat16)
    grad_last = jnp.dot(current.T, error_bf, preferred_element_type=jnp.float32)
    bias_last = jnp.sum(error_bf.astype(jnp.float32), axis=0)
    carried = jnp.dot(error_bf, w_last.T, preferred_element_type=jnp.float32)
    weight_grads = [None, None, None, None]
    bias_grads = [None, None, None, None]
    for layer_index in (3, 2, 1, 0):
        error_bf = (carried * silu_slope(preacts[layer_index])).astype(jnp.bfloat16)
        weight_grads[layer_index] = jnp.dot(
            feeds[layer_index].T, error_bf, preferred_element_type=jnp.float32
        )
        bias_grads[layer_index] = jnp.sum(error_bf.astype(jnp.float32), axis=0)
        carried = jnp.dot(error_bf, layers[layer_index].T, preferred_element_type=jnp.float32)
    returned_grad = (residue + carried).astype(jnp.bfloat16)
    gradients = (
        weight_grads[0],
        jnp.stack(weight_grads[1:]),
        grad_last,
        jnp.stack(bias_grads),
        bias_last,
    )
    return (returned_grad, gradients)


def normalize(gradients):
    total = 0.0
    count = 0
    for member in gradients:
        total = total + jnp.sum(member * member, axis=tuple(range(1, member.ndim)))
        count = count + member[0].size
    factor = 1.0 / jnp.sqrt(total / count + 1e-06)
    return tuple(
        (member * factor.reshape((-1,) + (1,) * (member.ndim - 1)) for member in gradients)
    )


def per_device(
    initial,
    targets,
    diffusivity,
    column_order,
    send_counts,
    w_first,
    w_inner,
    w_last,
    b_inner,
    b_last,
):
    levels, width_x, width_y = initial.shape
    column_count = width_x * width_y
    devices = send_counts.shape[1]
    grid_field = initial
    for iteration in range(STEPS):
        grid_field = grid_field + diffusivity[None] * laplace(grid_field)
    inputs = grid_field.reshape(levels, column_count).T.astype(jnp.bfloat16)
    misfit = (grid_field - targets).reshape(levels, column_count).T.astype(jnp.bfloat16)
    packed = jnp.concatenate([inputs, misfit], axis=1)
    ordered = packed[column_order[0]]
    counts_row = send_counts[0]
    networks = lax.axis_size("sub")
    share = column_count // networks
    device_ids = jnp.arange(devices, dtype=jnp.int32)
    earlier = device_ids[None, :] < device_ids[:, None]
    starts = jnp.sum(jnp.where(earlier, counts_row[None, :], 0), axis=1)
    by_network = counts_row.reshape(-1, networks).T.reshape(-1)
    slot_starts = jnp.sum(jnp.where(earlier, by_network[None, :], 0), axis=1)
    shift = starts.reshape(-1, networks).T.reshape(-1) - slot_starts
    change = shift - jnp.concatenate([jnp.zeros((1,), jnp.int32), shift[:-1]])
    slots = jnp.arange(column_count, dtype=jnp.int32)
    position = slots + jnp.sum(
        jnp.where(slot_starts[None, :] <= slots[:, None], change[None, :], 0), axis=1
    )
    outgoing = ordered[position].reshape(networks, share * 2 * levels)
    incoming = lax.all_to_all(outgoing, "sub", split_axis=0, concat_axis=0, tiled=True)
    received = incoming.reshape(column_count, 2 * levels)
    returned_grad, gradients = run_network(
        received[:, :levels],
        received[:, levels:],
        w_first[0],
        w_inner[0],
        w_last[0],
        b_inner[0],
        b_last[0],
    )
    returning = returned_grad.reshape(networks, share * levels)
    answers = lax.all_to_all(returning, "sub", split_axis=0, concat_axis=0, tiled=True)
    answer_rows = answers.reshape(column_count, levels).astype(jnp.float32)
    ordered_back = jnp.zeros((column_count, levels), jnp.float32).at[position].set(answer_rows)
    flat = jnp.concatenate([member.reshape(-1).astype(jnp.bfloat16) for member in gradients])
    flat = lax.psum(flat, "tile").astype(jnp.float32)
    summed = []
    first = 0
    for member in gradients:
        summed.append(flat[first : first + member.size].reshape(member.shape))
        first += member.size
    steps_out = normalize(tuple((member[None] for member in summed)))
    column_back = (
        jnp.zeros((column_count, levels), jnp.float32).at[column_order[0]].set(ordered_back)
    )
    cotangent = column_back.T.reshape(levels, width_x, width_y)
    for iteration in range(STEPS):
        cotangent = cotangent + laplace(diffusivity[None] * cotangent)
    return (cotangent, steps_out[0], steps_out[1], steps_out[2], steps_out[3], steps_out[4])


def solution(mesh):
    placed = (
        P(None, "tile", "sub"),
        P(None, "tile", "sub"),
        P("tile", "sub"),
        P(("tile", "sub"), None),
        P(("tile", "sub"), None),
        P("sub", None, None),
        P("sub", None, None, None),
        P("sub", None, None),
        P("sub", None, None),
        P("sub", None),
    )
    return jax.shard_map(
        per_device,
        mesh=mesh,
        in_specs=placed,
        out_specs=(
            P(None, "tile", "sub"),
            P("sub", None, None),
            P("sub", None, None, None),
            P("sub", None, None),
            P("sub", None, None),
            P("sub", None),
        ),
        check_vma=False,
    )
```

```python
import functools
import jax
import jax.numpy as jnp
from jax import lax
from jax.experimental import pallas as pl
from jax.experimental.pallas import tpu as pltpu
from jax.sharding import PartitionSpec as P

MESH = pl.DeviceIdType.MESH
F32 = jnp.float32
BF16 = jnp.bfloat16
LEV = 64
WIDTH = 192
CX = 16
CY = 256
NCOL = CX * CY
TILES = 8
SUBS = 16
SHARE = NCOL // SUBS
PARAMS = 136000
AUG = 16
PAD = 8
ROWS_Y = CY + 2 * PAD
CHUNK = 96
GRAD_ROWS = CHUNK * TILES
FIRST_INNER = LEV + AUG
FIRST_LAST = FIRST_INNER + 3 * (WIDTH + AUG)
VMEM = pl.BlockSpec(memory_space=pltpu.VMEM)
SMEM = pl.BlockSpec(memory_space=pltpu.SMEM)
LIMIT = 58 * 2**20


def wrapped(index, step, count):
    return lax.rem(index + step + count, count)


def greet(peers):
    barrier = pltpu.get_barrier_semaphore()
    for peer in peers:
        pl.semaphore_signal(barrier, inc=1, device_id=peer, device_id_type=MESH)
    pl.semaphore_wait(barrier, len(peers))


def remote(source, target, send_sem, recv_sem, peer):
    return pltpu.make_async_remote_copy(
        src_ref=source,
        dst_ref=target,
        send_sem=send_sem,
        recv_sem=recv_sem,
        device_id=peer,
        device_id_type=MESH,
    )


def neighbours():
    tile, sub = lax.axis_index("tile"), lax.axis_index("sub")
    up, down = wrapped(tile, 1, TILES), wrapped(tile, -1, TILES)
    right, left = wrapped(sub, 1, SUBS), wrapped(sub, -1, SUBS)
    return (
        (down, sub),
        (up, sub),
        (tile, left),
        (tile, right),
        (down, left),
        (down, right),
        (up, left),
        (up, right),
    )


def tiled(block):
    return block.reshape(LEV, CX // 8, 8, 2, 128).transpose(0, 1, 3, 2, 4).reshape(-1, 128)


def untiled(rows):
    return rows.reshape(LEV, CX // 8, 2, 8, 128).transpose(0, 1, 3, 2, 4).reshape(LEV, CX, CY)


def tiled_row(x, half):
    return (x // 8) * 16 + half * 8 + x % 8


def low_lanes(shape):
    return lax.broadcasted_iota(jnp.int32, shape, 1) < LEV


def five_point(ref, x, start, count):
    middle = ref[x, pl.ds(start, count), :]
    near = ref[x - 1, pl.ds(start, count), :] + ref[x + 1, pl.ds(start, count), :]
    near = near + ref[x, pl.ds(start - 1, count), :] + ref[x, pl.ds(start + 1, count), :]
    return middle, near - 4.0 * middle


def forward_kernel(
    initial, targets, diffusivity,
    columns, rates,
    field, middle, x_send, x_recv, y_send, y_recv, c_send, c_recv,
    send_sem, recv_sem,
):
    peers = neighbours()
    greet(peers)

    def rows_of(ref, x):
        return jnp.concatenate([ref[pl.ds(tiled_row(x, h), LEV, stride=2 * CX), :] for h in range(2)], axis=1)

    def own_rows(x):
        return rows_of(initial, x)

    def put(slab, fields, rate_row):
        rate = jnp.concatenate(
            [jnp.broadcast_to(rate_row, (LEV, CY)), jnp.zeros((LEV, CY), F32)], axis=0
        )
        field[slab, PAD : PAD + CY, :] = fields.T
        rates[slab, PAD : PAD + CY, :] = rate.T

    def put_own(x):
        both = jnp.concatenate([own_rows(x), rows_of(targets, x)], axis=0)
        put(x + 2, both, diffusivity[pl.ds(x, 1), :])

    copies = []
    for side in range(2):
        for k in range(2):
            x = k if side == 0 else CX - 2 + k
            x_send[side, k, 0:LEV, :] = own_rows(x)
            x_send[side, k, LEV : LEV + 8, :] = jnp.broadcast_to(diffusivity[x : x + 1, :], (8, CY))
        copy = remote(
            x_send.at[side], x_recv.at[1 - side], send_sem.at[side], recv_sem.at[1 - side], peers[side]
        )
        copy.start()
        copies.append(copy)

    def each(x, carry):
        put_own(x)
        return carry

    lax.fori_loop(0, CX, each, 0)

    for side in range(2):
        row = PAD if side == 0 else PAD + CY - 2
        for x in range(CX):
            y_send[side, 2 * x : 2 * x + 2, :] = field[x + 2, row : row + 2, :]
            y_send[side, 2 * CX + 2 * x : 2 * CX + 2 * x + 2, :] = rates[x + 2, row : row + 2, :]
        copy = remote(
            y_send.at[side], y_recv.at[1 - side], send_sem.at[2 + side], recv_sem.at[3 - side], peers[2 + side]
        )
        copy.start()
        copies.append(copy)
    for corner in range(4):
        x = 2 if corner < 2 else CX + 1
        row = PAD if corner % 2 == 0 else PAD + CY - 1
        c_send[corner, 0:1, :] = field[x, row : row + 1, :]
        c_send[corner, 1:2, :] = rates[x, row : row + 1, :]
        copy = remote(
            c_send.at[corner], c_recv.at[3 - corner], send_sem.at[4 + corner], recv_sem.at[7 - corner],
            peers[4 + corner],
        )
        copy.start()
        copies.append(copy)
    for copy in copies:
        copy.wait_send()
        copy.wait_recv()
    zeros = jnp.zeros((LEV, CY), F32)
    for side in range(2):
        for k in range(2):
            slab = k if side == 0 else CX + 2 + k
            put(
                slab,
                jnp.concatenate([x_recv[side, k, 0:LEV, :], zeros], axis=0),
                x_recv[side, k, LEV : LEV + 1, :],
            )
    for side in range(2):
        row = PAD - 2 if side == 0 else PAD + CY
        for x in range(CX):
            field[x + 2, row : row + 2, :] = y_recv[side, 2 * x : 2 * x + 2, :]
            rates[x + 2, row : row + 2, :] = y_recv[side, 2 * CX + 2 * x : 2 * CX + 2 * x + 2, :]
    for corner in range(4):
        x = 1 if corner < 2 else CX + 2
        row = PAD - 1 if corner % 2 == 0 else PAD + CY
        field[x, row : row + 1, :] = c_recv[corner, 0:1, :]
        rates[x, row : row + 1, :] = c_recv[corner, 1:2, :]

    def first(x, carry):
        now, change = five_point(field, x, PAD - 1, CY + 2)
        middle[x, PAD - 1 : PAD + CY + 1, :] = now + rates[x, PAD - 1 : PAD + CY + 1, :] * change
        return carry

    for x in (1, CX + 2):
        now, change = five_point(field, x, PAD, CY)
        middle[x, PAD : PAD + CY, :] = now + rates[x, PAD : PAD + CY, :] * change
    lax.fori_loop(2, CX + 2, first, 0)
    low = low_lanes((CY, 2 * LEV))

    def second(x, carry):
        now, change = five_point(middle, x, PAD, CY)
        later = now + rates[x, PAD : PAD + CY, :] * change
        moved = pltpu.roll(later, LEV, 1)
        columns[pl.ds(pl.multiple_of((x - 2) * CY, CY), CY), :] = jnp.where(low, later, moved - later)
        return carry

    lax.fori_loop(2, CX + 2, second, 0)


def silu_and_slope(preact):
    sigmoid_value = 0.5 + 0.5 * jnp.tanh(0.5 * preact)
    active = preact * sigmoid_value
    return active.astype(BF16), sigmoid_value + active * (1.0 - sigmoid_value)


def dot(left, right, contract=(1, 0)):
    return lax.dot_general(
        left, right, (((contract[0],), (contract[1],)), ((), ())), preferred_element_type=F32
    )


def network_kernel(
    columns, outward, homeward, w_first_t, w_inner_t, w_last_t, w_first, w_inner, w_last, b_inner, b_last,
    grads, step_first, step_inner, step_last, step_bias_inner, step_bias_last,
    stage, send, recv, answer, back, rows, total, wide, parts, whole,
    out_sem, in_sem, ret_sem, back_sem, part_sem, part_in_sem, whole_sem, whole_in_sem,
):
    tile, sub = lax.axis_index("tile"), lax.axis_index("sub")
    greet(
        [(tile, wrapped(sub, j, SUBS)) for j in range(1, SUBS)]
        + [(wrapped(tile, j, TILES), sub) for j in range(1, TILES)]
    )

    def outgoing(j):
        return remote(send.at[j], recv.at[j], out_sem.at[j], in_sem.at[j], (tile, wrapped(sub, j, SUBS)))

    def returning(j):
        return remote(answer.at[j], back.at[j], ret_sem.at[j], back_sem.at[j], (tile, wrapped(sub, -j, SUBS)))

    def gathered(j):
        def some(group, carry):
            base = group * 16
            for k in range(16):
                stage[pl.ds(base + k, 1), :] = columns[pl.ds(outward[j * SHARE + base + k], 1), :]
            return carry

        lax.fori_loop(0, SHARE // 16, some, 0)
        return stage[...].astype(BF16)

    def push(j, carry):
        send[j] = gathered(j)
        outgoing(j).start()
        return carry

    lax.fori_loop(1, SUBS, push, 0)
    recv[0] = gathered(0)
    total[...] = jnp.zeros_like(total)
    extra = (lax.broadcasted_iota(jnp.int32, (AUG, 2 * SHARE), 0) == 0).astype(F32).astype(BF16)

    def with_ones(value):
        return jnp.concatenate([value, extra], axis=0)

    def two_blocks(pair, carry):
        @pl.when(pair > 0)
        def _():
            outgoing(2 * pair).wait_recv()

        outgoing(2 * pair + 1).wait_recv()
        block = jnp.concatenate([recv[2 * pair], recv[2 * pair + 1]], axis=0)
        turned = block.astype(F32).T
        inputs = turned[:LEV].astype(BF16)
        misfit = turned[LEV:]
        current, slope1 = silu_and_slope(dot(w_first_t[...], inputs) + b_inner[0])
        feeds, slopes = [current], [slope1]
        for k in range(3):
            current, slope = silu_and_slope(dot(w_inner_t[k], current) + b_inner[k + 1])
            feeds.append(current)
            slopes.append(slope)
        residue = misfit + dot(w_last_t[...], current) + b_last[...]
        error = residue.astype(BF16)
        total[FIRST_LAST:, 0 : WIDTH + AUG] += dot(error, with_ones(current), (1, 1))
        carried = dot(w_last[...], error)
        for k in (2, 1, 0):
            error = (carried * slopes[k + 1]).astype(BF16)
            row = FIRST_INNER + k * (WIDTH + AUG)
            total[row : row + WIDTH + AUG, 0:WIDTH] += dot(with_ones(feeds[k]), error, (1, 1))
            carried = dot(w_inner[k], error)
        error = (carried * slopes[0]).astype(BF16)
        total[0:FIRST_INNER, 0:WIDTH] += dot(with_ones(inputs), error, (1, 1))
        result = residue + dot(w_first[...], error)
        half = SHARE // 2
        for k in range(2):
            first = k * SHARE
            packed = jnp.concatenate(
                [result[:, first : first + half], result[:, first + half : first + SHARE]], axis=0
            )
            answer[2 * pair + k] = packed.T.astype(BF16)

        @pl.when(pair > 0)
        def _():
            returning(2 * pair).start()

        returning(2 * pair + 1).start()
        return carry

    lax.fori_loop(0, SUBS // 2, two_blocks, 0)

    wide[...] = total[...].astype(BF16)

    def part(j):
        owner = wrapped(tile, j, TILES)
        first = pl.multiple_of(owner * CHUNK, CHUNK)
        return remote(
            wide.at[pl.ds(first, CHUNK)], parts.at[j], part_sem.at[j], part_in_sem.at[j], (owner, sub)
        )

    def share_of(j):
        return remote(
            whole.at[0], whole.at[j], whole_sem.at[j], whole_in_sem.at[j], (wrapped(tile, j, TILES), sub)
        )

    for j in range(1, TILES):
        part(j).start()

    def unpack(j, source):
        block = source.astype(F32)
        first = pl.multiple_of(j * SHARE, SHARE)
        rows[pl.ds(first, SHARE // 2), :] = block
        rows[pl.ds(first + SHARE // 2, SHARE // 2), :] = pltpu.roll(block, LEV, 1)

    unpack(0, answer[0])

    def take(j, carry):
        returning(j).wait_recv()
        unpack(j, back[j])
        return carry

    lax.fori_loop(1, SUBS, take, 0)

    mine = pl.multiple_of(tile * CHUNK, CHUNK)
    summed = wide[pl.ds(mine, CHUNK), :].astype(F32)
    for j in range(1, TILES):
        part(j).wait_recv()
        summed = summed + parts[j].astype(F32)
    whole[0] = summed.astype(BF16)
    for j in range(1, TILES):
        share_of(j).start()

    def home(group, carry):
        base = group * 16
        for k in range(16):
            grads[pl.ds(base + k, 1), :] = rows[pl.ds(homeward[base + k], 1), :]
        return carry

    lax.fori_loop(0, NCOL // 16, home, 0)

    for j in range(1, TILES):
        share_of(j).wait_recv()
    for j in range(TILES):
        owner = wrapped(tile, -j, TILES)
        total[pl.ds(pl.multiple_of(owner * CHUNK, CHUNK), CHUNK), :] = whole[j].astype(F32)
    everything = total[...]
    squares = jnp.sum(jnp.sum(everything * everything, axis=0, keepdims=True), axis=1, keepdims=True)
    factor = lax.rsqrt(squares / PARAMS + 1e-06)
    step_first[...] = total[0:LEV, 0:WIDTH] * factor
    step_bias_inner[0:1, :] = total[LEV : LEV + 1, 0:WIDTH] * factor
    for k in range(3):
        row = FIRST_INNER + k * (WIDTH + AUG)
        step_inner[k] = total[row : row + WIDTH, 0:WIDTH] * factor
        step_bias_inner[k + 1 : k + 2, :] = total[row + WIDTH : row + WIDTH + 1, 0:WIDTH] * factor
    last = (total[FIRST_LAST:, :] * factor).T
    step_last[...] = last[0:WIDTH, :]
    step_bias_last[...] = last[WIDTH : WIDTH + 1, :]

    def settle(j, carry):
        outgoing(j).wait_send()
        returning(j).wait_send()
        return carry

    lax.fori_loop(1, SUBS, settle, 0)
    for j in range(1, TILES):
        part(j).wait_send()
        share_of(j).wait_send()


def adjoint_kernel(
    grads, rates,
    result,
    field, middle, product, x_send, x_recv, y_send, y_recv, c_send, c_recv,
    send_sem, recv_sem,
):
    peers = neighbours()
    greet(peers)
    low = low_lanes((CY, 2 * LEV))

    def slab_of(x):
        return grads[pl.ds(pl.multiple_of(x * CY, CY), CY), :]

    copies = []
    for side in range(2):
        x = 0 if side == 0 else CX - 2
        x_send[side] = jnp.where(low, slab_of(x), pltpu.roll(slab_of(x + 1), LEV, 1)).astype(BF16)
        copy = remote(
            x_send.at[side], x_recv.at[1 - side], send_sem.at[side], recv_sem.at[1 - side], peers[side]
        )
        copy.start()
        copies.append(copy)
    for side in range(2):
        row = 0 if side == 0 else CY - 2
        for x in range(CX):
            y_send[side, 2 * x : 2 * x + 2, :] = grads[x * CY + row : x * CY + row + 2, :]
        copy = remote(
            y_send.at[side], y_recv.at[1 - side], send_sem.at[2 + side], recv_sem.at[3 - side], peers[2 + side]
        )
        copy.start()
        copies.append(copy)
    for corner in range(4):
        row = (0 if corner < 2 else (CX - 1) * CY) + (0 if corner % 2 == 0 else CY - 1)
        c_send[corner, 0:1, :] = grads[row : row + 1, :]
        copy = remote(
            c_send.at[corner], c_recv.at[3 - corner], send_sem.at[4 + corner], recv_sem.at[7 - corner],
            peers[4 + corner],
        )
        copy.start()
        copies.append(copy)

    def each(x, carry):
        field[x + 2, PAD : PAD + CY, :] = slab_of(x)
        return carry

    lax.fori_loop(0, CX, each, 0)
    for copy in copies:
        copy.wait_send()
        copy.wait_recv()
    for side in range(2):
        slab = 0 if side == 0 else CX + 2
        arrived = x_recv[side].astype(F32)
        field[slab, PAD : PAD + CY, :] = arrived
        field[slab + 1, PAD : PAD + CY, :] = pltpu.roll(arrived, LEV, 1)
        row = PAD - 2 if side == 0 else PAD + CY
        for x in range(CX):
            field[x + 2, row : row + 2, :] = y_recv[side, 2 * x : 2 * x + 2, :]
    for corner in range(4):
        x = 1 if corner < 2 else CX + 2
        row = PAD - 1 if corner % 2 == 0 else PAD + CY
        field[x, row : row + 1, :] = c_recv[corner, 0:1, :]

    def scaled(x, carry):
        rows = slice(PAD - 2, PAD + CY + 2)
        product[x, rows, :] = rates[x, rows, :] * field[x, rows, :]
        return carry

    lax.fori_loop(0, CX + 4, scaled, 0)

    def first(x, start, count):
        _, change = five_point(product, x, start, count)
        middle[x, pl.ds(start, count), :] = field[x, pl.ds(start, count), :] + change

    for x in (1, CX + 2):
        first(x, PAD, CY)

    def first_own(x, carry):
        first(x, PAD - 1, CY + 2)
        return carry

    lax.fori_loop(2, CX + 2, first_own, 0)

    def scaled_again(x, carry):
        rows = slice(PAD - 1, PAD + CY + 1)
        product[x, rows, :] = rates[x, rows, :] * middle[x, rows, :]
        return carry

    lax.fori_loop(1, CX + 3, scaled_again, 0)

    def second(pair, carry):
        x = 2 * pair
        done = []
        for k in range(2):
            _, change = five_point(product, x + k + 2, PAD, CY)
            done.append(middle[x + k + 2, PAD : PAD + CY, :] + change)
        turned = jnp.where(low, done[0], pltpu.roll(done[1], LEV, 1)).T
        for k in range(2):
            for h in range(2):
                half = turned[k * LEV : (k + 1) * LEV, h * 128 : (h + 1) * 128]
                result[pl.ds(tiled_row(x + k, h), LEV, stride=2 * CX), :] = half
        return carry

    lax.fori_loop(0, CX // 2, second, 0)


def params(collective):
    return pltpu.CompilerParams(
        collective_id=collective, has_side_effects=True, vmem_limit_bytes=LIMIT
    )


def routes(counts, order):
    sub = lax.axis_index("sub")
    devices = TILES * SUBS
    ids = jnp.arange(devices, dtype=jnp.int32)
    starts = jnp.sum(jnp.where(ids[None, :] < ids[:, None], counts[None, :], 0), axis=1)
    same = ids[None, :] % SUBS == ids[:, None] % SUBS
    within = jnp.sum(
        jnp.where((ids[None, :] < ids[:, None]) & same, counts[None, :], 0), axis=1
    )
    block = lax.rem(ids % SUBS - sub + SUBS, SUBS)
    shift = block * SHARE + within - starts
    before = jnp.concatenate([jnp.zeros((1,), jnp.int32), shift[:-1]])
    change = shift - before
    places = jnp.arange(NCOL, dtype=jnp.int32)
    slots = places + jnp.sum(
        jnp.where(starts[:, None] <= places[None, :], change[:, None], 0), axis=0
    )

    def scattered(where, what):
        sixty_four = jnp.arange(64, dtype=jnp.int32)[:, None]
        high = (where[None, :] // 64 == sixty_four).astype(BF16)
        low = where[None, :] % 64 == sixty_four
        values = jnp.concatenate(
            [
                jnp.where(low, (what // 64).astype(BF16)[None, :], jnp.zeros((), BF16)),
                jnp.where(low, (what % 64).astype(BF16)[None, :], jnp.zeros((), BF16)),
            ],
            axis=0,
        )
        both = dot(high, values, (1, 1)).astype(jnp.int32)
        return (both[:, :64] * 64 + both[:, 64:]).reshape(NCOL)

    return scattered(slots, order), scattered(order, slots)


def halo_scratch(x_shape, x_type, y_rows):
    return [
        pltpu.VMEM((2,) + x_shape, x_type),
        pltpu.VMEM((2,) + x_shape, x_type),
        pltpu.VMEM((2, y_rows, 2 * LEV), F32),
        pltpu.VMEM((2, y_rows, 2 * LEV), F32),
        pltpu.VMEM((4, 8, 2 * LEV), F32),
        pltpu.VMEM((4, 8, 2 * LEV), F32),
        pltpu.SemaphoreType.DMA((8,)),
        pltpu.SemaphoreType.DMA((8,)),
    ]


def per_device(
    initial, targets, diffusivity, column_order, send_counts, w_first, w_inner, w_last, b_inner, b_last
):
    slabs = pltpu.VMEM((CX + 4, ROWS_Y, 2 * LEV), F32)
    columns, rates = pl.pallas_call(
        forward_kernel,
        out_shape=(
            jax.ShapeDtypeStruct((NCOL, 2 * LEV), F32),
            jax.ShapeDtypeStruct((CX + 4, ROWS_Y, 2 * LEV), F32),
        ),
        in_specs=[VMEM] * 3,
        out_specs=(VMEM, VMEM),
        scratch_shapes=[slabs, slabs] + halo_scratch((2, LEV + 8, CY), F32, 4 * CX),
        compiler_params=params(0),
        name="forward",
    )(tiled(initial), tiled(targets), diffusivity)
    outward, homeward = routes(send_counts[0], column_order[0])
    grads, step_first, step_inner, step_last, step_bias_inner, step_bias_last = pl.pallas_call(
        network_kernel,
        out_shape=(
            jax.ShapeDtypeStruct((NCOL, 2 * LEV), F32),
            jax.ShapeDtypeStruct((LEV, WIDTH), F32),
            jax.ShapeDtypeStruct((3, WIDTH, WIDTH), F32),
            jax.ShapeDtypeStruct((WIDTH, LEV), F32),
            jax.ShapeDtypeStruct((4, WIDTH), F32),
            jax.ShapeDtypeStruct((1, LEV), F32),
        ),
        in_specs=[VMEM, SMEM, SMEM] + [VMEM] * 8,
        out_specs=(VMEM,) * 6,
        scratch_shapes=[
            pltpu.VMEM((SHARE, 2 * LEV), F32),
            pltpu.VMEM((SUBS, SHARE, 2 * LEV), BF16),
            pltpu.VMEM((SUBS, SHARE, 2 * LEV), BF16),
            pltpu.VMEM((SUBS, SHARE // 2, 2 * LEV), BF16),
            pltpu.VMEM((SUBS, SHARE // 2, 2 * LEV), BF16),
            pltpu.VMEM((NCOL, 2 * LEV), F32),
            pltpu.VMEM((GRAD_ROWS, 256), F32),
            pltpu.VMEM((GRAD_ROWS, 256), BF16),
            pltpu.VMEM((TILES, CHUNK, 256), BF16),
            pltpu.VMEM((TILES, CHUNK, 256), BF16),
        ]
        + [pltpu.SemaphoreType.DMA((SUBS,))] * 4
        + [pltpu.SemaphoreType.DMA((TILES,))] * 4,
        compiler_params=params(1),
        name="network",
    )(
        columns,
        outward,
        homeward,
        w_first[0].T,
        w_inner[0].transpose(0, 2, 1),
        w_last[0].T,
        w_first[0],
        w_inner[0],
        w_last[0],
        b_inner[0][:, :, None],
        b_last[0][:, None],
    )
    result = pl.pallas_call(
        adjoint_kernel,
        out_shape=jax.ShapeDtypeStruct((LEV * CX * 2, 128), F32),
        in_specs=[VMEM] * 2,
        out_specs=VMEM,
        scratch_shapes=[slabs, slabs, slabs] + halo_scratch((CY, 2 * LEV), BF16, 2 * CX),
        compiler_params=params(2),
        name="adjoint",
    )(grads, rates)
    return (
        untiled(result),
        step_first[None],
        step_inner[None],
        step_last[None],
        step_bias_inner[None],
        step_bias_last,
    )


def solution(mesh):
    placed = (
        P(None, "tile", "sub"),
        P(None, "tile", "sub"),
        P("tile", "sub"),
        P(("tile", "sub"), None),
        P(("tile", "sub"), None),
        P("sub", None, None),
        P("sub", None, None, None),
        P("sub", None, None),
        P("sub", None, None),
        P("sub", None),
    )
    return jax.shard_map(
        per_device,
        mesh=mesh,
        in_specs=placed,
        out_specs=(
            P(None, "tile", "sub"),
            P("sub", None, None),
            P("sub", None, None, None),
            P("sub", None, None),
            P("sub", None, None),
            P("sub", None),
        ),
        check_vma=False,
    )
```

```python
import jax
import jax.numpy as jnp
from jax import lax
from jax.experimental import pallas as pl
from jax.experimental.pallas import tpu as pltpu
from jax.sharding import PartitionSpec as P

MESH = pl.DeviceIdType.MESH
F32 = jnp.float32
BF16 = jnp.bfloat16
LEV = 64
WIDTH = 192
CX = 16
CY = 256
NCOL = CX * CY
TILES = 8
SUBS = 16
SHARE = NCOL // SUBS
PARAMS = 136000
AUG = 16
LANES = 128
SPAN = CY + LANES
SLABS = CX + 4
CHUNK = 96
GRAD_ROWS = CHUNK * TILES
FIRST_INNER = LEV + AUG
FIRST_LAST = FIRST_INNER + 3 * (WIDTH + AUG)
ANY = pl.BlockSpec(memory_space=pl.ANY)
LIMIT = 58 * 2**20


def wrapped(index, step, count):
    return lax.rem(index + step + count, count)


def remote(source, target, send_sem, recv_sem, peer):
    return pltpu.make_async_remote_copy(
        src_ref=source,
        dst_ref=target,
        send_sem=send_sem,
        recv_sem=recv_sem,
        device_id=peer,
        device_id_type=MESH,
    )


def tiled(block):
    return block.reshape(LEV, CX // 8, 8, 2, LANES).transpose(0, 1, 3, 2, 4).reshape(-1, LANES)


def untiled(rows):
    return rows.reshape(LEV, CX // 8, 2, 8, LANES).transpose(0, 1, 3, 2, 4).reshape(LEV, CX, CY)


def tiled_row(x, half):
    return (x // 8) * 16 + half * 8 + x % 8


def lanes(shape):
    return lax.broadcasted_iota(jnp.int32, shape, 1)


def sublanes(shape):
    return lax.broadcasted_iota(jnp.int32, shape, 0)


def dot(left, right, contract=(1, 0)):
    return lax.dot_general(
        left, right, (((contract[0],), (contract[1],)), ((), ())), preferred_element_type=F32
    )


def near_sum(value):
    return pltpu.roll(value, 1, 1) + pltpu.roll(value, SPAN - 1, 1)


def silu_and_slope(preact):
    sigmoid_value = 0.5 + 0.5 * jnp.tanh(0.5 * preact)
    active = preact * sigmoid_value
    return active.astype(BF16), sigmoid_value + active * (1.0 - sigmoid_value)


def find_routes(order, counts, sub, routes, tables, sems):
    count_row = counts[...]
    square = (TILES * SUBS, TILES * SUBS)
    earlier = lanes(square)

    def starts_and_shift(device):
        before = earlier < device
        same = earlier % SUBS == device % SUBS
        start = jnp.sum(jnp.where(before, count_row, 0), axis=1, keepdims=True)
        within = jnp.sum(jnp.where(before & same, count_row, 0), axis=1, keepdims=True)
        block = lax.rem(device[:, 0:1] % SUBS - sub + SUBS, SUBS)
        return start, block * SHARE + within - start

    device = sublanes(square)
    start, shift = starts_and_shift(device)
    _, shift_before = starts_and_shift(jnp.maximum(device - 1, 0))
    change = shift - jnp.where(device[:, 0:1] == 0, 0, shift_before)
    width = 512
    outward = jnp.zeros((32, 256), F32)
    homeward = jnp.zeros((32, 256), F32)

    def spread(where, what):
        high = (sublanes((32, width)) == where // LANES).astype(F32).astype(BF16)
        hit = sublanes((LANES, width)) == where % LANES
        values = jnp.concatenate(
            [jnp.where(hit, what // LANES, 0), jnp.where(hit, what % LANES, 0)], axis=0
        )
        return dot(high, values.astype(F32).astype(BF16), (1, 1))

    for first in range(0, NCOL, width):
        place = lanes((1, width)) + first
        slot = place + jnp.sum(jnp.where(start <= place, change, 0), axis=0, keepdims=True)
        column = order[:, first : first + width]
        outward = outward + spread(slot, column)
        homeward = homeward + spread(column, slot)
    for k, table in enumerate((outward, homeward)):
        whole = table.astype(jnp.int32)
        tables[k] = jnp.clip(whole[:, 0:LANES] * LANES + whole[:, LANES:], 0, NCOL - 1)
    for k in range(2):
        copy = pltpu.make_async_copy(tables.at[k], routes.at[k], sems.at[k])
        copy.start()
        copy.wait()


def step_kernel(
    initial_hbm, targets_hbm, diffusivity_hbm, order_hbm, counts_hbm,
    w_first_hbm, w_inner_hbm, w_last_hbm, b_inner_hbm, b_last_hbm,
    result_hbm, step_first_hbm, step_inner_hbm, step_last_hbm, step_bias_inner_hbm, step_bias_last_hbm,
    initial, targets, diffusivity, order, counts, w_first, w_inner, w_last_t, b_inner, b_last,
    result, step_first, step_inner, step_last_t, step_bias_inner, step_bias_last,
    load_sem, store_sem,
    field, middle, rates, columns, tables, routes,
    xs, xr, ys, yr, cs, cr, gxs, gxr, gys, gyr, gcs, gcr,
    wt_first, wt_inner, w_last, bias,
    stage, send, recv, answer, back, rows, grads, total, wide, parts, whole,
    table_sem, halo_sem, halo_in_sem, ghalo_sem, ghalo_in_sem,
    out_sem, in_sem, ret_sem, back_sem, part_sem, part_in_sem, whole_sem, whole_in_sem,
):
    tile, sub = lax.axis_index("tile"), lax.axis_index("sub")
    up, down = wrapped(tile, 1, TILES), wrapped(tile, -1, TILES)
    right, left = wrapped(sub, 1, SUBS), wrapped(sub, -1, SUBS)
    around = (
        (down, sub), (up, sub), (tile, left), (tile, right),
        (down, left), (down, right), (up, left), (up, right),
    )
    peers = (
        [(tile, wrapped(sub, j, SUBS)) for j in range(1, SUBS)]
        + [(wrapped(tile, j, TILES), sub) for j in range(1, TILES)]
        + list(around[4:])
    )
    barrier = pltpu.get_barrier_semaphore()
    for peer in peers:
        pl.semaphore_signal(barrier, inc=1, device_id=peer, device_id_type=MESH)

    loads = [
        pltpu.make_async_copy(source, target, load_sem.at[k])
        for k, (source, target) in enumerate(
            (
                (initial_hbm, initial), (diffusivity_hbm, diffusivity), (order_hbm, order),
                (counts_hbm, counts), (w_first_hbm, w_first), (w_inner_hbm, w_inner),
                (w_last_hbm, w_last_t), (b_inner_hbm, b_inner), (b_last_hbm, b_last),
                (targets_hbm, targets),
            )
        )
    ]
    for load in loads:
        load.start()
    stores = [
        pltpu.make_async_copy(source, target, store_sem.at[k])
        for k, (source, target) in enumerate(
            (
                (result, result_hbm), (step_first, step_first_hbm), (step_inner, step_inner_hbm),
                (step_last_t, step_last_hbm), (step_bias_inner, step_bias_inner_hbm),
                (step_bias_last, step_bias_last_hbm),
            )
        )
    ]

    def cells(ref, x):
        return jnp.concatenate(
            [ref[pl.ds(tiled_row(x, h), LEV, stride=2 * CX), :] for h in range(2)], axis=1
        )

    def halo(group, k, sends, receives, out_sems, in_sems):
        place = {"x": k, "y": 2 + k, "c": 4 + k}[group]
        other = (3 - k) if group == "c" else (1 - k)
        opposite = place - k + other
        return remote(
            sends.at[k], receives.at[other], out_sems.at[place], in_sems.at[opposite], around[place]
        )

    def strip(tile_of, side):
        pair = lanes((LEV, LANES)) // 2
        packed = jnp.zeros((LEV, LANES), F32)
        for x in range(CX):
            moved = tile_of(x, side)
            shift = (2 * x + 2 * side) % LANES
            if shift:
                moved = pltpu.roll(moved, shift, 1)
            packed = jnp.where(pair == x, moved, packed)
        return packed

    def edge_tile(x, side):
        return field[x + 2, :, side * LANES : (side + 1) * LANES]

    low = lanes((LEV, LANES)) < LEV

    def halo_tile(from_left, from_right, x):
        back_right = pltpu.roll(from_right, LANES - 2 * x, 1) if x else from_right
        return jnp.where(low, back_right, pltpu.roll(from_left, LANES - 2 - 2 * x, 1))

    def fill(x, carry):
        field[x + 2, :, 0:CY] = cells(initial, x)
        return carry

    loads[0].wait()
    loads[1].wait()
    lax.fori_loop(0, CX, fill, 0)
    for side in range(2):
        for k in range(2):
            xs[side, k * LEV : (k + 1) * LEV, :] = field[2 + (k if side == 0 else CX - 2 + k), :, 0:CY]
        xs[side, 2 * LEV :, :] = diffusivity[8 * side : 8 * side + 8, :]
    for corner in range(4):
        side, edge = corner // 2, corner % 2
        cs[corner, 0:LEV, :] = edge_tile(0 if side == 0 else CX - 1, edge)
        cs[corner, LEV:, :] = diffusivity[8 * side : 8 * side + 8, edge * LANES : (edge + 1) * LANES]
    pl.semaphore_wait(barrier, len(peers))
    copies = []
    for side in range(2):
        copies.append(halo("x", side, xs, xr, halo_sem, halo_in_sem))
        copies[-1].start()
    for corner in range(4):
        copies.append(halo("c", corner, cs, cr, halo_sem, halo_in_sem))
        copies[-1].start()
    for side in range(2):
        ys[side, 0:LEV, :] = strip(edge_tile, side)
        ys[side, LEV:, :] = diffusivity[:, side * LANES : (side + 1) * LANES]
        copies.append(halo("y", side, ys, yr, halo_sem, halo_in_sem))
        copies[-1].start()

    for load in loads[2:]:
        load.wait()
    find_routes(order, counts, sub, routes, tables, table_sem)
    same = sublanes((WIDTH, WIDTH)) == lanes((WIDTH, WIDTH))
    unit = same.astype(F32).astype(BF16)
    wt_first[...] = dot(unit, w_first[...], (1, 1)).astype(BF16)
    for k in range(3):
        wt_inner[k] = dot(unit, w_inner[k], (1, 1)).astype(BF16)
    w_last[...] = dot(unit, w_last_t[...], (1, 1)).astype(BF16)
    for k in range(4):
        bias[k] = jnp.sum(jnp.where(same, b_inner[k : k + 1, :], 0.0), axis=1, keepdims=True)
    same_lev = sublanes((LEV, LEV)) == lanes((LEV, LEV))
    bias[4, 0:LEV, :] = jnp.sum(jnp.where(same_lev, b_last[...], 0.0), axis=1, keepdims=True)
    total[...] = jnp.zeros_like(total)

    for copy in copies:
        copy.wait_recv()
    rates[0:2, 0:CY] = xr[0, 2 * LEV + 6 :, :]
    rates[2 : CX + 2, 0:CY] = diffusivity[...]
    rates[CX + 2 : CX + 4, 0:CY] = xr[1, 2 * LEV : 2 * LEV + 2, :]
    first_rows = lanes((CX, LANES)) < LEV
    rates[0:8, CY:] = jnp.zeros((8, LANES), F32)
    rates[16:24, CY:] = jnp.zeros((8, LANES), F32)
    rates[2 : CX + 2, CY:] = jnp.where(first_rows, yr[1, LEV:, :], yr[0, LEV:, :])
    one_row = lanes((1, LANES)) < LEV
    rates[1:2, CY:] = jnp.where(one_row, cr[1, LEV + 7 :, :], cr[0, LEV + 7 :, :])
    rates[CX + 2 : CX + 3, CY:] = jnp.where(
        one_row, cr[3, LEV : LEV + 1, :], cr[2, LEV : LEV + 1, :]
    )

    def spread_halo(x_in, y_in, c_in):
        for side in range(2):
            for k in range(2):
                slab = k if side == 0 else CX + 2 + k
                field[slab, :, 0:CY] = x_in[side, k * LEV : (k + 1) * LEV, :].astype(F32)
            outer = 0 if side == 0 else CX + 3
            field[outer, :, CY:] = jnp.zeros((LEV, LANES), F32)
            inner = 1 if side == 0 else CX + 2
            field[inner, :, CY:] = jnp.where(
                low, c_in[2 * side + 1, 0:LEV, :].astype(F32), c_in[2 * side, 0:LEV, :].astype(F32)
            )
        from_left, from_right = y_in[0, 0:LEV, :].astype(F32), y_in[1, 0:LEV, :].astype(F32)
        for x in range(CX):
            field[x + 2, :, CY:] = halo_tile(from_left, from_right, x)

    spread_halo(xr, yr, cr)

    def diffused(ref, slab):
        now = ref[slab]
        near = ref[slab - 1] + ref[slab + 1] + near_sum(now)
        return now + rates[pl.ds(slab, 1), :] * (near - 4.0 * now)

    def forward_first(slab, carry):
        middle[slab] = diffused(field, slab)
        return carry

    lax.fori_loop(1, CX + 3, forward_first, 0)

    def forward_second(x, carry):
        later = diffused(middle, x + 2)[:, 0:CY]
        both = jnp.concatenate([later, later - cells(targets, x)], axis=0)
        columns[pl.ds(pl.multiple_of(x * CY, CY), CY), :] = both.T
        return carry

    lax.fori_loop(0, CX, forward_second, 0)

    def outgoing(j):
        return remote(send.at[j], recv.at[j], out_sem.at[j], in_sem.at[j], (tile, wrapped(sub, j, SUBS)))

    def returning(j):
        return remote(answer.at[j], back.at[j], ret_sem.at[j], back_sem.at[j], (tile, wrapped(sub, -j, SUBS)))

    def gathered(j):
        def some(group, carry):
            base = group * 16
            line = j * 2 + group // 8
            taken = [columns[pl.ds(routes[0, line, (group % 8) * 16 + k], 1), :] for k in range(16)]
            for k in range(16):
                stage[pl.ds(base + k, 1), :] = taken[k]
            return carry

        lax.fori_loop(0, SHARE // 16, some, 0)
        return stage[...].astype(BF16)

    def push(j, carry):
        send[j] = gathered(j)
        outgoing(j).start()
        return carry

    lax.fori_loop(1, SUBS, push, 0)
    recv[0] = gathered(0)

    extra = (sublanes((AUG, SHARE)) == 0).astype(F32).astype(BF16)

    def with_ones(value):
        return jnp.concatenate([value, extra], axis=0)

    def two_blocks(pair, carry):
        @pl.when(pair > 0)
        def _():
            outgoing(2 * pair).wait_recv()

        outgoing(2 * pair + 1).wait_recv()
        both = range(2)
        turned = [recv[2 * pair + b].astype(F32).T for b in both]
        inputs = [turned[b][:LEV].astype(BF16) for b in both]
        current = inputs
        feeds, slopes = [inputs], []
        for k in range(4):
            weight = wt_first[...] if k == 0 else wt_inner[k - 1]
            outs = [silu_and_slope(dot(weight, current[b]) + bias[k]) for b in both]
            current = [outs[b][0] for b in both]
            feeds.append(current)
            slopes.append([outs[b][1] for b in both])
        residue = [
            turned[b][LEV:] + dot(w_last_t[...], current[b]) + bias[4, 0:LEV, :] for b in both
        ]
        error = [residue[b].astype(BF16) for b in both]
        total[FIRST_LAST:, 0 : WIDTH + AUG] += sum(
            dot(error[b], with_ones(current[b]), (1, 1)) for b in both
        )
        carried = [dot(w_last[...], error[b]) for b in both]
        for k in (3, 2, 1, 0):
            error = [(carried[b] * slopes[k][b]).astype(BF16) for b in both]
            row = FIRST_INNER + (k - 1) * (WIDTH + AUG) if k else 0
            high = (WIDTH if k else LEV) + AUG
            total[row : row + high, 0:WIDTH] += sum(
                dot(with_ones(feeds[k][b]), error[b], (1, 1)) for b in both
            )
            weight = w_inner[k - 1] if k else w_first[...]
            carried = [dot(weight, error[b]) for b in both]
        half = SHARE // 2
        for b in both:
            outcome = residue[b] + carried[b]
            packed = jnp.concatenate([outcome[:, :half], outcome[:, half:]], axis=0)
            answer[2 * pair + b] = packed.T.astype(BF16)

        @pl.when(pair > 0)
        def _():
            returning(2 * pair).start()

        returning(2 * pair + 1).start()
        return carry

    lax.fori_loop(0, SUBS // 2, two_blocks, 0)

    wide[...] = total[...].astype(BF16)

    def part(j):
        owner = wrapped(tile, j, TILES)
        first = pl.multiple_of(owner * CHUNK, CHUNK)
        return remote(
            wide.at[pl.ds(first, CHUNK)], parts.at[j], part_sem.at[j], part_in_sem.at[j], (owner, sub)
        )

    def share_of(j):
        return remote(
            whole.at[0], whole.at[j], whole_sem.at[j], whole_in_sem.at[j], (wrapped(tile, j, TILES), sub)
        )

    for j in range(1, TILES):
        part(j).start()

    def unpack(j, source):
        block = source.astype(F32)
        first = pl.multiple_of(j * SHARE, SHARE)
        rows[pl.ds(first, SHARE // 2), :] = block
        rows[pl.ds(first + SHARE // 2, SHARE // 2), :] = pltpu.roll(block, LEV, 1)

    unpack(0, answer[0])

    def take(j, carry):
        returning(j).wait_recv()
        unpack(j, back[j])
        return carry

    lax.fori_loop(1, SUBS, take, 0)

    left_half = lanes((CY, LANES)) < LEV

    def home(x):
        def some(group, carry):
            base = group * 16
            line = x * 2 + group // 8
            taken = [rows[pl.ds(routes[1, line, (group % 8) * 16 + k], 1), :] for k in range(16)]
            for k in range(16):
                grads[pl.ds(base + k, 1), :] = taken[k]
            return carry

        lax.fori_loop(0, 2 * CY // 16, some, 0)
        turned = jnp.where(left_half, grads[0:CY, :], pltpu.roll(grads[CY:, :], LEV, 1)).T
        for k in range(2):
            field[x + k + 2, :, 0:CY] = turned[k * LEV : (k + 1) * LEV]

    copies = list(copies)
    ghalos = []
    for side in range(2):
        x = 0 if side == 0 else CX - 2
        home(x)
        for k in range(2):
            gxs[side, k * LEV : (k + 1) * LEV, :] = field[x + k + 2, :, 0:CY].astype(BF16)
        for edge in range(2):
            gcs[2 * side + edge] = edge_tile(0 if side == 0 else CX - 1, edge).astype(BF16)
        ghalos.append(halo("x", side, gxs, gxr, ghalo_sem, ghalo_in_sem))
        for edge in range(2):
            ghalos.append(halo("c", 2 * side + edge, gcs, gcr, ghalo_sem, ghalo_in_sem))
        for copy in ghalos[-3:]:
            copy.start()

    mine = pl.multiple_of(tile * CHUNK, CHUNK)
    summed = wide[pl.ds(mine, CHUNK), :].astype(F32)
    for j in range(1, TILES):
        part(j).wait_recv()
        summed = summed + parts[j].astype(F32)
    whole[0] = summed.astype(BF16)
    for j in range(1, TILES):
        share_of(j).start()

    def home_pair(pair, carry):
        home(2 * pair)
        return carry

    lax.fori_loop(1, CX // 2 - 1, home_pair, 0)
    for side in range(2):
        gys[side] = strip(edge_tile, side).astype(BF16)
        ghalos.append(halo("y", side, gys, gyr, ghalo_sem, ghalo_in_sem))
        ghalos[-1].start()

    for j in range(1, TILES):
        share_of(j).wait_recv()
    for j in range(TILES):
        owner = wrapped(tile, -j, TILES)
        total[pl.ds(pl.multiple_of(owner * CHUNK, CHUNK), CHUNK), :] = whole[j].astype(F32)
    everything = total[...]
    squares = jnp.sum(jnp.sum(everything * everything, axis=0, keepdims=True), axis=1, keepdims=True)
    factor = lax.rsqrt(squares / PARAMS + 1e-06)
    step_first[...] = total[0:LEV, 0:WIDTH] * factor
    step_bias_inner[0:1, :] = total[LEV : LEV + 1, 0:WIDTH] * factor
    for k in range(3):
        row = FIRST_INNER + k * (WIDTH + AUG)
        step_inner[k] = total[row : row + WIDTH, 0:WIDTH] * factor
        step_bias_inner[k + 1 : k + 2, :] = total[row + WIDTH : row + WIDTH + 1, 0:WIDTH] * factor
    step_last_t[...] = total[FIRST_LAST:, 0:WIDTH] * factor
    last_bias = total[FIRST_LAST:, WIDTH : WIDTH + 1] * factor
    step_bias_last[...] = jnp.sum(jnp.where(same_lev, last_bias, 0.0), axis=0, keepdims=True)
    for store in stores[1:]:
        store.start()

    for copy in ghalos:
        copy.wait_recv()
    spread_halo(gxr, gyr, gcr)

    def adjoint(ref, slab):
        rate = [rates[pl.ds(slab + k, 1), :] for k in (-1, 0, 1)]
        now = ref[slab]
        flow = rate[1] * now
        near = rate[0] * ref[slab - 1] + rate[2] * ref[slab + 1] + near_sum(flow)
        return now + (near - 4.0 * flow)

    def adjoint_first(slab, carry):
        middle[slab] = adjoint(field, slab)
        return carry

    lax.fori_loop(1, CX + 3, adjoint_first, 0)

    def adjoint_second(x, carry):
        done = adjoint(middle, x + 2)
        for h in range(2):
            result[pl.ds(tiled_row(x, h), LEV, stride=2 * CX), :] = done[:, h * LANES : (h + 1) * LANES]
        return carry

    lax.fori_loop(0, CX, adjoint_second, 0)

    stores[0].start()

    def settle(j, carry):
        outgoing(j).wait_send()
        returning(j).wait_send()
        return carry

    lax.fori_loop(1, SUBS, settle, 0)
    for j in range(1, TILES):
        part(j).wait_send()
        share_of(j).wait_send()
    for copy in copies + ghalos:
        copy.wait_send()
    for store in stores:
        store.wait()


def both_ways(shape, kind):
    return [pltpu.VMEM(shape, kind), pltpu.VMEM(shape, kind)]


def per_device(
    initial, targets, diffusivity, column_order, send_counts, w_first, w_inner, w_last, b_inner, b_last
):
    slabs = pltpu.VMEM((SLABS, LEV, SPAN), F32)
    result, step_first, step_inner, step_last_t, step_bias_inner, step_bias_last = pl.pallas_call(
        step_kernel,
        out_shape=(
            jax.ShapeDtypeStruct((LEV * CX * 2, LANES), F32),
            jax.ShapeDtypeStruct((LEV, WIDTH), F32),
            jax.ShapeDtypeStruct((3, WIDTH, WIDTH), F32),
            jax.ShapeDtypeStruct((LEV, WIDTH), F32),
            jax.ShapeDtypeStruct((4, WIDTH), F32),
            jax.ShapeDtypeStruct((1, LEV), F32),
        ),
        in_specs=[ANY] * 10,
        out_specs=(ANY,) * 6,
        scratch_shapes=[
            pltpu.VMEM((LEV * CX * 2, LANES), F32),
            pltpu.VMEM((LEV * CX * 2, LANES), F32),
            pltpu.VMEM((CX, CY), F32),
            pltpu.VMEM((1, NCOL), jnp.int32),
            pltpu.VMEM((1, TILES * SUBS), jnp.int32),
            pltpu.VMEM((LEV, WIDTH), BF16),
            pltpu.VMEM((3, WIDTH, WIDTH), BF16),
            pltpu.VMEM((LEV, WIDTH), BF16),
            pltpu.VMEM((4, WIDTH), F32),
            pltpu.VMEM((1, LEV), F32),
            pltpu.VMEM((LEV * CX * 2, LANES), F32),
            pltpu.VMEM((LEV, WIDTH), F32),
            pltpu.VMEM((3, WIDTH, WIDTH), F32),
            pltpu.VMEM((LEV, WIDTH), F32),
            pltpu.VMEM((4, WIDTH), F32),
            pltpu.VMEM((1, LEV), F32),
            pltpu.SemaphoreType.DMA((10,)),
            pltpu.SemaphoreType.DMA((6,)),
            slabs,
            slabs,
            pltpu.VMEM((24, SPAN), F32),
            pltpu.VMEM((NCOL, LANES), F32),
            pltpu.VMEM((2, NCOL // LANES, LANES), jnp.int32),
            pltpu.SMEM((2, NCOL // LANES, LANES), jnp.int32),
        ]
        + both_ways((2, 2 * LEV + 8, CY), F32)
        + both_ways((2, LEV + CX, LANES), F32)
        + both_ways((4, LEV + 8, LANES), F32)
        + both_ways((2, 2 * LEV, CY), BF16)
        + both_ways((2, LEV, LANES), BF16)
        + both_ways((4, LEV, LANES), BF16)
        + [
            pltpu.VMEM((WIDTH, LEV), BF16),
            pltpu.VMEM((3, WIDTH, WIDTH), BF16),
            pltpu.VMEM((WIDTH, LEV), BF16),
            pltpu.VMEM((5, WIDTH, 1), F32),
            pltpu.VMEM((SHARE, LANES), F32),
        ]
        + both_ways((SUBS, SHARE, LANES), BF16)
        + both_ways((SUBS, SHARE // 2, LANES), BF16)
        + [
            pltpu.VMEM((NCOL, LANES), F32),
            pltpu.VMEM((2 * CY, LANES), F32),
            pltpu.VMEM((GRAD_ROWS, 256), F32),
            pltpu.VMEM((GRAD_ROWS, 256), BF16),
        ]
        + both_ways((TILES, CHUNK, 256), BF16)
        + [pltpu.SemaphoreType.DMA((2,))]
        + [pltpu.SemaphoreType.DMA((8,))] * 4
        + [pltpu.SemaphoreType.DMA((SUBS,))] * 4
        + [pltpu.SemaphoreType.DMA((TILES,))] * 4,
        compiler_params=pltpu.CompilerParams(
            collective_id=0, has_side_effects=True, vmem_limit_bytes=LIMIT
        ),
        name="step",
    )(
        tiled(initial),
        tiled(targets),
        diffusivity,
        column_order,
        send_counts,
        w_first[0],
        w_inner[0],
        w_last[0].T,
        b_inner[0],
        b_last,
    )
    return (
        untiled(result),
        step_first[None],
        step_inner[None],
        step_last_t.T[None],
        step_bias_inner[None],
        step_bias_last,
    )


def solution(mesh):
    placed = (
        P(None, "tile", "sub"),
        P(None, "tile", "sub"),
        P("tile", "sub"),
        P(("tile", "sub"), None),
        P(("tile", "sub"), None),
        P("sub", None, None),
        P("sub", None, None, None),
        P("sub", None, None),
        P("sub", None, None),
        P("sub", None),
    )
    return jax.shard_map(
        per_device,
        mesh=mesh,
        in_specs=placed,
        out_specs=(
            P(None, "tile", "sub"),
            P("sub", None, None),
            P("sub", None, None, None),
            P("sub", None, None),
            P("sub", None, None),
            P("sub", None),
        ),
        check_vma=False,
    )
```

```python
import jax
import jax.numpy as jnp
from jax import lax
from jax.experimental import pallas as pl
from jax.experimental.pallas import tpu as pltpu
from jax.sharding import PartitionSpec as P

MESH = pl.DeviceIdType.MESH
F32 = jnp.float32
BF16 = jnp.bfloat16
LEV = 64
WIDTH = 192
CX = 16
CY = 256
NCOL = CX * CY
TILES = 8
SUBS = 16
SHARE = NCOL // SUBS
PARAMS = 136000
AUG = 16
LANES = 128
SPAN = CY + LANES
SLABS = CX + 4
CHUNK = 96
GROUP = 4
GRAD_ROWS = CHUNK * TILES
FIRST_INNER = LEV + AUG
FIRST_LAST = FIRST_INNER + 3 * (WIDTH + AUG)
ANY = pl.BlockSpec(memory_space=pl.ANY)
LIMIT = 58 * 2**20


def wrapped(index, step, count):
    return lax.rem(index + step + count, count)


def remote(source, target, send_sem, recv_sem, peer):
    return pltpu.make_async_remote_copy(
        src_ref=source,
        dst_ref=target,
        send_sem=send_sem,
        recv_sem=recv_sem,
        device_id=peer,
        device_id_type=MESH,
    )


def tiled(block):
    return block.reshape(LEV, CX // 8, 8, 2, LANES).transpose(0, 1, 3, 2, 4).reshape(-1, LANES)


def untiled(rows):
    return rows.reshape(LEV, CX // 8, 2, 8, LANES).transpose(0, 1, 3, 2, 4).reshape(LEV, CX, CY)


def tiled_row(x, half):
    return (x // 8) * 16 + half * 8 + x % 8


def lanes(shape):
    return lax.broadcasted_iota(jnp.int32, shape, 1)


def sublanes(shape):
    return lax.broadcasted_iota(jnp.int32, shape, 0)


def dot(left, right, contract=(1, 0)):
    return lax.dot_general(
        left, right, (((contract[0],), (contract[1],)), ((), ())), preferred_element_type=F32
    )


def near_sum(value):
    return pltpu.roll(value, 1, 1) + pltpu.roll(value, SPAN - 1, 1)


def silu_and_slope(preact):
    sigmoid_value = 0.5 + 0.5 * jnp.tanh(0.5 * preact)
    active = preact * sigmoid_value
    return active.astype(BF16), sigmoid_value + active * (1.0 - sigmoid_value)


def find_routes(order, counts, sub, routes, tables, sems):
    count_row = counts[...]
    square = (TILES * SUBS, TILES * SUBS)
    earlier = lanes(square)

    def starts_and_shift(device):
        before = earlier < device
        same = earlier % SUBS == device % SUBS
        start = jnp.sum(jnp.where(before, count_row, 0), axis=1, keepdims=True)
        within = jnp.sum(jnp.where(before & same, count_row, 0), axis=1, keepdims=True)
        block = lax.rem(device[:, 0:1] % SUBS - sub + SUBS, SUBS)
        return start, block * SHARE + within - start

    device = sublanes(square)
    start, shift = starts_and_shift(device)
    _, shift_before = starts_and_shift(jnp.maximum(device - 1, 0))
    change = shift - jnp.where(device[:, 0:1] == 0, 0, shift_before)
    width = 512
    outward = jnp.zeros((32, 256), F32)
    homeward = jnp.zeros((32, 256), F32)

    def spread(where, what):
        high = (sublanes((32, width)) == where // LANES).astype(F32).astype(BF16)
        hit = sublanes((LANES, width)) == where % LANES
        values = jnp.concatenate(
            [jnp.where(hit, what // LANES, 0), jnp.where(hit, what % LANES, 0)], axis=0
        )
        return dot(high, values.astype(F32).astype(BF16), (1, 1))

    for first in range(0, NCOL, width):
        place = lanes((1, width)) + first
        slot = place + jnp.sum(jnp.where(start <= place, change, 0), axis=0, keepdims=True)
        column = order[:, first : first + width]
        outward = outward + spread(slot, column)
        homeward = homeward + spread(column, slot)
    for k, table in enumerate((outward, homeward)):
        whole = table.astype(jnp.int32)
        tables[k] = jnp.clip(whole[:, 0:LANES] * LANES + whole[:, LANES:], 0, NCOL - 1)
    for k in range(2):
        copy = pltpu.make_async_copy(tables.at[k], routes.at[k], sems.at[k])
        copy.start()
        copy.wait()


def step_kernel(
    initial_hbm, targets_hbm, diffusivity_hbm, order_hbm, counts_hbm,
    w_first_hbm, w_inner_hbm, w_last_hbm, b_inner_hbm, b_last_hbm,
    result_hbm, step_first_hbm, step_inner_hbm, step_last_hbm, step_bias_inner_hbm, step_bias_last_hbm,
    initial, targets, diffusivity, order, counts, w_first, w_inner, w_last_t, b_inner, b_last,
    result, step_first, step_inner, step_last_t, step_bias_inner, step_bias_last,
    load_sem, store_sem,
    field, middle, rates, columns, tables, routes,
    xs, xr, ys, yr, cs, cr, gxs, gxr, gys, gyr, gcs, gcr,
    wt_first, wt_inner, w_last, bias,
    stage, send, recv, answer, back, rows, grads, total, wide, parts, whole,
    table_sem, halo_sem, halo_in_sem, ghalo_sem, ghalo_in_sem,
    out_sem, in_sem, ret_sem, back_sem, part_sem, part_in_sem, whole_sem, whole_in_sem,
):
    tile, sub = lax.axis_index("tile"), lax.axis_index("sub")
    up, down = wrapped(tile, 1, TILES), wrapped(tile, -1, TILES)
    right, left = wrapped(sub, 1, SUBS), wrapped(sub, -1, SUBS)
    around = (
        (down, sub), (up, sub), (tile, left), (tile, right),
        (down, left), (down, right), (up, left), (up, right),
    )
    peers = (
        [(tile, wrapped(sub, j, SUBS)) for j in range(1, SUBS)]
        + [(wrapped(tile, j, TILES), sub) for j in range(1, TILES)]
        + list(around[4:])
    )
    barrier = pltpu.get_barrier_semaphore()
    for peer in peers:
        pl.semaphore_signal(barrier, inc=1, device_id=peer, device_id_type=MESH)

    loads = [
        pltpu.make_async_copy(source, target, load_sem.at[k])
        for k, (source, target) in enumerate(
            (
                (initial_hbm, initial), (diffusivity_hbm, diffusivity), (order_hbm, order),
                (counts_hbm, counts), (w_first_hbm, w_first), (w_inner_hbm, w_inner),
                (w_last_hbm, w_last_t), (b_inner_hbm, b_inner), (b_last_hbm, b_last),
                (targets_hbm, targets),
            )
        )
    ]
    for load in loads:
        load.start()
    stores = [
        pltpu.make_async_copy(source, target, store_sem.at[k])
        for k, (source, target) in enumerate(
            (
                (result, result_hbm), (step_first, step_first_hbm), (step_inner, step_inner_hbm),
                (step_last_t, step_last_hbm), (step_bias_inner, step_bias_inner_hbm),
                (step_bias_last, step_bias_last_hbm),
            )
        )
    ]

    def cells(ref, x):
        return jnp.concatenate(
            [ref[pl.ds(tiled_row(x, h), LEV, stride=2 * CX), :] for h in range(2)], axis=1
        )

    def halo(group, k, sends, receives, out_sems, in_sems):
        place = {"x": k, "y": 2 + k, "c": 4 + k}[group]
        other = (3 - k) if group == "c" else (1 - k)
        opposite = place - k + other
        return remote(
            sends.at[k], receives.at[other], out_sems.at[place], in_sems.at[opposite], around[place]
        )

    def strip(tile_of, side):
        pair = lanes((LEV, LANES)) // 2
        packed = jnp.zeros((LEV, LANES), F32)
        for x in range(CX):
            moved = tile_of(x, side)
            shift = (2 * x + 2 * side) % LANES
            if shift:
                moved = pltpu.roll(moved, shift, 1)
            packed = jnp.where(pair == x, moved, packed)
        return packed

    def edge_tile(x, side):
        return field[x + 2, :, side * LANES : (side + 1) * LANES]

    low = lanes((LEV, LANES)) < LEV

    def halo_tile(from_left, from_right, x):
        back_right = pltpu.roll(from_right, LANES - 2 * x, 1) if x else from_right
        return jnp.where(low, back_right, pltpu.roll(from_left, LANES - 2 - 2 * x, 1))

    def fill(x, carry):
        field[x + 2, :, 0:CY] = cells(initial, x)
        return carry

    loads[0].wait()
    loads[1].wait()
    lax.fori_loop(0, CX, fill, 0)
    for side in range(2):
        for k in range(2):
            xs[side, k * LEV : (k + 1) * LEV, :] = field[2 + (k if side == 0 else CX - 2 + k), :, 0:CY]
        xs[side, 2 * LEV :, :] = diffusivity[8 * side : 8 * side + 8, :]
    for corner in range(4):
        side, edge = corner // 2, corner % 2
        cs[corner, 0:LEV, :] = edge_tile(0 if side == 0 else CX - 1, edge)
        cs[corner, LEV:, :] = diffusivity[8 * side : 8 * side + 8, edge * LANES : (edge + 1) * LANES]
    pl.semaphore_wait(barrier, len(peers))
    copies = []
    for side in range(2):
        copies.append(halo("x", side, xs, xr, halo_sem, halo_in_sem))
        copies[-1].start()
    for corner in range(4):
        copies.append(halo("c", corner, cs, cr, halo_sem, halo_in_sem))
        copies[-1].start()
    for side in range(2):
        ys[side, 0:LEV, :] = strip(edge_tile, side)
        ys[side, LEV:, :] = diffusivity[:, side * LANES : (side + 1) * LANES]
        copies.append(halo("y", side, ys, yr, halo_sem, halo_in_sem))
        copies[-1].start()

    for load in loads[2:]:
        load.wait()
    find_routes(order, counts, sub, routes, tables, table_sem)
    same = sublanes((WIDTH, WIDTH)) == lanes((WIDTH, WIDTH))
    unit = same.astype(F32).astype(BF16)
    wt_first[...] = dot(unit, w_first[...], (1, 1)).astype(BF16)
    for k in range(3):
        wt_inner[k] = dot(unit, w_inner[k], (1, 1)).astype(BF16)
    w_last[...] = dot(unit, w_last_t[...], (1, 1)).astype(BF16)
    for k in range(4):
        bias[k] = jnp.sum(jnp.where(same, b_inner[k : k + 1, :], 0.0), axis=1, keepdims=True)
    same_lev = sublanes((LEV, LEV)) == lanes((LEV, LEV))
    bias[4, 0:LEV, :] = jnp.sum(jnp.where(same_lev, b_last[...], 0.0), axis=1, keepdims=True)
    total[...] = jnp.zeros_like(total)

    for copy in copies:
        copy.wait_recv()
    rates[0:2, 0:CY] = xr[0, 2 * LEV + 6 :, :]
    rates[2 : CX + 2, 0:CY] = diffusivity[...]
    rates[CX + 2 : CX + 4, 0:CY] = xr[1, 2 * LEV : 2 * LEV + 2, :]
    first_rows = lanes((CX, LANES)) < LEV
    rates[0:8, CY:] = jnp.zeros((8, LANES), F32)
    rates[16:24, CY:] = jnp.zeros((8, LANES), F32)
    rates[2 : CX + 2, CY:] = jnp.where(first_rows, yr[1, LEV:, :], yr[0, LEV:, :])
    one_row = lanes((1, LANES)) < LEV
    rates[1:2, CY:] = jnp.where(one_row, cr[1, LEV + 7 :, :], cr[0, LEV + 7 :, :])
    rates[CX + 2 : CX + 3, CY:] = jnp.where(
        one_row, cr[3, LEV : LEV + 1, :], cr[2, LEV : LEV + 1, :]
    )

    def spread_halo(x_in, y_in, c_in):
        for side in range(2):
            for k in range(2):
                slab = k if side == 0 else CX + 2 + k
                field[slab, :, 0:CY] = x_in[side, k * LEV : (k + 1) * LEV, :].astype(F32)
            outer = 0 if side == 0 else CX + 3
            field[outer, :, CY:] = jnp.zeros((LEV, LANES), F32)
            inner = 1 if side == 0 else CX + 2
            field[inner, :, CY:] = jnp.where(
                low, c_in[2 * side + 1, 0:LEV, :].astype(F32), c_in[2 * side, 0:LEV, :].astype(F32)
            )
        from_left, from_right = y_in[0, 0:LEV, :].astype(F32), y_in[1, 0:LEV, :].astype(F32)
        for x in range(CX):
            field[x + 2, :, CY:] = halo_tile(from_left, from_right, x)

    spread_halo(xr, yr, cr)

    def diffused(ref, slab):
        now = ref[slab]
        near = ref[slab - 1] + ref[slab + 1] + near_sum(now)
        return now + rates[pl.ds(slab, 1), :] * (near - 4.0 * now)

    def forward_first(slab, carry):
        middle[slab] = diffused(field, slab)
        return carry

    lax.fori_loop(1, CX + 3, forward_first, 0)

    def forward_second(x, carry):
        later = diffused(middle, x + 2)[:, 0:CY]
        both = jnp.concatenate([later, later - cells(targets, x)], axis=0)
        columns[pl.ds(pl.multiple_of(x * CY, CY), CY), :] = both.T
        return carry

    lax.fori_loop(0, CX, forward_second, 0)

    def outgoing(j):
        return remote(send.at[j], recv.at[j], out_sem.at[j], in_sem.at[j], (tile, wrapped(sub, j, SUBS)))

    def returning(j):
        return remote(answer.at[j], back.at[j], ret_sem.at[j], back_sem.at[j], (tile, wrapped(sub, -j, SUBS)))

    def gathered(table, line, source, target):
        for first in range(0, LANES, 16):
            taken = [source[pl.ds(routes[table, line, first + k], 1), :] for k in range(16)]
            for k in range(16):
                target[first + k : first + k + 1, :] = taken[k]

    def push(step, carry):
        j = lax.rem(step, SUBS)
        for half in range(2):
            gathered(0, 2 * j + half, columns, stage.at[half])
        send[j] = stage[...].reshape(SHARE, LANES).astype(BF16)

        @pl.when(j > 0)
        def _():
            outgoing(j).start()

        return carry

    lax.fori_loop(1, SUBS + 1, push, 0)
    recv[0] = send[0]

    extra = (sublanes((AUG, SHARE)) == 0).astype(F32).astype(BF16)

    def with_ones(value):
        return jnp.concatenate([value, extra], axis=0)

    def some_blocks(turn, carry):
        @pl.when(turn > 0)
        def _():
            outgoing(GROUP * turn).wait_recv()

        for b in range(1, GROUP):
            outgoing(GROUP * turn + b).wait_recv()
        both = range(GROUP)
        turned = [recv[GROUP * turn + b].astype(F32).T for b in both]
        inputs = [turned[b][:LEV].astype(BF16) for b in both]
        current = inputs
        feeds, slopes = [inputs], []
        for k in range(4):
            weight = wt_first[...] if k == 0 else wt_inner[k - 1]
            outs = [silu_and_slope(dot(weight, current[b]) + bias[k]) for b in both]
            current = [outs[b][0] for b in both]
            feeds.append(current)
            slopes.append([outs[b][1] for b in both])
        residue = [
            turned[b][LEV:] + dot(w_last_t[...], current[b]) + bias[4, 0:LEV, :] for b in both
        ]
        error = [residue[b].astype(BF16) for b in both]
        total[FIRST_LAST:, 0 : WIDTH + AUG] += sum(
            dot(error[b], with_ones(current[b]), (1, 1)) for b in both
        )
        carried = [dot(w_last[...], error[b]) for b in both]
        for k in (3, 2, 1, 0):
            error = [(carried[b] * slopes[k][b]).astype(BF16) for b in both]
            row = FIRST_INNER + (k - 1) * (WIDTH + AUG) if k else 0
            high = (WIDTH if k else LEV) + AUG
            total[row : row + high, 0:WIDTH] += sum(
                dot(with_ones(feeds[k][b]), error[b], (1, 1)) for b in both
            )
            weight = w_inner[k - 1] if k else w_first[...]
            carried = [dot(weight, error[b]) for b in both]
        half = SHARE // 2
        for b in both:
            outcome = residue[b] + carried[b]
            packed = jnp.concatenate([outcome[:, :half], outcome[:, half:]], axis=0)
            answer[GROUP * turn + b] = packed.T.astype(BF16)

        @pl.when(turn > 0)
        def _():
            returning(GROUP * turn).start()

        for b in range(1, GROUP):
            returning(GROUP * turn + b).start()
        return carry

    lax.fori_loop(0, SUBS // GROUP, some_blocks, 0)

    wide[...] = total[...].astype(BF16)

    def part(j):
        owner = wrapped(tile, j, TILES)
        first = pl.multiple_of(owner * CHUNK, CHUNK)
        return remote(
            wide.at[pl.ds(first, CHUNK)], parts.at[j], part_sem.at[j], part_in_sem.at[j], (owner, sub)
        )

    def share_of(j):
        return remote(
            whole.at[0], whole.at[j], whole_sem.at[j], whole_in_sem.at[j], (wrapped(tile, j, TILES), sub)
        )

    for j in range(1, TILES):
        part(j).start()

    def unpack(j, source):
        block = source.astype(F32)
        first = pl.multiple_of(j * SHARE, SHARE)
        rows[pl.ds(first, SHARE // 2), :] = block
        rows[pl.ds(first + SHARE // 2, SHARE // 2), :] = pltpu.roll(block, LEV, 1)

    unpack(0, answer[0])

    def take(j, carry):
        returning(j).wait_recv()
        unpack(j, back[j])
        return carry

    lax.fori_loop(1, SUBS, take, 0)

    left_half = lanes((CY, LANES)) < LEV

    def home(x):
        def some(line, carry):
            gathered(1, x * 2 + line, rows, grads.at[line])
            return carry

        lax.fori_loop(0, 4, some, 0)
        slab = [grads[2 * k : 2 * k + 2].reshape(CY, LANES) for k in range(2)]
        turned = jnp.where(left_half, slab[0], pltpu.roll(slab[1], LEV, 1)).T
        for k in range(2):
            field[x + k + 2, :, 0:CY] = turned[k * LEV : (k + 1) * LEV]

    copies = list(copies)
    ghalos = []

    def home_edge(side, carry):
        home(side * (CX - 2))
        return carry

    lax.fori_loop(0, 2, home_edge, 0)
    for side in range(2):
        x = 0 if side == 0 else CX - 2
        for k in range(2):
            gxs[side, k * LEV : (k + 1) * LEV, :] = field[x + k + 2, :, 0:CY].astype(BF16)
        for edge in range(2):
            gcs[2 * side + edge] = edge_tile(0 if side == 0 else CX - 1, edge).astype(BF16)
        ghalos.append(halo("x", side, gxs, gxr, ghalo_sem, ghalo_in_sem))
        for edge in range(2):
            ghalos.append(halo("c", 2 * side + edge, gcs, gcr, ghalo_sem, ghalo_in_sem))
        for copy in ghalos[-3:]:
            copy.start()

    mine = pl.multiple_of(tile * CHUNK, CHUNK)
    summed = wide[pl.ds(mine, CHUNK), :].astype(F32)
    for j in range(1, TILES):
        part(j).wait_recv()
        summed = summed + parts[j].astype(F32)
    whole[0] = summed.astype(BF16)
    for j in range(1, TILES):
        share_of(j).start()

    def home_pair(pair, carry):
        home(2 * pair)
        return carry

    lax.fori_loop(1, CX // 2 - 1, home_pair, 0)
    for side in range(2):
        gys[side] = strip(edge_tile, side).astype(BF16)
        ghalos.append(halo("y", side, gys, gyr, ghalo_sem, ghalo_in_sem))
        ghalos[-1].start()

    for j in range(1, TILES):
        share_of(j).wait_recv()
    for j in range(TILES):
        owner = wrapped(tile, -j, TILES)
        total[pl.ds(pl.multiple_of(owner * CHUNK, CHUNK), CHUNK), :] = whole[j].astype(F32)
    everything = total[...]
    squares = jnp.sum(jnp.sum(everything * everything, axis=0, keepdims=True), axis=1, keepdims=True)
    factor = lax.rsqrt(squares / PARAMS + 1e-06)
    step_first[...] = total[0:LEV, 0:WIDTH] * factor
    step_bias_inner[0:1, :] = total[LEV : LEV + 1, 0:WIDTH] * factor
    for k in range(3):
        row = FIRST_INNER + k * (WIDTH + AUG)
        step_inner[k] = total[row : row + WIDTH, 0:WIDTH] * factor
        step_bias_inner[k + 1 : k + 2, :] = total[row + WIDTH : row + WIDTH + 1, 0:WIDTH] * factor
    step_last_t[...] = total[FIRST_LAST:, 0:WIDTH] * factor
    last_bias = total[FIRST_LAST:, WIDTH : WIDTH + 1] * factor
    step_bias_last[...] = jnp.sum(jnp.where(same_lev, last_bias, 0.0), axis=0, keepdims=True)
    for store in stores[1:]:
        store.start()

    for copy in ghalos:
        copy.wait_recv()
    spread_halo(gxr, gyr, gcr)

    def adjoint(ref, slab):
        rate = [rates[pl.ds(slab + k, 1), :] for k in (-1, 0, 1)]
        now = ref[slab]
        flow = rate[1] * now
        near = rate[0] * ref[slab - 1] + rate[2] * ref[slab + 1] + near_sum(flow)
        return now + (near - 4.0 * flow)

    def adjoint_first(slab, carry):
        middle[slab] = adjoint(field, slab)
        return carry

    lax.fori_loop(1, CX + 3, adjoint_first, 0)

    def adjoint_second(x, carry):
        done = adjoint(middle, x + 2)
        for h in range(2):
            result[pl.ds(tiled_row(x, h), LEV, stride=2 * CX), :] = done[:, h * LANES : (h + 1) * LANES]
        return carry

    lax.fori_loop(0, CX, adjoint_second, 0)

    stores[0].start()

    def settle(j, carry):
        outgoing(j).wait_send()
        returning(j).wait_send()
        return carry

    lax.fori_loop(1, SUBS, settle, 0)
    for j in range(1, TILES):
        part(j).wait_send()
        share_of(j).wait_send()
    for copy in copies + ghalos:
        copy.wait_send()
    for store in stores:
        store.wait()


def copy_kernel(*refs):
    sources, targets, held = refs[0:6], refs[6:12], refs[12:18]
    in_sem, out_sem = refs[18:]
    loads = [pltpu.make_async_copy(sources[k], held[k], in_sem.at[k]) for k in range(6)]
    stores = [pltpu.make_async_copy(held[k], targets[k], out_sem.at[k]) for k in range(6)]
    for load in loads:
        load.start()
    for load, store in zip(loads, stores):
        load.wait()
        store.start()
    for store in stores:
        store.wait()


def both_ways(shape, kind):
    return [pltpu.VMEM(shape, kind), pltpu.VMEM(shape, kind)]


def per_device(
    initial, targets, diffusivity, column_order, send_counts, w_first, w_inner, w_last, b_inner, b_last
):
    slabs = pltpu.VMEM((SLABS, LEV, SPAN), F32)
    made = pl.pallas_call(
        step_kernel,
        out_shape=(
            jax.ShapeDtypeStruct((LEV * CX * 2, LANES), F32),
            jax.ShapeDtypeStruct((LEV, WIDTH), F32),
            jax.ShapeDtypeStruct((3, WIDTH, WIDTH), F32),
            jax.ShapeDtypeStruct((LEV, WIDTH), F32),
            jax.ShapeDtypeStruct((4, WIDTH), F32),
            jax.ShapeDtypeStruct((1, LEV), F32),
        ),
        in_specs=[ANY] * 10,
        out_specs=(ANY,) * 6,
        scratch_shapes=[
            pltpu.VMEM((LEV * CX * 2, LANES), F32),
            pltpu.VMEM((LEV * CX * 2, LANES), F32),
            pltpu.VMEM((CX, CY), F32),
            pltpu.VMEM((1, NCOL), jnp.int32),
            pltpu.VMEM((1, TILES * SUBS), jnp.int32),
            pltpu.VMEM((LEV, WIDTH), BF16),
            pltpu.VMEM((3, WIDTH, WIDTH), BF16),
            pltpu.VMEM((LEV, WIDTH), BF16),
            pltpu.VMEM((4, WIDTH), F32),
            pltpu.VMEM((1, LEV), F32),
            pltpu.VMEM((LEV * CX * 2, LANES), F32),
            pltpu.VMEM((LEV, WIDTH), F32),
            pltpu.VMEM((3, WIDTH, WIDTH), F32),
            pltpu.VMEM((LEV, WIDTH), F32),
            pltpu.VMEM((4, WIDTH), F32),
            pltpu.VMEM((1, LEV), F32),
            pltpu.SemaphoreType.DMA((10,)),
            pltpu.SemaphoreType.DMA((6,)),
            slabs,
            slabs,
            pltpu.VMEM((24, SPAN), F32),
            pltpu.VMEM((NCOL, LANES), F32),
            pltpu.VMEM((2, NCOL // LANES, LANES), jnp.int32),
            pltpu.SMEM((2, NCOL // LANES, LANES), jnp.int32),
        ]
        + both_ways((2, 2 * LEV + 8, CY), F32)
        + both_ways((2, LEV + CX, LANES), F32)
        + both_ways((4, LEV + 8, LANES), F32)
        + both_ways((2, 2 * LEV, CY), BF16)
        + both_ways((2, LEV, LANES), BF16)
        + both_ways((4, LEV, LANES), BF16)
        + [
            pltpu.VMEM((WIDTH, LEV), BF16),
            pltpu.VMEM((3, WIDTH, WIDTH), BF16),
            pltpu.VMEM((WIDTH, LEV), BF16),
            pltpu.VMEM((5, WIDTH, 1), F32),
            pltpu.VMEM((2, LANES, LANES), F32),
        ]
        + both_ways((SUBS, SHARE, LANES), BF16)
        + both_ways((SUBS, SHARE // 2, LANES), BF16)
        + [
            pltpu.VMEM((NCOL, LANES), F32),
            pltpu.VMEM((4, LANES, LANES), F32),
            pltpu.VMEM((GRAD_ROWS, 256), F32),
            pltpu.VMEM((GRAD_ROWS, 256), BF16),
        ]
        + both_ways((TILES, CHUNK, 256), BF16)
        + [pltpu.SemaphoreType.DMA((2,))]
        + [pltpu.SemaphoreType.DMA((8,))] * 4
        + [pltpu.SemaphoreType.DMA((SUBS,))] * 4
        + [pltpu.SemaphoreType.DMA((TILES,))] * 4,
        compiler_params=pltpu.CompilerParams(
            collective_id=0, has_side_effects=True, vmem_limit_bytes=LIMIT
        ),
        name="step",
    )(
        tiled(initial),
        tiled(targets),
        diffusivity,
        column_order,
        send_counts,
        w_first[0],
        w_inner[0],
        w_last[0].T,
        b_inner[0],
        b_last,
    )
    result, step_first, step_inner, step_last_t, step_bias_inner, step_bias_last = pl.pallas_call(
        copy_kernel,
        out_shape=tuple(jax.ShapeDtypeStruct(one.shape, one.dtype) for one in made),
        in_specs=[ANY] * 6,
        out_specs=(ANY,) * 6,
        scratch_shapes=[pltpu.VMEM(one.shape, one.dtype) for one in made]
        + [pltpu.SemaphoreType.DMA((6,))] * 2,
        name="finish",
    )(*made)
    return (
        untiled(result),
        step_first[None],
        step_inner[None],
        step_last_t.T[None],
        step_bias_inner[None],
        step_bias_last,
    )


def solution(mesh):
    placed = (
        P(None, "tile", "sub"),
        P(None, "tile", "sub"),
        P("tile", "sub"),
        P(("tile", "sub"), None),
        P(("tile", "sub"), None),
        P("sub", None, None),
        P("sub", None, None, None),
        P("sub", None, None),
        P("sub", None, None),
        P("sub", None),
    )
    return jax.shard_map(
        per_device,
        mesh=mesh,
        in_specs=placed,
        out_specs=(
            P(None, "tile", "sub"),
            P("sub", None, None),
            P("sub", None, None, None),
            P("sub", None, None),
            P("sub", None, None),
            P("sub", None),
        ),
        check_vma=False,
    )
```

```python
import jax
import jax.numpy as jnp
from jax import lax
from jax.experimental import pallas as pl
from jax.experimental.pallas import tpu as pltpu
from jax.sharding import PartitionSpec as P

MESH = pl.DeviceIdType.MESH
F32 = jnp.float32
BF16 = jnp.bfloat16
LEV = 64
WIDTH = 192
CX = 16
CY = 256
NCOL = CX * CY
TILES = 8
SUBS = 16
SHARE = NCOL // SUBS
PARAMS = 136000
AUG = 16
LANES = 128
SPAN = CY + LANES
SLABS = CX + 4
CHUNK = 96
GROUP = 4
GRAD_ROWS = CHUNK * TILES
FIRST_INNER = LEV + AUG
FIRST_LAST = FIRST_INNER + 3 * (WIDTH + AUG)
ANY = pl.BlockSpec(memory_space=pl.ANY)
LIMIT = 58 * 2**20


def wrapped(index, step, count):
    return lax.rem(index + step + count, count)


def remote(source, target, send_sem, recv_sem, peer):
    return pltpu.make_async_remote_copy(
        src_ref=source,
        dst_ref=target,
        send_sem=send_sem,
        recv_sem=recv_sem,
        device_id=peer,
        device_id_type=MESH,
    )


def gray(step):
    return step + step // 2 - 2 * (step // 3)


def partner(sub, j, sign):
    late = jnp.minimum(j // 2, 1)
    turned = late * (1 - j % 2) + (1 - late) * (j % 2)
    x = gray(j // 2 % 4)
    high = (sub // 8 + turned) % 2
    middle = (sub // 2 + sign * x + 4) % 4
    return high * 8 + middle * 2 + (sub + j // 8) % 2


def place_of(sub, other):
    turned = (other // 8 + sub // 8) % 2
    step = (other + sub) % 2 * 4 + gray((other // 2 - sub // 2 + 8) % 4)
    late = jnp.minimum(step, 1)
    return 2 * step + late * (1 - turned) + (1 - late) * turned


def tiled(block):
    return block.reshape(LEV, CX // 8, 8, 2, LANES).transpose(0, 1, 3, 2, 4).reshape(-1, LANES)


def untiled(rows):
    return rows.reshape(LEV, CX // 8, 2, 8, LANES).transpose(0, 1, 3, 2, 4).reshape(LEV, CX, CY)


def tiled_row(x, half):
    return (x // 8) * 16 + half * 8 + x % 8


def lanes(shape):
    return lax.broadcasted_iota(jnp.int32, shape, 1)


def sublanes(shape):
    return lax.broadcasted_iota(jnp.int32, shape, 0)


def dot(left, right, contract=(1, 0)):
    return lax.dot_general(
        left, right, (((contract[0],), (contract[1],)), ((), ())), preferred_element_type=F32
    )


def near_sum(value):
    return pltpu.roll(value, 1, 1) + pltpu.roll(value, SPAN - 1, 1)


def silu_and_slope(preact):
    sigmoid_value = 0.5 + 0.5 * jnp.tanh(0.5 * preact)
    active = preact * sigmoid_value
    return active.astype(BF16), sigmoid_value + active * (1.0 - sigmoid_value)


def find_routes(order, counts, sub, routes, tables, sems):
    count_row = counts[...]
    square = (TILES * SUBS, TILES * SUBS)
    earlier = lanes(square)

    def starts_and_shift(device):
        before = earlier < device
        same = earlier % SUBS == device % SUBS
        start = jnp.sum(jnp.where(before, count_row, 0), axis=1, keepdims=True)
        within = jnp.sum(jnp.where(before & same, count_row, 0), axis=1, keepdims=True)
        block = place_of(sub, device[:, 0:1] % SUBS)
        return start, block * SHARE + within - start

    device = sublanes(square)
    start, shift = starts_and_shift(device)
    _, shift_before = starts_and_shift(jnp.maximum(device - 1, 0))
    change = shift - jnp.where(device[:, 0:1] == 0, 0, shift_before)
    width = 512
    outward = jnp.zeros((32, 256), F32)
    homeward = jnp.zeros((32, 256), F32)

    def spread(where, what):
        high = (sublanes((32, width)) == where // LANES).astype(F32).astype(BF16)
        hit = sublanes((LANES, width)) == where % LANES
        values = jnp.concatenate(
            [jnp.where(hit, what // LANES, 0), jnp.where(hit, what % LANES, 0)], axis=0
        )
        return dot(high, values.astype(F32).astype(BF16), (1, 1))

    for first in range(0, NCOL, width):
        place = lanes((1, width)) + first
        slot = place + jnp.sum(jnp.where(start <= place, change, 0), axis=0, keepdims=True)
        column = order[:, first : first + width]
        outward = outward + spread(slot, column)
        homeward = homeward + spread(column, slot)
    for k, table in enumerate((outward, homeward)):
        whole = table.astype(jnp.int32)
        tables[k] = jnp.clip(whole[:, 0:LANES] * LANES + whole[:, LANES:], 0, NCOL - 1)
    for k in range(2):
        copy = pltpu.make_async_copy(tables.at[k], routes.at[k], sems.at[k])
        copy.start()
        copy.wait()


def step_kernel(
    initial_hbm, targets_hbm, diffusivity_hbm, order_hbm, counts_hbm,
    w_first_hbm, w_inner_hbm, w_last_hbm, b_inner_hbm, b_last_hbm,
    result_hbm, step_first_hbm, step_inner_hbm, step_last_hbm, step_bias_inner_hbm, step_bias_last_hbm,
    initial, targets, diffusivity, order, counts, w_first, w_inner, w_last_t, b_inner, b_last,
    result, step_first, step_inner, step_last_t, step_bias_inner, step_bias_last,
    load_sem, store_sem,
    field, middle, rates, columns, tables, routes,
    xs, xr, ys, yr, cs, cr, gxs, gxr, gys, gyr, gcs, gcr,
    wt_first, wt_inner, w_last, bias,
    stage, send, recv, answer, back, rows, grads, edges, total, wide, parts, whole,
    table_sem, halo_sem, halo_in_sem, ghalo_sem, ghalo_in_sem,
    out_sem, in_sem, ret_sem, back_sem, part_sem, part_in_sem, whole_sem, whole_in_sem,
):
    tile, sub = lax.axis_index("tile"), lax.axis_index("sub")
    up, down = wrapped(tile, 1, TILES), wrapped(tile, -1, TILES)
    right, left = wrapped(sub, 1, SUBS), wrapped(sub, -1, SUBS)
    around = (
        (down, sub), (up, sub), (tile, left), (tile, right),
        (down, left), (down, right), (up, left), (up, right),
    )
    peers = (
        [(tile, wrapped(sub, j, SUBS)) for j in range(1, SUBS)]
        + [(wrapped(tile, j, TILES), sub) for j in range(1, TILES)]
        + list(around[4:])
    )
    barrier = pltpu.get_barrier_semaphore()
    for peer in peers:
        pl.semaphore_signal(barrier, inc=1, device_id=peer, device_id_type=MESH)

    loads = [
        pltpu.make_async_copy(source, target, load_sem.at[k])
        for k, (source, target) in enumerate(
            (
                (initial_hbm, initial), (diffusivity_hbm, diffusivity), (order_hbm, order),
                (counts_hbm, counts), (w_first_hbm, w_first), (w_inner_hbm, w_inner),
                (w_last_hbm, w_last_t), (b_inner_hbm, b_inner), (b_last_hbm, b_last),
                (targets_hbm, targets),
            )
        )
    ]
    for load in loads:
        load.start()
    stores = [
        pltpu.make_async_copy(source, target, store_sem.at[k])
        for k, (source, target) in enumerate(
            (
                (result, result_hbm), (step_first, step_first_hbm), (step_inner, step_inner_hbm),
                (step_last_t, step_last_hbm), (step_bias_inner, step_bias_inner_hbm),
                (step_bias_last, step_bias_last_hbm),
            )
        )
    ]

    def cells(ref, x):
        return jnp.concatenate(
            [ref[pl.ds(tiled_row(x, h), LEV, stride=2 * CX), :] for h in range(2)], axis=1
        )

    def halo(group, k, sends, receives, out_sems, in_sems):
        place = {"x": k, "y": 2 + k, "c": 4 + k}[group]
        other = (3 - k) if group == "c" else (1 - k)
        opposite = place - k + other
        return remote(
            sends.at[k], receives.at[other], out_sems.at[place], in_sems.at[opposite], around[place]
        )

    def strip(tile_of, side):
        pair = lanes((LEV, LANES)) // 2
        packed = jnp.zeros((LEV, LANES), F32)
        for x in range(CX):
            moved = tile_of(x, side)
            shift = (2 * x + 2 * side) % LANES
            if shift:
                moved = pltpu.roll(moved, shift, 1)
            packed = jnp.where(pair == x, moved, packed)
        return packed

    def edge_tile(x, side):
        return field[x + 2, :, side * LANES : (side + 1) * LANES]

    low = lanes((LEV, LANES)) < LEV

    def halo_tile(from_left, from_right, x):
        back_right = pltpu.roll(from_right, LANES - 2 * x, 1) if x else from_right
        return jnp.where(low, back_right, pltpu.roll(from_left, LANES - 2 - 2 * x, 1))

    def fill(x, carry):
        field[x + 2, :, 0:CY] = cells(initial, x)
        return carry

    loads[0].wait()
    loads[1].wait()
    lax.fori_loop(0, CX, fill, 0)
    rate_high = diffusivity[...].astype(BF16)
    rate_parts = (rate_high, (diffusivity[...] - rate_high.astype(F32)).astype(BF16))
    same_lev = sublanes((LEV, LEV)) == lanes((LEV, LEV))
    for side in range(2):
        for k in range(2):
            edge = field[2 + (k if side == 0 else CX - 2 + k), :, 0:CY]
            xs[side, k * LEV : (k + 1) * LEV, :] = edge.astype(BF16)
        for k in range(2):
            xs[side, 2 * LEV + k * CX : 2 * LEV + (k + 1) * CX, :] = rate_parts[k]
    for corner in range(4):
        side, edge = corner // 2, corner % 2
        x = 0 if side == 0 else CX - 1
        y = edge * (CY - 1)
        cell = jnp.where(same_lev, field[x + 2, :, y : y + 1], 0.0)
        cs[corner, 0:1, 0:LEV] = jnp.sum(cell, axis=0, keepdims=True)
        cs[corner, 1:2, :] = diffusivity[x : x + 1, edge * LANES : (edge + 1) * LANES]
    pl.semaphore_wait(barrier, len(peers))
    copies = []
    for side in range(2):
        copies.append(halo("x", side, xs, xr, halo_sem, halo_in_sem))
        copies[-1].start()
    for corner in range(4):
        copies.append(halo("c", corner, cs, cr, halo_sem, halo_in_sem))
        copies[-1].start()
    for side in range(2):
        ys[side, 0:LEV, :] = strip(edge_tile, side).astype(BF16)
        for k in range(2):
            part_rows = rate_parts[k][:, side * LANES : (side + 1) * LANES]
            ys[side, LEV + k * CX : LEV + (k + 1) * CX, :] = part_rows
        copies.append(halo("y", side, ys, yr, halo_sem, halo_in_sem))
        copies[-1].start()

    for load in loads[2:]:
        load.wait()
    find_routes(order, counts, sub, routes, tables, table_sem)
    same = sublanes((WIDTH, WIDTH)) == lanes((WIDTH, WIDTH))
    unit = same.astype(F32).astype(BF16)
    wt_first[...] = dot(unit, w_first[...], (1, 1)).astype(BF16)
    for k in range(3):
        wt_inner[k] = dot(unit, w_inner[k], (1, 1)).astype(BF16)
    w_last[...] = dot(unit, w_last_t[...], (1, 1)).astype(BF16)
    for k in range(4):
        bias[k] = jnp.sum(jnp.where(same, b_inner[k : k + 1, :], 0.0), axis=1, keepdims=True)
    bias[4, 0:LEV, :] = jnp.sum(jnp.where(same_lev, b_last[...], 0.0), axis=1, keepdims=True)
    total[...] = jnp.zeros_like(total)

    for copy in copies:
        copy.wait_recv()
    def arrived_rates(message, first):
        high, rest = (message[first + k * CX : first + (k + 1) * CX, :].astype(F32) for k in range(2))
        return high + rest

    rates[0:2, 0:CY] = arrived_rates(xr.at[0], 2 * LEV)[CX - 2 :, :]
    rates[2 : CX + 2, 0:CY] = diffusivity[...]
    rates[CX + 2 : CX + 4, 0:CY] = arrived_rates(xr.at[1], 2 * LEV)[0:2, :]
    first_rows = lanes((CX, LANES)) < LEV
    rates[0:8, CY:] = jnp.zeros((8, LANES), F32)
    rates[16:24, CY:] = jnp.zeros((8, LANES), F32)
    rates[2 : CX + 2, CY:] = jnp.where(
        first_rows, arrived_rates(yr.at[1], LEV), arrived_rates(yr.at[0], LEV)
    )
    one_row = lanes((1, LANES)) < LEV
    rates[1:2, CY:] = jnp.where(one_row, cr[1, 1:2, :], cr[0, 1:2, :])
    rates[CX + 2 : CX + 3, CY:] = jnp.where(one_row, cr[3, 1:2, :], cr[2, 1:2, :])

    def spread_halo(x_in, y_in, c_in):
        for side in range(2):
            for k in range(2):
                slab = k if side == 0 else CX + 2 + k
                field[slab, :, 0:CY] = x_in[side, k * LEV : (k + 1) * LEV, :].astype(F32)
            outer = 0 if side == 0 else CX + 3
            field[outer, :, CY:] = jnp.zeros((LEV, LANES), F32)
            inner = 1 if side == 0 else CX + 2
            cell = [
                jnp.sum(jnp.where(same_lev, c_in[2 * side + k, 0:1, 0:LEV], 0.0), axis=1, keepdims=True)
                for k in range(2)
            ]
            field[inner, :, CY:] = jnp.where(low, cell[1], cell[0])
        from_left, from_right = y_in[0, 0:LEV, :].astype(F32), y_in[1, 0:LEV, :].astype(F32)
        for x in range(CX):
            field[x + 2, :, CY:] = halo_tile(from_left, from_right, x)

    spread_halo(xr, yr, cr)

    def diffused(ref, slab):
        now = ref[slab]
        near = ref[slab - 1] + ref[slab + 1] + near_sum(now)
        return now + rates[pl.ds(slab, 1), :] * (near - 4.0 * now)

    def forward_first(pair, carry):
        done = [diffused(field, 2 * pair + k) for k in (1, 2)]
        for k in (1, 2):
            middle[2 * pair + k] = done[k - 1]
        return carry

    lax.fori_loop(0, CX // 2 + 1, forward_first, 0)

    def forward_second(pair, carry):
        for x in (2 * pair, 2 * pair + 1):
            later = diffused(middle, x + 2)[:, 0:CY]
            both = jnp.concatenate([later, later - cells(targets, x)], axis=0)
            columns[pl.ds(pl.multiple_of(x * CY, CY), CY), :] = both.T
        return carry

    lax.fori_loop(0, CX // 2, forward_second, 0)

    def outgoing(j):
        return remote(send.at[j], recv.at[j], out_sem.at[j], in_sem.at[j], (tile, partner(sub, j, 1)))

    def returning(j):
        return remote(answer.at[j], back.at[j], ret_sem.at[j], back_sem.at[j], (tile, partner(sub, j, -1)))

    def gathered(table, line, source, target):
        for first in range(0, LANES, 16):
            taken = [source[pl.ds(routes[table, line, first + k], 1), :] for k in range(16)]
            for k in range(16):
                target[first + k : first + k + 1, :] = taken[k]

    def push(step, carry):
        j = lax.rem(step, SUBS)
        for half in range(2):
            gathered(0, 2 * j + half, columns, stage.at[half])
        send[j] = stage[...].reshape(SHARE, LANES).astype(BF16)

        @pl.when(j > 0)
        def _():
            outgoing(j).start()

        return carry

    lax.fori_loop(1, SUBS + 1, push, 0)
    recv[0] = send[0]

    extra = (sublanes((AUG, SHARE)) == 0).astype(F32).astype(BF16)

    def with_ones(value):
        return jnp.concatenate([value, extra], axis=0)

    def some_blocks(turn, carry):
        @pl.when(turn > 0)
        def _():
            outgoing(GROUP * turn).wait_recv()

        for b in range(1, GROUP):
            outgoing(GROUP * turn + b).wait_recv()
        both = range(GROUP)
        turned = [recv[GROUP * turn + b].astype(F32).T for b in both]
        inputs = [turned[b][:LEV].astype(BF16) for b in both]
        current = inputs
        feeds, slopes = [inputs], []
        for k in range(4):
            weight = wt_first[...] if k == 0 else wt_inner[k - 1]
            outs = [silu_and_slope(dot(weight, current[b]) + bias[k]) for b in both]
            current = [outs[b][0] for b in both]
            feeds.append(current)
            slopes.append([outs[b][1] for b in both])
        residue = [
            turned[b][LEV:] + dot(w_last_t[...], current[b]) + bias[4, 0:LEV, :] for b in both
        ]
        error = [residue[b].astype(BF16) for b in both]
        total[FIRST_LAST:, 0 : WIDTH + AUG] += sum(
            dot(error[b], with_ones(current[b]), (1, 1)) for b in both
        )
        carried = [dot(w_last[...], error[b]) for b in both]
        for k in (3, 2, 1, 0):
            error = [(carried[b] * slopes[k][b]).astype(BF16) for b in both]
            row = FIRST_INNER + (k - 1) * (WIDTH + AUG) if k else 0
            high = (WIDTH if k else LEV) + AUG
            total[row : row + high, 0:WIDTH] += sum(
                dot(with_ones(feeds[k][b]), error[b], (1, 1)) for b in both
            )
            weight = w_inner[k - 1] if k else w_first[...]
            carried = [dot(weight, error[b]) for b in both]
        half = SHARE // 2
        for b in both:
            outcome = residue[b] + carried[b]
            packed = jnp.concatenate([outcome[:, :half], outcome[:, half:]], axis=0)
            answer[GROUP * turn + b] = packed.T.astype(BF16)

        @pl.when(turn > 0)
        def _():
            returning(GROUP * turn).start()

        for b in range(1, GROUP):
            returning(GROUP * turn + b).start()
        return carry

    lax.fori_loop(0, SUBS // GROUP, some_blocks, 0)

    wide[...] = total[...].astype(BF16)

    def part(j):
        owner = wrapped(tile, j, TILES)
        first = pl.multiple_of(owner * CHUNK, CHUNK)
        return remote(
            wide.at[pl.ds(first, CHUNK)], parts.at[j], part_sem.at[j], part_in_sem.at[j], (owner, sub)
        )

    def share_of(j):
        return remote(
            whole.at[0], whole.at[j], whole_sem.at[j], whole_in_sem.at[j], (wrapped(tile, j, TILES), sub)
        )

    for j in range(1, TILES):
        part(j).start()

    def unpack(j, source):
        block = source.astype(F32)
        first = pl.multiple_of(j * SHARE, SHARE)
        rows[pl.ds(first, SHARE // 2), :] = block
        rows[pl.ds(first + SHARE // 2, SHARE // 2), :] = pltpu.roll(block, LEV, 1)

    unpack(0, answer[0])

    def take(j, carry):
        returning(j).wait_recv()
        unpack(j, back[j])
        return carry

    lax.fori_loop(1, SUBS, take, 0)

    left_half = lanes((CY, LANES)) < LEV

    def home(x):
        def some(line, carry):
            gathered(1, x * 2 + line, rows, grads.at[line])
            return carry

        lax.fori_loop(0, 4, some, 0)
        slab = [grads[2 * k : 2 * k + 2].reshape(CY, LANES) for k in range(2)]
        turned = jnp.where(left_half, slab[0], pltpu.roll(slab[1], LEV, 1)).T
        for k in range(2):
            field[x + k + 2, :, 0:CY] = turned[k * LEV : (k + 1) * LEV]

    ghalos = []

    def home_row(line, k):
        return rows[pl.ds(routes[1, line, k], 1), :]

    for corner in range(4):
        line = (0 if corner < 2 else 2 * CX - 2) + corner % 2
        gcs[corner, 0:1, :] = home_row(line, (LANES - 1) * (corner % 2))
        ghalos.append(halo("c", corner, gcs, gcr, ghalo_sem, ghalo_in_sem))
        ghalos[-1].start()
    edges[2 * 2 * CX :, :] = jnp.zeros((LANES - 4 * CX, LANES), F32)
    for side in range(2):
        taken = [
            home_row(2 * x + side, (LANES - 2) * side + k) for x in range(CX) for k in range(2)
        ]
        for k in range(2 * CX):
            edges[2 * CX * side + k : 2 * CX * side + k + 1, :] = taken[k]
    turned_edges = edges[...].T[0:LEV, :]
    for side in range(2):
        moved = pltpu.roll(turned_edges, LANES - 2 * CX, 1) if side else turned_edges
        gys[side] = moved.astype(BF16)
        ghalos.append(halo("y", side, gys, gyr, ghalo_sem, ghalo_in_sem))
        ghalos[-1].start()

    def home_edge(side, carry):
        home(side * (CX - 2))
        return carry

    lax.fori_loop(0, 2, home_edge, 0)
    for side in range(2):
        x = 0 if side == 0 else CX - 2
        for k in range(2):
            gxs[side, k * LEV : (k + 1) * LEV, :] = field[x + k + 2, :, 0:CY].astype(BF16)
        ghalos.append(halo("x", side, gxs, gxr, ghalo_sem, ghalo_in_sem))
        ghalos[-1].start()

    mine = pl.multiple_of(tile * CHUNK, CHUNK)
    summed = wide[pl.ds(mine, CHUNK), :].astype(F32)
    for j in range(1, TILES):
        part(j).wait_recv()
        summed = summed + parts[j].astype(F32)
    whole[0] = summed.astype(BF16)
    for j in range(1, TILES):
        share_of(j).start()

    def home_pair(pair, carry):
        home(2 * pair)
        return carry

    lax.fori_loop(1, CX // 2 - 1, home_pair, 0)
    for j in range(1, TILES):
        share_of(j).wait_recv()
    for j in range(TILES):
        owner = wrapped(tile, -j, TILES)
        total[pl.ds(pl.multiple_of(owner * CHUNK, CHUNK), CHUNK), :] = whole[j].astype(F32)
    everything = total[...]
    squares = jnp.sum(jnp.sum(everything * everything, axis=0, keepdims=True), axis=1, keepdims=True)
    factor = lax.rsqrt(squares / PARAMS + 1e-06)
    step_first[...] = total[0:LEV, 0:WIDTH] * factor
    step_bias_inner[0:1, :] = total[LEV : LEV + 1, 0:WIDTH] * factor
    for k in range(3):
        row = FIRST_INNER + k * (WIDTH + AUG)
        step_inner[k] = total[row : row + WIDTH, 0:WIDTH] * factor
        step_bias_inner[k + 1 : k + 2, :] = total[row + WIDTH : row + WIDTH + 1, 0:WIDTH] * factor
    step_last_t[...] = total[FIRST_LAST:, 0:WIDTH] * factor
    last_bias = total[FIRST_LAST:, WIDTH : WIDTH + 1] * factor
    step_bias_last[...] = jnp.sum(jnp.where(same_lev, last_bias, 0.0), axis=0, keepdims=True)
    for store in stores[1:]:
        store.start()

    for copy in ghalos:
        copy.wait_recv()
    spread_halo(gxr, gyr, gcr)

    def adjoint(ref, slab):
        rate = [rates[pl.ds(slab + k, 1), :] for k in (-1, 0, 1)]
        now = ref[slab]
        flow = rate[1] * now
        near = rate[0] * ref[slab - 1] + rate[2] * ref[slab + 1] + near_sum(flow)
        return now + (near - 4.0 * flow)

    def adjoint_first(pair, carry):
        done = [adjoint(field, 2 * pair + k) for k in (1, 2)]
        for k in (1, 2):
            middle[2 * pair + k] = done[k - 1]
        return carry

    lax.fori_loop(0, CX // 2 + 1, adjoint_first, 0)

    def adjoint_second(pair, carry):
        done = [adjoint(middle, 2 * pair + k + 2) for k in range(2)]
        for k in range(2):
            for h in range(2):
                row = tiled_row(2 * pair + k, h)
                result[pl.ds(row, LEV, stride=2 * CX), :] = done[k][:, h * LANES : (h + 1) * LANES]
        return carry

    lax.fori_loop(0, CX // 2, adjoint_second, 0)

    stores[0].start()

    def settle(j, carry):
        outgoing(j).wait_send()
        returning(j).wait_send()
        return carry

    lax.fori_loop(1, SUBS, settle, 0)
    for j in range(1, TILES):
        part(j).wait_send()
        share_of(j).wait_send()
    for copy in copies + ghalos:
        copy.wait_send()
    for store in stores:
        store.wait()


def copy_kernel(*refs):
    sources, targets, held = refs[0:6], refs[6:12], refs[12:18]
    in_sem, out_sem = refs[18:]
    loads = [pltpu.make_async_copy(sources[k], held[k], in_sem.at[k]) for k in range(6)]
    stores = [pltpu.make_async_copy(held[k], targets[k], out_sem.at[k]) for k in range(6)]
    for load in loads:
        load.start()
    for load, store in zip(loads, stores):
        load.wait()
        store.start()
    for store in stores:
        store.wait()


def both_ways(shape, kind):
    return [pltpu.VMEM(shape, kind), pltpu.VMEM(shape, kind)]


def per_device(
    initial, targets, diffusivity, column_order, send_counts, w_first, w_inner, w_last, b_inner, b_last
):
    slabs = pltpu.VMEM((SLABS, LEV, SPAN), F32)
    made = pl.pallas_call(
        step_kernel,
        out_shape=(
            jax.ShapeDtypeStruct((LEV * CX * 2, LANES), F32),
            jax.ShapeDtypeStruct((LEV, WIDTH), F32),
            jax.ShapeDtypeStruct((3, WIDTH, WIDTH), F32),
            jax.ShapeDtypeStruct((LEV, WIDTH), F32),
            jax.ShapeDtypeStruct((4, WIDTH), F32),
            jax.ShapeDtypeStruct((1, LEV), F32),
        ),
        in_specs=[ANY] * 10,
        out_specs=(ANY,) * 6,
        scratch_shapes=[
            pltpu.VMEM((LEV * CX * 2, LANES), F32),
            pltpu.VMEM((LEV * CX * 2, LANES), F32),
            pltpu.VMEM((CX, CY), F32),
            pltpu.VMEM((1, NCOL), jnp.int32),
            pltpu.VMEM((1, TILES * SUBS), jnp.int32),
            pltpu.VMEM((LEV, WIDTH), BF16),
            pltpu.VMEM((3, WIDTH, WIDTH), BF16),
            pltpu.VMEM((LEV, WIDTH), BF16),
            pltpu.VMEM((4, WIDTH), F32),
            pltpu.VMEM((1, LEV), F32),
            pltpu.VMEM((LEV * CX * 2, LANES), F32),
            pltpu.VMEM((LEV, WIDTH), F32),
            pltpu.VMEM((3, WIDTH, WIDTH), F32),
            pltpu.VMEM((LEV, WIDTH), F32),
            pltpu.VMEM((4, WIDTH), F32),
            pltpu.VMEM((1, LEV), F32),
            pltpu.SemaphoreType.DMA((10,)),
            pltpu.SemaphoreType.DMA((6,)),
            slabs,
            slabs,
            pltpu.VMEM((24, SPAN), F32),
            pltpu.VMEM((NCOL, LANES), F32),
            pltpu.VMEM((2, NCOL // LANES, LANES), jnp.int32),
            pltpu.SMEM((2, NCOL // LANES, LANES), jnp.int32),
        ]
        + both_ways((2, 2 * LEV + 2 * CX, CY), BF16)
        + both_ways((2, LEV + 2 * CX, LANES), BF16)
        + both_ways((4, 8, LANES), F32)
        + both_ways((2, 2 * LEV, CY), BF16)
        + both_ways((2, LEV, LANES), BF16)
        + both_ways((4, 8, LANES), F32)
        + [
            pltpu.VMEM((WIDTH, LEV), BF16),
            pltpu.VMEM((3, WIDTH, WIDTH), BF16),
            pltpu.VMEM((WIDTH, LEV), BF16),
            pltpu.VMEM((5, WIDTH, 1), F32),
            pltpu.VMEM((2, LANES, LANES), F32),
        ]
        + both_ways((SUBS, SHARE, LANES), BF16)
        + both_ways((SUBS, SHARE // 2, LANES), BF16)
        + [
            pltpu.VMEM((NCOL, LANES), F32),
            pltpu.VMEM((4, LANES, LANES), F32),
            pltpu.VMEM((LANES, LANES), F32),
            pltpu.VMEM((GRAD_ROWS, 256), F32),
            pltpu.VMEM((GRAD_ROWS, 256), BF16),
        ]
        + both_ways((TILES, CHUNK, 256), BF16)
        + [pltpu.SemaphoreType.DMA((2,))]
        + [pltpu.SemaphoreType.DMA((8,))] * 4
        + [pltpu.SemaphoreType.DMA((SUBS,))] * 4
        + [pltpu.SemaphoreType.DMA((TILES,))] * 4,
        compiler_params=pltpu.CompilerParams(
            collective_id=0, has_side_effects=True, vmem_limit_bytes=LIMIT
        ),
        name="step",
    )(
        tiled(initial),
        tiled(targets),
        diffusivity,
        column_order,
        send_counts,
        w_first[0],
        w_inner[0],
        w_last[0].T,
        b_inner[0],
        b_last,
    )
    result, step_first, step_inner, step_last_t, step_bias_inner, step_bias_last = pl.pallas_call(
        copy_kernel,
        out_shape=tuple(jax.ShapeDtypeStruct(one.shape, one.dtype) for one in made),
        in_specs=[ANY] * 6,
        out_specs=(ANY,) * 6,
        scratch_shapes=[pltpu.VMEM(one.shape, one.dtype) for one in made]
        + [pltpu.SemaphoreType.DMA((6,))] * 2,
        name="finish",
    )(*made)
    return (
        untiled(result),
        step_first[None],
        step_inner[None],
        step_last_t.T[None],
        step_bias_inner[None],
        step_bias_last,
    )


def solution(mesh):
    placed = (
        P(None, "tile", "sub"),
        P(None, "tile", "sub"),
        P("tile", "sub"),
        P(("tile", "sub"), None),
        P(("tile", "sub"), None),
        P("sub", None, None),
        P("sub", None, None, None),
        P("sub", None, None),
        P("sub", None, None),
        P("sub", None),
    )
    return jax.shard_map(
        per_device,
        mesh=mesh,
        in_specs=placed,
        out_specs=(
            P(None, "tile", "sub"),
            P("sub", None, None),
            P("sub", None, None, None),
            P("sub", None, None),
            P("sub", None, None),
            P("sub", None),
        ),
        check_vma=False,
    )
```

```python
import jax
import jax.numpy as jnp
from jax import lax
from jax.experimental import pallas as pl
from jax.experimental.pallas import tpu as pltpu
from jax.sharding import PartitionSpec as P

MESH = pl.DeviceIdType.MESH
F32 = jnp.float32
BF16 = jnp.bfloat16
LEV = 64
WIDTH = 192
CX = 16
CY = 256
NCOL = CX * CY
TILES = 8
SUBS = 16
SHARE = NCOL // SUBS
PARAMS = 136000
AUG = 16
LANES = 128
SPAN = CY + LANES
SLABS = CX + 4
CHUNK = 96
GROUP = 4
GRAD_ROWS = CHUNK * TILES
FIRST_INNER = LEV + AUG
FIRST_LAST = FIRST_INNER + 3 * (WIDTH + AUG)
ANY = pl.BlockSpec(memory_space=pl.ANY)
LIMIT = 58 * 2**20


def wrapped(index, step, count):
    return lax.rem(index + step + count, count)


def remote(source, target, send_sem, recv_sem, peer):
    return pltpu.make_async_remote_copy(
        src_ref=source,
        dst_ref=target,
        send_sem=send_sem,
        recv_sem=recv_sem,
        device_id=peer,
        device_id_type=MESH,
    )


PAIRS = ((0, 0), (2, 0), (2, 1), (1, 0), (3, 0), (1, 1), (3, 1), (0, 1))


def crossing(j):
    late = jnp.minimum(j // 2, 1)
    return late * (1 - j % 2) + (1 - late) * (j % 2)


def partner(tile, sub, j, sign):
    turned = crossing(j)
    x = sum(jnp.where(j // 2 == k, pair[0], 0) for k, pair in enumerate(PAIRS))
    core = sum(jnp.where(j // 2 == k, pair[1], 0) for k, pair in enumerate(PAIRS))
    high = (sub // 8 + turned) % 2
    middle = (sub // 2 + sign * x + 4) % 4
    return (tile + 4 * turned) % TILES, high * 8 + middle * 2 + (sub + core) % 2


def place_of(sub, other):
    turned = (other // 8 + sub // 8) % 2
    x = (other // 2 - sub // 2 + 8) % 4
    core = (other + sub) % 2
    step = sum(
        jnp.where((x == pair[0]) & (core == pair[1]), k, 0) for k, pair in enumerate(PAIRS)
    )
    late = jnp.minimum(step, 1)
    return 2 * step + late * (1 - turned) + (1 - late) * turned


def tiled(block):
    return block.reshape(LEV, CX // 8, 8, 2, LANES).transpose(0, 1, 3, 2, 4).reshape(-1, LANES)


def untiled(rows):
    return rows.reshape(LEV, CX // 8, 2, 8, LANES).transpose(0, 1, 3, 2, 4).reshape(LEV, CX, CY)


def tiled_row(x, half):
    return (x // 8) * 16 + half * 8 + x % 8


def lanes(shape):
    return lax.broadcasted_iota(jnp.int32, shape, 1)


def sublanes(shape):
    return lax.broadcasted_iota(jnp.int32, shape, 0)


def dot(left, right, contract=(1, 0)):
    return lax.dot_general(
        left, right, (((contract[0],), (contract[1],)), ((), ())), preferred_element_type=F32
    )


def near_sum(value):
    return pltpu.roll(value, 1, 1) + pltpu.roll(value, SPAN - 1, 1)


def silu_and_slope(preact):
    sigmoid_value = 0.5 + 0.5 * jnp.tanh(0.5 * preact)
    active = preact * sigmoid_value
    return active.astype(BF16), sigmoid_value + active * (1.0 - sigmoid_value)


def find_routes(order, counts, sub, routes, tables, sems):
    count_row = counts[...]
    square = (TILES * SUBS, TILES * SUBS)
    earlier = lanes(square)

    def starts_and_shift(device):
        before = earlier < device
        same = earlier % SUBS == device % SUBS
        start = jnp.sum(jnp.where(before, count_row, 0), axis=1, keepdims=True)
        within = jnp.sum(jnp.where(before & same, count_row, 0), axis=1, keepdims=True)
        block = place_of(sub, device[:, 0:1] % SUBS)
        return start, block * SHARE + within - start

    device = sublanes(square)
    start, shift = starts_and_shift(device)
    _, shift_before = starts_and_shift(jnp.maximum(device - 1, 0))
    change = shift - jnp.where(device[:, 0:1] == 0, 0, shift_before)
    width = 512
    outward = jnp.zeros((32, 256), F32)
    homeward = jnp.zeros((32, 256), F32)

    def spread(where, what):
        high = (sublanes((32, width)) == where // LANES).astype(F32).astype(BF16)
        hit = sublanes((LANES, width)) == where % LANES
        values = jnp.concatenate(
            [jnp.where(hit, what // LANES, 0), jnp.where(hit, what % LANES, 0)], axis=0
        )
        return dot(high, values.astype(F32).astype(BF16), (1, 1))

    for first in range(0, NCOL, width):
        place = lanes((1, width)) + first
        slot = place + jnp.sum(jnp.where(start <= place, change, 0), axis=0, keepdims=True)
        column = order[:, first : first + width]
        outward = outward + spread(slot, column)
        homeward = homeward + spread(column, slot)
    for k, table in enumerate((outward, homeward)):
        whole = table.astype(jnp.int32)
        tables[k] = jnp.clip(whole[:, 0:LANES] * LANES + whole[:, LANES:], 0, NCOL - 1)
    for k in range(2):
        copy = pltpu.make_async_copy(tables.at[k], routes.at[k], sems.at[k])
        copy.start()
        copy.wait()


def step_kernel(
    initial_hbm, targets_hbm, diffusivity_hbm, order_hbm, counts_hbm,
    w_first_hbm, w_inner_hbm, w_last_hbm, b_inner_hbm, b_last_hbm,
    result_hbm, step_first_hbm, step_inner_hbm, step_last_hbm, step_bias_inner_hbm, step_bias_last_hbm,
    initial, targets, diffusivity, order, counts, w_first, w_inner, w_last_t, b_inner, b_last,
    result, step_first, step_inner, step_last_t, step_bias_inner, step_bias_last,
    load_sem, store_sem,
    field, middle, rates, columns, tables, routes,
    xs, xr, ys, yr, cs, cr, gxs, gxr, gys, gyr, gcs, gcr,
    wt_first, wt_inner, w_last, bias,
    stage, send, recv, answer, back, rows, grads_even, grads_odd, edges, total, wide, parts, whole,
    table_sem, halo_sem, halo_in_sem, ghalo_sem, ghalo_in_sem,
    out_sem, in_sem, ret_sem, back_sem, part_sem, part_in_sem, whole_sem, whole_in_sem,
):
    tile, sub = lax.axis_index("tile"), lax.axis_index("sub")
    up, down = wrapped(tile, 1, TILES), wrapped(tile, -1, TILES)
    right, left = wrapped(sub, 1, SUBS), wrapped(sub, -1, SUBS)
    around = (
        (down, sub), (up, sub), (tile, left), (tile, right),
        (down, left), (down, right), (up, left), (up, right),
    )
    peers = (
        [partner(tile, sub, j, 1) for j in range(1, SUBS)]
        + [(wrapped(tile, j, TILES), sub) for j in range(1, TILES)]
        + list(around[2:])
    )
    barrier = pltpu.get_barrier_semaphore()
    for peer in peers:
        pl.semaphore_signal(barrier, inc=1, device_id=peer, device_id_type=MESH)

    loads = [
        pltpu.make_async_copy(source, target, load_sem.at[k])
        for k, (source, target) in enumerate(
            (
                (initial_hbm, initial), (diffusivity_hbm, diffusivity), (order_hbm, order),
                (counts_hbm, counts), (w_first_hbm, w_first), (w_inner_hbm, w_inner),
                (w_last_hbm, w_last_t), (b_inner_hbm, b_inner), (b_last_hbm, b_last),
                (targets_hbm, targets),
            )
        )
    ]
    for load in loads:
        load.start()
    stores = [
        pltpu.make_async_copy(source, target, store_sem.at[k])
        for k, (source, target) in enumerate(
            (
                (result, result_hbm), (step_first, step_first_hbm), (step_inner, step_inner_hbm),
                (step_last_t, step_last_hbm), (step_bias_inner, step_bias_inner_hbm),
                (step_bias_last, step_bias_last_hbm),
            )
        )
    ]

    def cells(ref, x):
        return jnp.concatenate(
            [ref[pl.ds(tiled_row(x, h), LEV, stride=2 * CX), :] for h in range(2)], axis=1
        )

    def halo(group, k, sends, receives, out_sems, in_sems):
        place = {"x": k, "y": 2 + k, "c": 4 + k}[group]
        other = (3 - k) if group == "c" else (1 - k)
        opposite = place - k + other
        return remote(
            sends.at[k], receives.at[other], out_sems.at[place], in_sems.at[opposite], around[place]
        )

    def strip(tile_of, side):
        pair = lanes((LEV, LANES)) // 2
        packed = jnp.zeros((LEV, LANES), F32)
        for x in range(CX):
            moved = tile_of(x, side)
            shift = (2 * x + 2 * side) % LANES
            if shift:
                moved = pltpu.roll(moved, shift, 1)
            packed = jnp.where(pair == x, moved, packed)
        return packed

    def edge_tile(x, side):
        return field[x + 2, :, side * LANES : (side + 1) * LANES]

    low = lanes((LEV, LANES)) < LEV

    def halo_tile(from_left, from_right, x):
        back_right = pltpu.roll(from_right, LANES - 2 * x, 1) if x else from_right
        return jnp.where(low, back_right, pltpu.roll(from_left, LANES - 2 - 2 * x, 1))

    def fill(x, carry):
        field[x + 2, :, 0:CY] = cells(initial, x)
        return carry

    loads[0].wait()
    loads[1].wait()
    lax.fori_loop(0, CX, fill, 0)
    rate_high = diffusivity[...].astype(BF16)
    rate_parts = (rate_high, (diffusivity[...] - rate_high.astype(F32)).astype(BF16))
    same_lev = sublanes((LEV, LEV)) == lanes((LEV, LEV))
    for side in range(2):
        for k in range(2):
            edge = field[2 + (k if side == 0 else CX - 2 + k), :, 0:CY]
            xs[side, k * LEV : (k + 1) * LEV, :] = edge.astype(BF16)
        for k in range(2):
            xs[side, 2 * LEV + k * CX : 2 * LEV + (k + 1) * CX, :] = rate_parts[k]
    for corner in range(4):
        side, edge = corner // 2, corner % 2
        x = 0 if side == 0 else CX - 1
        y = edge * (CY - 1)
        cell = jnp.where(same_lev, field[x + 2, :, y : y + 1], 0.0)
        cs[corner, 0:1, 0:LEV] = jnp.sum(cell, axis=0, keepdims=True)
        cs[corner, 1:2, :] = diffusivity[x : x + 1, edge * LANES : (edge + 1) * LANES]
    pl.semaphore_wait(barrier, len(peers))
    copies = []
    for side in range(2):
        copies.append(halo("x", side, xs, xr, halo_sem, halo_in_sem))
        copies[-1].start()
    for corner in range(4):
        copies.append(halo("c", corner, cs, cr, halo_sem, halo_in_sem))
        copies[-1].start()
    for side in range(2):
        ys[side, 0:LEV, :] = strip(edge_tile, side).astype(BF16)
        for k in range(2):
            part_rows = rate_parts[k][:, side * LANES : (side + 1) * LANES]
            ys[side, LEV + k * CX : LEV + (k + 1) * CX, :] = part_rows
        copies.append(halo("y", side, ys, yr, halo_sem, halo_in_sem))
        copies[-1].start()

    for load in loads[2:]:
        load.wait()
    find_routes(order, counts, sub, routes, tables, table_sem)
    for copy in copies:
        copy.wait_recv()
    def arrived_rates(message, first):
        high, rest = (message[first + k * CX : first + (k + 1) * CX, :].astype(F32) for k in range(2))
        return high + rest

    rates[0:2, 0:CY] = arrived_rates(xr.at[0], 2 * LEV)[CX - 2 :, :]
    rates[2 : CX + 2, 0:CY] = diffusivity[...]
    rates[CX + 2 : CX + 4, 0:CY] = arrived_rates(xr.at[1], 2 * LEV)[0:2, :]
    first_rows = lanes((CX, LANES)) < LEV
    rates[0:8, CY:] = jnp.zeros((8, LANES), F32)
    rates[16:24, CY:] = jnp.zeros((8, LANES), F32)
    rates[2 : CX + 2, CY:] = jnp.where(
        first_rows, arrived_rates(yr.at[1], LEV), arrived_rates(yr.at[0], LEV)
    )
    one_row = lanes((1, LANES)) < LEV
    rates[1:2, CY:] = jnp.where(one_row, cr[1, 1:2, :], cr[0, 1:2, :])
    rates[CX + 2 : CX + 3, CY:] = jnp.where(one_row, cr[3, 1:2, :], cr[2, 1:2, :])

    def spread_halo(x_in, y_in, c_in):
        for side in range(2):
            for k in range(2):
                slab = k if side == 0 else CX + 2 + k
                field[slab, :, 0:CY] = x_in[side, k * LEV : (k + 1) * LEV, :].astype(F32)
            outer = 0 if side == 0 else CX + 3
            field[outer, :, CY:] = jnp.zeros((LEV, LANES), F32)
            inner = 1 if side == 0 else CX + 2
            cell = [
                jnp.sum(jnp.where(same_lev, c_in[2 * side + k, 0:1, 0:LEV], 0.0), axis=1, keepdims=True)
                for k in range(2)
            ]
            field[inner, :, CY:] = jnp.where(low, cell[1], cell[0])
        from_left, from_right = y_in[0, 0:LEV, :].astype(F32), y_in[1, 0:LEV, :].astype(F32)
        for x in range(CX):
            field[x + 2, :, CY:] = halo_tile(from_left, from_right, x)

    spread_halo(xr, yr, cr)

    def diffused(ref, slab):
        now = ref[slab]
        near = ref[slab - 1] + ref[slab + 1] + near_sum(now)
        return now + rates[pl.ds(slab, 1), :] * (near - 4.0 * now)

    def forward_first(pair, carry):
        done = [diffused(field, 2 * pair + k) for k in (1, 2)]
        for k in (1, 2):
            middle[2 * pair + k] = done[k - 1]
        return carry

    lax.fori_loop(0, CX // 2 + 1, forward_first, 0)

    def forward_second(pair, carry):
        for x in (2 * pair, 2 * pair + 1):
            later = diffused(middle, x + 2)[:, 0:CY]
            both = jnp.concatenate([later, later - cells(targets, x)], axis=0)
            columns[pl.ds(pl.multiple_of(x * CY, CY), CY), :] = both.T
        return carry

    lax.fori_loop(0, CX // 2, forward_second, 0)

    def outgoing(j):
        return remote(send.at[j], recv.at[j], out_sem.at[j], in_sem.at[j], partner(tile, sub, j, 1))

    def returning(j):
        return remote(answer.at[j], back.at[j], ret_sem.at[j], back_sem.at[j], partner(tile, sub, j, -1))

    def gathered(table, line, source, target):
        for first in range(0, LANES, 16):
            taken = [source[pl.ds(routes[table, line, first + k], 1), :] for k in range(16)]
            for k in range(16):
                target[first + k : first + k + 1, :] = taken[k]

    def push(step, carry):
        j = lax.rem(step, SUBS)
        for half in range(2):
            gathered(0, 2 * j + half, columns, stage.at[half])
        send[j] = stage[...].reshape(SHARE, LANES).astype(BF16)

        @pl.when(j > 0)
        def _():
            outgoing(j).start()

        return carry

    lax.fori_loop(1, SUBS + 1, push, 0)
    recv[0] = send[0]

    same = sublanes((WIDTH, WIDTH)) == lanes((WIDTH, WIDTH))
    unit = same.astype(F32).astype(BF16)
    wt_first[...] = dot(unit, w_first[...], (1, 1)).astype(BF16)
    for k in range(3):
        wt_inner[k] = dot(unit, w_inner[k], (1, 1)).astype(BF16)
    w_last[...] = dot(unit, w_last_t[...], (1, 1)).astype(BF16)
    for k in range(4):
        bias[k] = jnp.sum(jnp.where(same, b_inner[k : k + 1, :], 0.0), axis=1, keepdims=True)
    bias[4, 0:LEV, :] = jnp.sum(jnp.where(same_lev, b_last[...], 0.0), axis=1, keepdims=True)
    total[...] = jnp.zeros_like(total)

    extra = (sublanes((AUG, SHARE)) == 0).astype(F32).astype(BF16)

    def with_ones(value):
        return jnp.concatenate([value, extra], axis=0)

    def some_blocks(turn, carry):
        @pl.when(turn > 0)
        def _():
            outgoing(GROUP * turn).wait_recv()

        for b in range(1, GROUP):
            outgoing(GROUP * turn + b).wait_recv()
        both = range(GROUP)
        turned = [recv[GROUP * turn + b].astype(F32).T for b in both]
        inputs = [turned[b][:LEV].astype(BF16) for b in both]
        current = inputs
        feeds, slopes = [inputs], []
        for k in range(4):
            weight = wt_first[...] if k == 0 else wt_inner[k - 1]
            outs = [silu_and_slope(dot(weight, current[b]) + bias[k]) for b in both]
            current = [outs[b][0] for b in both]
            feeds.append(current)
            slopes.append([outs[b][1] for b in both])
        residue = [
            turned[b][LEV:] + dot(w_last_t[...], current[b]) + bias[4, 0:LEV, :] for b in both
        ]
        error = [residue[b].astype(BF16) for b in both]
        total[FIRST_LAST:, 0 : WIDTH + AUG] += sum(
            dot(error[b], with_ones(current[b]), (1, 1)) for b in both
        )
        carried = [dot(w_last[...], error[b]) for b in both]
        for k in (3, 2, 1, 0):
            error = [(carried[b] * slopes[k][b]).astype(BF16) for b in both]
            row = FIRST_INNER + (k - 1) * (WIDTH + AUG) if k else 0
            high = (WIDTH if k else LEV) + AUG
            total[row : row + high, 0:WIDTH] += sum(
                dot(with_ones(feeds[k][b]), error[b], (1, 1)) for b in both
            )
            weight = w_inner[k - 1] if k else w_first[...]
            carried = [dot(weight, error[b]) for b in both]
        half = SHARE // 2
        for b in both:
            outcome = residue[b] + carried[b]
            packed = jnp.concatenate([outcome[:, :half], outcome[:, half:]], axis=0)
            answer[GROUP * turn + b] = packed.T.astype(BF16)

        @pl.when(turn > 0)
        def _():
            returning(GROUP * turn).start()

        for b in range(1, GROUP):
            returning(GROUP * turn + b).start()
        return carry

    lax.fori_loop(0, SUBS // GROUP, some_blocks, 0)

    wide[...] = total[...].astype(BF16)

    def part(j):
        owner = wrapped(tile, j, TILES)
        first = pl.multiple_of(owner * CHUNK, CHUNK)
        return remote(
            wide.at[pl.ds(first, CHUNK)], parts.at[j], part_sem.at[j], part_in_sem.at[j], (owner, sub)
        )

    def share_of(j):
        return remote(
            whole.at[0], whole.at[j], whole_sem.at[j], whole_in_sem.at[j], (wrapped(tile, j, TILES), sub)
        )

    for j in range(1, TILES):
        part(j).start()

    def unpack(j, source):
        block = source.astype(F32)
        first = pl.multiple_of(j * SHARE, SHARE)
        rows[pl.ds(first, SHARE // 2), :] = block
        rows[pl.ds(first + SHARE // 2, SHARE // 2), :] = pltpu.roll(block, LEV, 1)

    unpack(0, answer[0])

    def take(j, carry):
        returning(j).wait_recv()
        unpack(j, back[j])
        return carry

    lax.fori_loop(1, SUBS, take, 0)

    left_half = lanes((CY, LANES)) < LEV
    grads = (grads_even, grads_odd)

    def home(first_slabs):
        for held, x in zip(grads, first_slabs):
            for line in range(4):
                gathered(1, x * 2 + line, rows, held.at[line])
        for held, x in zip(grads, first_slabs):
            slab = [held[2 * k : 2 * k + 2].reshape(CY, LANES) for k in range(2)]
            turned = jnp.where(left_half, slab[0], pltpu.roll(slab[1], LEV, 1)).T
            for k in range(2):
                field[x + k + 2, :, 0:CY] = turned[k * LEV : (k + 1) * LEV]

    ghalos = []

    def home_row(line, k):
        return rows[pl.ds(routes[1, line, k], 1), :]

    for corner in range(4):
        line = (0 if corner < 2 else 2 * CX - 2) + corner % 2
        gcs[corner, 0:1, :] = home_row(line, (LANES - 1) * (corner % 2))
        ghalos.append(halo("c", corner, gcs, gcr, ghalo_sem, ghalo_in_sem))
        ghalos[-1].start()
    edges[2 * 2 * CX :, :] = jnp.zeros((LANES - 4 * CX, LANES), F32)
    for side in range(2):
        taken = [
            home_row(2 * x + side, (LANES - 2) * side + k) for x in range(CX) for k in range(2)
        ]
        for k in range(2 * CX):
            edges[2 * CX * side + k : 2 * CX * side + k + 1, :] = taken[k]
    turned_edges = edges[...].T[0:LEV, :]
    for side in range(2):
        moved = pltpu.roll(turned_edges, LANES - 2 * CX, 1) if side else turned_edges
        gys[side] = moved.astype(BF16)
        ghalos.append(halo("y", side, gys, gyr, ghalo_sem, ghalo_in_sem))
        ghalos[-1].start()

    home((0, CX - 2))
    for side in range(2):
        x = 0 if side == 0 else CX - 2
        for k in range(2):
            gxs[side, k * LEV : (k + 1) * LEV, :] = field[x + k + 2, :, 0:CY].astype(BF16)
        ghalos.append(halo("x", side, gxs, gxr, ghalo_sem, ghalo_in_sem))
        ghalos[-1].start()

    mine = pl.multiple_of(tile * CHUNK, CHUNK)
    summed = wide[pl.ds(mine, CHUNK), :].astype(F32)
    for j in range(1, TILES):
        part(j).wait_recv()
        summed = summed + parts[j].astype(F32)
    whole[0] = summed.astype(BF16)
    for j in range(1, TILES):
        share_of(j).start()

    def home_pairs(turn, carry):
        home((4 * turn + 2, 4 * turn + 4))
        return carry

    lax.fori_loop(0, CX // 4 - 1, home_pairs, 0)
    for copy in ghalos:
        copy.wait_recv()
    spread_halo(gxr, gyr, gcr)

    def adjoint(ref, slab):
        rate = [rates[pl.ds(slab + k, 1), :] for k in (-1, 0, 1)]
        now = ref[slab]
        flow = rate[1] * now
        near = rate[0] * ref[slab - 1] + rate[2] * ref[slab + 1] + near_sum(flow)
        return now + (near - 4.0 * flow)

    def adjoint_first(pair, carry):
        done = [adjoint(field, 2 * pair + k) for k in (1, 2)]
        for k in (1, 2):
            middle[2 * pair + k] = done[k - 1]
        return carry

    lax.fori_loop(0, CX // 2 + 1, adjoint_first, 0)

    for j in range(1, TILES):
        share_of(j).wait_recv()
    for j in range(TILES):
        owner = wrapped(tile, -j, TILES)
        total[pl.ds(pl.multiple_of(owner * CHUNK, CHUNK), CHUNK), :] = whole[j].astype(F32)
    everything = total[...]
    squares = jnp.sum(jnp.sum(everything * everything, axis=0, keepdims=True), axis=1, keepdims=True)
    factor = lax.rsqrt(squares / PARAMS + 1e-06)
    step_first[...] = total[0:LEV, 0:WIDTH] * factor
    step_bias_inner[0:1, :] = total[LEV : LEV + 1, 0:WIDTH] * factor
    for k in range(3):
        row = FIRST_INNER + k * (WIDTH + AUG)
        step_inner[k] = total[row : row + WIDTH, 0:WIDTH] * factor
        step_bias_inner[k + 1 : k + 2, :] = total[row + WIDTH : row + WIDTH + 1, 0:WIDTH] * factor
    step_last_t[...] = total[FIRST_LAST:, 0:WIDTH] * factor
    last_bias = total[FIRST_LAST:, WIDTH : WIDTH + 1] * factor
    step_bias_last[...] = jnp.sum(jnp.where(same_lev, last_bias, 0.0), axis=0, keepdims=True)
    for store in stores[1:]:
        store.start()

    def adjoint_second(pair, carry):
        done = [adjoint(middle, 2 * pair + k + 2) for k in range(2)]
        for k in range(2):
            for h in range(2):
                row = tiled_row(2 * pair + k, h)
                result[pl.ds(row, LEV, stride=2 * CX), :] = done[k][:, h * LANES : (h + 1) * LANES]
        return carry

    lax.fori_loop(0, CX // 2, adjoint_second, 0)

    stores[0].start()

    def settle(j, carry):
        outgoing(j).wait_send()
        returning(j).wait_send()
        return carry

    lax.fori_loop(1, SUBS, settle, 0)
    for j in range(1, TILES):
        part(j).wait_send()
        share_of(j).wait_send()
    for copy in copies + ghalos:
        copy.wait_send()
    for store in stores:
        store.wait()


def copy_kernel(*refs):
    sources, targets, held = refs[0:6], refs[6:12], refs[12:18]
    in_sem, out_sem = refs[18:]
    loads = [pltpu.make_async_copy(sources[k], held[k], in_sem.at[k]) for k in range(6)]
    stores = [pltpu.make_async_copy(held[k], targets[k], out_sem.at[k]) for k in range(6)]
    for load in loads:
        load.start()
    for load, store in zip(loads, stores):
        load.wait()
        store.start()
    for store in stores:
        store.wait()


def both_ways(shape, kind):
    return [pltpu.VMEM(shape, kind), pltpu.VMEM(shape, kind)]


def per_device(
    initial, targets, diffusivity, column_order, send_counts, w_first, w_inner, w_last, b_inner, b_last
):
    slabs = pltpu.VMEM((SLABS, LEV, SPAN), F32)
    made = pl.pallas_call(
        step_kernel,
        out_shape=(
            jax.ShapeDtypeStruct((LEV * CX * 2, LANES), F32),
            jax.ShapeDtypeStruct((LEV, WIDTH), F32),
            jax.ShapeDtypeStruct((3, WIDTH, WIDTH), F32),
            jax.ShapeDtypeStruct((LEV, WIDTH), F32),
            jax.ShapeDtypeStruct((4, WIDTH), F32),
            jax.ShapeDtypeStruct((1, LEV), F32),
        ),
        in_specs=[ANY] * 10,
        out_specs=(ANY,) * 6,
        scratch_shapes=[
            pltpu.VMEM((LEV * CX * 2, LANES), F32),
            pltpu.VMEM((LEV * CX * 2, LANES), F32),
            pltpu.VMEM((CX, CY), F32),
            pltpu.VMEM((1, NCOL), jnp.int32),
            pltpu.VMEM((1, TILES * SUBS), jnp.int32),
            pltpu.VMEM((LEV, WIDTH), BF16),
            pltpu.VMEM((3, WIDTH, WIDTH), BF16),
            pltpu.VMEM((LEV, WIDTH), BF16),
            pltpu.VMEM((4, WIDTH), F32),
            pltpu.VMEM((1, LEV), F32),
            pltpu.VMEM((LEV * CX * 2, LANES), F32),
            pltpu.VMEM((LEV, WIDTH), F32),
            pltpu.VMEM((3, WIDTH, WIDTH), F32),
            pltpu.VMEM((LEV, WIDTH), F32),
            pltpu.VMEM((4, WIDTH), F32),
            pltpu.VMEM((1, LEV), F32),
            pltpu.SemaphoreType.DMA((10,)),
            pltpu.SemaphoreType.DMA((6,)),
            slabs,
            slabs,
            pltpu.VMEM((24, SPAN), F32),
            pltpu.VMEM((NCOL, LANES), F32),
            pltpu.VMEM((2, NCOL // LANES, LANES), jnp.int32),
            pltpu.SMEM((2, NCOL // LANES, LANES), jnp.int32),
        ]
        + both_ways((2, 2 * LEV + 2 * CX, CY), BF16)
        + both_ways((2, LEV + 2 * CX, LANES), BF16)
        + both_ways((4, 8, LANES), F32)
        + both_ways((2, 2 * LEV, CY), BF16)
        + both_ways((2, LEV, LANES), BF16)
        + both_ways((4, 8, LANES), F32)
        + [
            pltpu.VMEM((WIDTH, LEV), BF16),
            pltpu.VMEM((3, WIDTH, WIDTH), BF16),
            pltpu.VMEM((WIDTH, LEV), BF16),
            pltpu.VMEM((5, WIDTH, 1), F32),
            pltpu.VMEM((2, LANES, LANES), F32),
        ]
        + both_ways((SUBS, SHARE, LANES), BF16)
        + both_ways((SUBS, SHARE // 2, LANES), BF16)
        + [
            pltpu.VMEM((NCOL, LANES), F32),
            pltpu.VMEM((4, LANES, LANES), F32),
            pltpu.VMEM((4, LANES, LANES), F32),
            pltpu.VMEM((LANES, LANES), F32),
            pltpu.VMEM((GRAD_ROWS, 256), F32),
            pltpu.VMEM((GRAD_ROWS, 256), BF16),
        ]
        + both_ways((TILES, CHUNK, 256), BF16)
        + [pltpu.SemaphoreType.DMA((2,))]
        + [pltpu.SemaphoreType.DMA((8,))] * 4
        + [pltpu.SemaphoreType.DMA((SUBS,))] * 4
        + [pltpu.SemaphoreType.DMA((TILES,))] * 4,
        compiler_params=pltpu.CompilerParams(
            collective_id=0, has_side_effects=True, vmem_limit_bytes=LIMIT
        ),
        name="step",
    )(
        tiled(initial),
        tiled(targets),
        diffusivity,
        column_order,
        send_counts,
        w_first[0],
        w_inner[0],
        w_last[0].T,
        b_inner[0],
        b_last,
    )
    result, step_first, step_inner, step_last_t, step_bias_inner, step_bias_last = pl.pallas_call(
        copy_kernel,
        out_shape=tuple(jax.ShapeDtypeStruct(one.shape, one.dtype) for one in made),
        in_specs=[ANY] * 6,
        out_specs=(ANY,) * 6,
        scratch_shapes=[pltpu.VMEM(one.shape, one.dtype) for one in made]
        + [pltpu.SemaphoreType.DMA((6,))] * 2,
        name="finish",
    )(*made)
    return (
        untiled(result),
        step_first[None],
        step_inner[None],
        step_last_t.T[None],
        step_bias_inner[None],
        step_bias_last,
    )


def solution(mesh):
    placed = (
        P(None, "tile", "sub"),
        P(None, "tile", "sub"),
        P("tile", "sub"),
        P(("tile", "sub"), None),
        P(("tile", "sub"), None),
        P("sub", None, None),
        P("sub", None, None, None),
        P("sub", None, None),
        P("sub", None, None),
        P("sub", None),
    )
    return jax.shard_map(
        per_device,
        mesh=mesh,
        in_specs=placed,
        out_specs=(
            P(None, "tile", "sub"),
            P("sub", None, None),
            P("sub", None, None, None),
            P("sub", None, None),
            P("sub", None, None),
            P("sub", None),
        ),
        check_vma=False,
    )
```

```python
import jax
import jax.numpy as jnp
from jax import lax
from jax.experimental import pallas as pl
from jax.experimental.pallas import tpu as pltpu
from jax.sharding import PartitionSpec as P

MESH = pl.DeviceIdType.MESH
F32 = jnp.float32
BF16 = jnp.bfloat16
LEV = 64
WIDTH = 192
CX = 16
CY = 256
NCOL = CX * CY
TILES = 8
SUBS = 16
SHARE = NCOL // SUBS
PARAMS = 136000
AUG = 16
LANES = 128
SPAN = CY + LANES
SLABS = CX + 4
CHUNK = 144
GRAD_ROWS = 768
UPPER = GRAD_ROWS // 2
PACKED_ROWS = CHUNK * TILES
LAST_BIAS = LEV + 2
GROUP = 4
FIRST_INNER = LEV + AUG
FIRST_LAST = FIRST_INNER + 3 * (WIDTH + AUG)
ANY = pl.BlockSpec(memory_space=pl.ANY)
LIMIT = 58 * 2**20


def wrapped(index, step, count):
    return lax.rem(index + step + count, count)


def remote(source, target, send_sem, recv_sem, peer):
    return pltpu.make_async_remote_copy(
        src_ref=source,
        dst_ref=target,
        send_sem=send_sem,
        recv_sem=recv_sem,
        device_id=peer,
        device_id_type=MESH,
    )


PAIRS = ((0, 0), (2, 0), (2, 1), (1, 0), (3, 0), (1, 1), (3, 1), (0, 1))


def crossing(j):
    late = jnp.minimum(j // 2, 1)
    return late * (1 - j % 2) + (1 - late) * (j % 2)


def partner(tile, sub, j, sign):
    turned = crossing(j)
    x = sum(jnp.where(j // 2 == k, pair[0], 0) for k, pair in enumerate(PAIRS))
    core = sum(jnp.where(j // 2 == k, pair[1], 0) for k, pair in enumerate(PAIRS))
    high = (sub // 8 + turned) % 2
    middle = (sub // 2 + sign * x + 4) % 4
    return (tile + 4 * turned) % TILES, high * 8 + middle * 2 + (sub + core) % 2


def place_of(sub, other):
    turned = (other // 8 + sub // 8) % 2
    x = (other // 2 - sub // 2 + 8) % 4
    core = (other + sub) % 2
    step = sum(
        jnp.where((x == pair[0]) & (core == pair[1]), k, 0) for k, pair in enumerate(PAIRS)
    )
    late = jnp.minimum(step, 1)
    return 2 * step + late * (1 - turned) + (1 - late) * turned


def tiled(block):
    return block.reshape(LEV, CX // 8, 8, 2, LANES).transpose(0, 1, 3, 2, 4).reshape(-1, LANES)


def untiled(rows):
    return rows.reshape(LEV, CX // 8, 2, 8, LANES).transpose(0, 1, 3, 2, 4).reshape(LEV, CX, CY)


def tiled_row(x, half):
    return (x // 8) * 16 + half * 8 + x % 8


def lanes(shape):
    return lax.broadcasted_iota(jnp.int32, shape, 1)


def sublanes(shape):
    return lax.broadcasted_iota(jnp.int32, shape, 0)


def dot(left, right, contract=(1, 0)):
    return lax.dot_general(
        left, right, (((contract[0],), (contract[1],)), ((), ())), preferred_element_type=F32
    )


def near_sum(value):
    return pltpu.roll(value, 1, 1) + pltpu.roll(value, SPAN - 1, 1)


def silu_and_slope(preact):
    sigmoid_value = 0.5 + 0.5 * jnp.tanh(0.5 * preact)
    active = preact * sigmoid_value
    return active.astype(BF16), sigmoid_value + active * (1.0 - sigmoid_value)


def find_routes(order, counts, sub, routes, tables, sems):
    count_row = counts[...]
    square = (TILES * SUBS, TILES * SUBS)
    earlier = lanes(square)

    def starts_and_shift(device):
        before = earlier < device
        same = earlier % SUBS == device % SUBS
        start = jnp.sum(jnp.where(before, count_row, 0), axis=1, keepdims=True)
        within = jnp.sum(jnp.where(before & same, count_row, 0), axis=1, keepdims=True)
        block = place_of(sub, device[:, 0:1] % SUBS)
        return start, block * SHARE + within - start

    device = sublanes(square)
    start, shift = starts_and_shift(device)
    _, shift_before = starts_and_shift(jnp.maximum(device - 1, 0))
    change = shift - jnp.where(device[:, 0:1] == 0, 0, shift_before)
    width = 512
    outward = jnp.zeros((32, 256), F32)
    homeward = jnp.zeros((32, 256), F32)

    def spread(where, what):
        high = (sublanes((32, width)) == where // LANES).astype(F32).astype(BF16)
        hit = sublanes((LANES, width)) == where % LANES
        values = jnp.concatenate(
            [jnp.where(hit, what // LANES, 0), jnp.where(hit, what % LANES, 0)], axis=0
        )
        return dot(high, values.astype(F32).astype(BF16), (1, 1))

    for first in range(0, NCOL, width):
        place = lanes((1, width)) + first
        slot = place + jnp.sum(jnp.where(start <= place, change, 0), axis=0, keepdims=True)
        column = order[:, first : first + width]
        outward = outward + spread(slot, column)
        homeward = homeward + spread(column, slot)
    for k, table in enumerate((outward, homeward)):
        whole = table.astype(jnp.int32)
        tables[k] = jnp.clip(whole[:, 0:LANES] * LANES + whole[:, LANES:], 0, NCOL - 1)
    for k in range(2):
        copy = pltpu.make_async_copy(tables.at[k], routes.at[k], sems.at[k])
        copy.start()
        copy.wait()


def step_kernel(
    initial_hbm, targets_hbm, diffusivity_hbm, order_hbm, counts_hbm,
    w_first_hbm, w_inner_hbm, w_last_hbm, b_inner_hbm, b_last_hbm,
    result_hbm, step_first_hbm, step_inner_hbm, step_last_hbm, step_bias_inner_hbm, step_bias_last_hbm,
    initial, targets, diffusivity, order, counts, w_first, w_inner, w_last_t, b_inner, b_last,
    result, step_first, step_inner, step_last_t, step_bias_inner, step_bias_last,
    load_sem, store_sem,
    field, middle, rates, columns, tables, routes,
    xs, xr, ys, yr, cs, cr, gxs, gxr, gys, gyr, gcs, gcr,
    wt_first, wt_inner, w_last, bias,
    stage, send, recv, answer, back, rows, grads_even, grads_odd, edges, total, wide, flat, parts, whole,
    table_sem, halo_sem, halo_in_sem, ghalo_sem, ghalo_in_sem,
    out_sem, in_sem, ret_sem, back_sem, part_sem, part_in_sem, whole_sem, whole_in_sem,
):
    tile, sub = lax.axis_index("tile"), lax.axis_index("sub")
    up, down = wrapped(tile, 1, TILES), wrapped(tile, -1, TILES)
    right, left = wrapped(sub, 1, SUBS), wrapped(sub, -1, SUBS)
    around = (
        (down, sub), (up, sub), (tile, left), (tile, right),
        (down, left), (down, right), (up, left), (up, right),
    )
    peers = (
        [partner(tile, sub, j, 1) for j in range(1, SUBS)]
        + [(wrapped(tile, j, TILES), sub) for j in range(1, TILES)]
        + list(around[2:])
    )
    loads = [
        pltpu.make_async_copy(source, target, load_sem.at[k])
        for k, (source, target) in enumerate(
            (
                (initial_hbm, initial), (diffusivity_hbm, diffusivity), (order_hbm, order),
                (counts_hbm, counts), (w_first_hbm, w_first), (w_inner_hbm, w_inner),
                (w_last_hbm, w_last_t), (b_inner_hbm, b_inner), (b_last_hbm, b_last),
                (targets_hbm, targets),
            )
        )
    ]
    for load in loads:
        load.start()
    barrier = pltpu.get_barrier_semaphore()
    for peer in peers:
        pl.semaphore_signal(barrier, inc=1, device_id=peer, device_id_type=MESH)
    stores = [
        pltpu.make_async_copy(source, target, store_sem.at[k])
        for k, (source, target) in enumerate(
            (
                (result, result_hbm), (step_first, step_first_hbm), (step_inner, step_inner_hbm),
                (step_last_t, step_last_hbm), (step_bias_inner, step_bias_inner_hbm),
                (step_bias_last, step_bias_last_hbm),
            )
        )
    ]

    def cells(ref, x):
        return jnp.concatenate(
            [ref[pl.ds(tiled_row(x, h), LEV, stride=2 * CX), :] for h in range(2)], axis=1
        )

    def halo(group, k, sends, receives, out_sems, in_sems):
        place = {"x": k, "y": 2 + k, "c": 4 + k}[group]
        other = (3 - k) if group == "c" else (1 - k)
        opposite = place - k + other
        return remote(
            sends.at[k], receives.at[other], out_sems.at[place], in_sems.at[opposite], around[place]
        )

    def strip(tile_of, side):
        pair = lanes((LEV, LANES)) // 2
        packed = jnp.zeros((LEV, LANES), F32)
        for x in range(CX):
            moved = tile_of(x, side)
            shift = (2 * x + 2 * side) % LANES
            if shift:
                moved = pltpu.roll(moved, shift, 1)
            packed = jnp.where(pair == x, moved, packed)
        return packed

    def edge_tile(x, side):
        return field[x + 2, :, side * LANES : (side + 1) * LANES]

    low = lanes((LEV, LANES)) < LEV

    def halo_tile(from_left, from_right, x):
        back_right = pltpu.roll(from_right, LANES - 2 * x, 1) if x else from_right
        return jnp.where(low, back_right, pltpu.roll(from_left, LANES - 2 - 2 * x, 1))

    def fill(x, carry):
        field[x + 2, :, 0:CY] = cells(initial, x)
        return carry

    loads[0].wait()
    loads[1].wait()
    for x in (0, 1, CX - 2, CX - 1):
        fill(x, 0)
    rate_high = diffusivity[...].astype(BF16)
    rate_parts = (rate_high, (diffusivity[...] - rate_high.astype(F32)).astype(BF16))
    same_lev = sublanes((LEV, LEV)) == lanes((LEV, LEV))
    for side in range(2):
        for k in range(2):
            edge = field[2 + (k if side == 0 else CX - 2 + k), :, 0:CY]
            xs[side, k * LEV : (k + 1) * LEV, :] = edge.astype(BF16)
        for k in range(2):
            xs[side, 2 * LEV + k * CX : 2 * LEV + (k + 1) * CX, :] = rate_parts[k]
    for corner in range(4):
        side, edge = corner // 2, corner % 2
        x = 0 if side == 0 else CX - 1
        y = edge * (CY - 1)
        cell = jnp.where(same_lev, field[x + 2, :, y : y + 1], 0.0)
        cs[corner, 0:1, 0:LEV] = jnp.sum(cell, axis=0, keepdims=True)
        cs[corner, 1:2, :] = diffusivity[x : x + 1, edge * LANES : (edge + 1) * LANES]
    pl.semaphore_wait(barrier, len(peers))
    copies = []
    for side in range(2):
        copies.append(halo("x", side, xs, xr, halo_sem, halo_in_sem))
        copies[-1].start()
    for corner in range(4):
        copies.append(halo("c", corner, cs, cr, halo_sem, halo_in_sem))
        copies[-1].start()
    lax.fori_loop(2, CX - 2, fill, 0)
    for side in range(2):
        ys[side, 0:LEV, :] = strip(edge_tile, side).astype(BF16)
        for k in range(2):
            part_rows = rate_parts[k][:, side * LANES : (side + 1) * LANES]
            ys[side, LEV + k * CX : LEV + (k + 1) * CX, :] = part_rows
        copies.append(halo("y", side, ys, yr, halo_sem, halo_in_sem))
        copies[-1].start()

    for load in loads[2:]:
        load.wait()
    find_routes(order, counts, sub, routes, tables, table_sem)
    for copy in copies:
        copy.wait_recv()
    def arrived_rates(message, first):
        high, rest = (message[first + k * CX : first + (k + 1) * CX, :].astype(F32) for k in range(2))
        return high + rest

    rates[0:2, 0:CY] = arrived_rates(xr.at[0], 2 * LEV)[CX - 2 :, :]
    rates[2 : CX + 2, 0:CY] = diffusivity[...]
    rates[CX + 2 : CX + 4, 0:CY] = arrived_rates(xr.at[1], 2 * LEV)[0:2, :]
    first_rows = lanes((CX, LANES)) < LEV
    rates[0:8, CY:] = jnp.zeros((8, LANES), F32)
    rates[16:24, CY:] = jnp.zeros((8, LANES), F32)
    rates[2 : CX + 2, CY:] = jnp.where(
        first_rows, arrived_rates(yr.at[1], LEV), arrived_rates(yr.at[0], LEV)
    )
    one_row = lanes((1, LANES)) < LEV
    rates[1:2, CY:] = jnp.where(one_row, cr[1, 1:2, :], cr[0, 1:2, :])
    rates[CX + 2 : CX + 3, CY:] = jnp.where(one_row, cr[3, 1:2, :], cr[2, 1:2, :])

    def spread_halo(x_in, y_in, c_in):
        for side in range(2):
            for k in range(2):
                slab = k if side == 0 else CX + 2 + k
                field[slab, :, 0:CY] = x_in[side, k * LEV : (k + 1) * LEV, :].astype(F32)
            outer = 0 if side == 0 else CX + 3
            field[outer, :, CY:] = jnp.zeros((LEV, LANES), F32)
            inner = 1 if side == 0 else CX + 2
            cell = [
                jnp.sum(jnp.where(same_lev, c_in[2 * side + k, 0:1, 0:LEV], 0.0), axis=1, keepdims=True)
                for k in range(2)
            ]
            field[inner, :, CY:] = jnp.where(low, cell[1], cell[0])
        from_left, from_right = y_in[0, 0:LEV, :].astype(F32), y_in[1, 0:LEV, :].astype(F32)
        for x in range(CX):
            field[x + 2, :, CY:] = halo_tile(from_left, from_right, x)

    spread_halo(xr, yr, cr)

    def diffused(ref, slab):
        now = ref[slab]
        near = ref[slab - 1] + ref[slab + 1] + near_sum(now)
        return now + rates[pl.ds(slab, 1), :] * (near - 4.0 * now)

    def forward_first(pair, carry):
        done = [diffused(field, 2 * pair + k) for k in (1, 2)]
        for k in (1, 2):
            middle[2 * pair + k] = done[k - 1]
        return carry

    lax.fori_loop(0, CX // 2 + 1, forward_first, 0)

    def forward_second(pair, carry):
        for x in (2 * pair, 2 * pair + 1):
            later = diffused(middle, x + 2)[:, 0:CY]
            both = jnp.concatenate([later, later - cells(targets, x)], axis=0)
            columns[pl.ds(pl.multiple_of(x * CY, CY), CY), :] = both.T
        return carry

    lax.fori_loop(0, CX // 2, forward_second, 0)

    def outgoing(j):
        return remote(send.at[j], recv.at[j], out_sem.at[j], in_sem.at[j], partner(tile, sub, j, 1))

    def returning(j):
        return remote(answer.at[j], back.at[j], ret_sem.at[j], back_sem.at[j], partner(tile, sub, j, -1))

    def gathered(table, line, source, target):
        for first in range(0, LANES, 16):
            taken = [source[pl.ds(routes[table, line, first + k], 1), :] for k in range(16)]
            for k in range(16):
                target[first + k : first + k + 1, :] = taken[k]

    def push(step, carry):
        j = lax.rem(step, SUBS)
        for half in range(2):
            gathered(0, 2 * j + half, columns, stage.at[half])
        send[j] = stage[...].reshape(SHARE, LANES).astype(BF16)

        @pl.when(j > 0)
        def _():
            outgoing(j).start()

        return carry

    lax.fori_loop(1, SUBS + 1, push, 0)
    recv[0] = send[0]

    same = sublanes((WIDTH, WIDTH)) == lanes((WIDTH, WIDTH))
    unit = same.astype(F32).astype(BF16)
    wt_first[...] = dot(unit, w_first[...], (1, 1)).astype(BF16)
    for k in range(3):
        wt_inner[k] = dot(unit, w_inner[k], (1, 1)).astype(BF16)
    w_last[...] = dot(unit, w_last_t[...], (1, 1)).astype(BF16)
    for k in range(4):
        bias[k] = jnp.sum(jnp.where(same, b_inner[k : k + 1, :], 0.0), axis=1, keepdims=True)
    bias[4, 0:LEV, :] = jnp.sum(jnp.where(same_lev, b_last[...], 0.0), axis=1, keepdims=True)
    total[...] = jnp.zeros_like(total)

    extra = (sublanes((AUG, SHARE)) == 0).astype(F32).astype(BF16)

    def with_ones(value):
        return jnp.concatenate([value, extra], axis=0)

    def some_blocks(turn, carry):
        @pl.when(turn > 0)
        def _():
            outgoing(GROUP * turn).wait_recv()

        for b in range(1, GROUP):
            outgoing(GROUP * turn + b).wait_recv()
        both = range(GROUP)
        turned = [recv[GROUP * turn + b].astype(F32).T for b in both]
        inputs = [turned[b][:LEV].astype(BF16) for b in both]
        current = inputs
        feeds, slopes = [inputs], []
        for k in range(4):
            weight = wt_first[...] if k == 0 else wt_inner[k - 1]
            outs = [silu_and_slope(dot(weight, current[b]) + bias[k]) for b in both]
            current = [outs[b][0] for b in both]
            feeds.append(current)
            slopes.append([outs[b][1] for b in both])
        residue = [
            turned[b][LEV:] + dot(w_last_t[...], current[b]) + bias[4, 0:LEV, :] for b in both
        ]
        error = [residue[b].astype(BF16) for b in both]
        total[FIRST_LAST:, 0 : WIDTH + AUG] += sum(
            dot(error[b], with_ones(current[b]), (1, 1)) for b in both
        )
        carried = [dot(w_last[...], error[b]) for b in both]
        for k in (3, 2, 1, 0):
            error = [(carried[b] * slopes[k][b]).astype(BF16) for b in both]
            row = FIRST_INNER + (k - 1) * (WIDTH + AUG) if k else 0
            high = (WIDTH if k else LEV) + AUG
            total[row : row + high, 0:WIDTH] += sum(
                dot(with_ones(feeds[k][b]), error[b], (1, 1)) for b in both
            )
            weight = w_inner[k - 1] if k else w_first[...]
            carried = [dot(weight, error[b]) for b in both]
        half = SHARE // 2
        for b in both:
            outcome = residue[b] + carried[b]
            packed = jnp.concatenate([outcome[:, :half], outcome[:, half:]], axis=0)
            answer[GROUP * turn + b] = packed.T.astype(BF16)

        @pl.when(turn > 0)
        def _():
            returning(GROUP * turn).start()

        for b in range(1, GROUP):
            returning(GROUP * turn + b).start()
        return carry

    lax.fori_loop(0, SUBS // GROUP, some_blocks, 0)

    last_bias = jnp.where(same_lev, total[FIRST_LAST:, WIDTH : WIDTH + 1], 0.0)
    total[LAST_BIAS : LAST_BIAS + 1, 0:LEV] = jnp.sum(last_bias, axis=0, keepdims=True)
    upper_low = lanes((UPPER, LANES)) < LEV
    wide[0:GRAD_ROWS, :] = total[:, 0:LANES].astype(BF16)
    wide[GRAD_ROWS:, :] = jnp.where(
        upper_low, total[0:UPPER, LANES:], pltpu.roll(total[UPPER:, LANES:], LEV, 1)
    ).astype(BF16)

    def part(j):
        owner = wrapped(tile, j, TILES)
        first = pl.multiple_of(owner * CHUNK, CHUNK)
        return remote(
            wide.at[pl.ds(first, CHUNK)], parts.at[j], part_sem.at[j], part_in_sem.at[j], (owner, sub)
        )

    def share_of(j):
        return remote(
            whole.at[0], whole.at[j], whole_sem.at[j], whole_in_sem.at[j], (wrapped(tile, j, TILES), sub)
        )

    for j in range(1, TILES):
        part(j).start()

    def unpack(j, source):
        block = source.astype(F32)
        first = pl.multiple_of(j * SHARE, SHARE)
        rows[pl.ds(first, SHARE // 2), :] = block
        rows[pl.ds(first + SHARE // 2, SHARE // 2), :] = pltpu.roll(block, LEV, 1)

    unpack(0, answer[0])

    def take(j, carry):
        returning(j).wait_recv()
        unpack(j, back[j])
        return carry

    lax.fori_loop(1, SUBS, take, 0)

    left_half = lanes((CY, LANES)) < LEV
    grads = (grads_even, grads_odd)

    def home(first_slabs):
        for held, x in zip(grads, first_slabs):
            for line in range(4):
                gathered(1, x * 2 + line, rows, held.at[line])
        for held, x in zip(grads, first_slabs):
            slab = [held[2 * k : 2 * k + 2].reshape(CY, LANES) for k in range(2)]
            turned = jnp.where(left_half, slab[0], pltpu.roll(slab[1], LEV, 1)).T
            for k in range(2):
                field[x + k + 2, :, 0:CY] = turned[k * LEV : (k + 1) * LEV]

    ghalos = []

    def home_row(line, k):
        return rows[pl.ds(routes[1, line, k], 1), :]

    for corner in range(4):
        line = (0 if corner < 2 else 2 * CX - 2) + corner % 2
        gcs[corner, 0:1, :] = home_row(line, (LANES - 1) * (corner % 2))
        ghalos.append(halo("c", corner, gcs, gcr, ghalo_sem, ghalo_in_sem))
        ghalos[-1].start()
    edges[2 * 2 * CX :, :] = jnp.zeros((LANES - 4 * CX, LANES), F32)
    for side in range(2):
        taken = [
            home_row(2 * x + side, (LANES - 2) * side + k) for x in range(CX) for k in range(2)
        ]
        for k in range(2 * CX):
            edges[2 * CX * side + k : 2 * CX * side + k + 1, :] = taken[k]
    turned_edges = edges[...].T[0:LEV, :]
    for side in range(2):
        moved = pltpu.roll(turned_edges, LANES - 2 * CX, 1) if side else turned_edges
        gys[side] = moved.astype(BF16)
        ghalos.append(halo("y", side, gys, gyr, ghalo_sem, ghalo_in_sem))
        ghalos[-1].start()

    home((0, CX - 2))
    for side in range(2):
        x = 0 if side == 0 else CX - 2
        for k in range(2):
            gxs[side, k * LEV : (k + 1) * LEV, :] = field[x + k + 2, :, 0:CY].astype(BF16)
        ghalos.append(halo("x", side, gxs, gxr, ghalo_sem, ghalo_in_sem))
        ghalos[-1].start()

    mine = pl.multiple_of(tile * CHUNK, CHUNK)
    summed = wide[pl.ds(mine, CHUNK), :].astype(F32)
    for j in range(1, TILES):
        part(j).wait_recv()
        summed = summed + parts[j].astype(F32)
    whole[0] = summed.astype(BF16)
    for j in range(1, TILES):
        share_of(j).start()

    def home_pairs(turn, carry):
        home((4 * turn + 2, 4 * turn + 4))
        return carry

    lax.fori_loop(0, CX // 4 - 1, home_pairs, 0)
    for copy in ghalos:
        copy.wait_recv()
    spread_halo(gxr, gyr, gcr)

    def adjoint(ref, slab):
        rate = [rates[pl.ds(slab + k, 1), :] for k in (-1, 0, 1)]
        now = ref[slab]
        flow = rate[1] * now
        near = rate[0] * ref[slab - 1] + rate[2] * ref[slab + 1] + near_sum(flow)
        return now + (near - 4.0 * flow)

    def adjoint_first(pair, carry):
        done = [adjoint(field, 2 * pair + k) for k in (1, 2)]
        for k in (1, 2):
            middle[2 * pair + k] = done[k - 1]
        return carry

    lax.fori_loop(0, CX // 2 + 1, adjoint_first, 0)

    for j in range(1, TILES):
        share_of(j).wait_recv()
    for j in range(TILES):
        owner = wrapped(tile, -j, TILES)
        flat[pl.ds(pl.multiple_of(owner * CHUNK, CHUNK), CHUNK), :] = whole[j].astype(F32)
    everything = flat[...]
    total[:, 0:LANES] = flat[0:GRAD_ROWS, :]
    total[0:UPPER, LANES:] = flat[GRAD_ROWS:, :]
    total[UPPER:, LANES:] = pltpu.roll(flat[GRAD_ROWS:, :], LEV, 1)
    squares = jnp.sum(jnp.sum(everything * everything, axis=0, keepdims=True), axis=1, keepdims=True)
    factor = lax.rsqrt(squares / PARAMS + 1e-06)
    step_first[...] = total[0:LEV, 0:WIDTH] * factor
    step_bias_inner[0:1, :] = total[LEV : LEV + 1, 0:WIDTH] * factor
    for k in range(3):
        row = FIRST_INNER + k * (WIDTH + AUG)
        step_inner[k] = total[row : row + WIDTH, 0:WIDTH] * factor
        step_bias_inner[k + 1 : k + 2, :] = total[row + WIDTH : row + WIDTH + 1, 0:WIDTH] * factor
    step_last_t[...] = total[FIRST_LAST:, 0:WIDTH] * factor
    step_bias_last[...] = total[LAST_BIAS : LAST_BIAS + 1, 0:LEV] * factor
    for store in stores[1:]:
        store.start()

    def adjoint_second(pair, carry):
        done = [adjoint(middle, 2 * pair + k + 2) for k in range(2)]
        for k in range(2):
            for h in range(2):
                row = tiled_row(2 * pair + k, h)
                result[pl.ds(row, LEV, stride=2 * CX), :] = done[k][:, h * LANES : (h + 1) * LANES]
        return carry

    lax.fori_loop(0, CX // 2, adjoint_second, 0)

    stores[0].start()

    def settle(j, carry):
        outgoing(j).wait_send()
        returning(j).wait_send()
        return carry

    lax.fori_loop(1, SUBS, settle, 0)
    for j in range(1, TILES):
        part(j).wait_send()
        share_of(j).wait_send()
    for copy in copies + ghalos:
        copy.wait_send()
    for store in stores:
        store.wait()


def copy_kernel(*refs):
    sources, targets, held = refs[0:6], refs[6:12], refs[12:18]
    in_sem, out_sem = refs[18:]
    piece = LEV * CX * 2 // 4
    places = [(0, pl.ds(k * piece, piece)) for k in range(4)] + [(k, slice(None)) for k in range(1, 6)]
    loads, stores = [], []
    for k, (which, rows) in enumerate(places):
        source, middle, target = (group[which].at[rows] for group in (sources, held, targets))
        loads.append(pltpu.make_async_copy(source, middle, in_sem.at[k]))
        stores.append(pltpu.make_async_copy(middle, target, out_sem.at[k]))
    for load in loads:
        load.start()
    for load, store in zip(loads, stores):
        load.wait()
        store.start()
    for store in stores:
        store.wait()


def both_ways(shape, kind):
    return [pltpu.VMEM(shape, kind), pltpu.VMEM(shape, kind)]


def per_device(
    initial, targets, diffusivity, column_order, send_counts, w_first, w_inner, w_last, b_inner, b_last
):
    slabs = pltpu.VMEM((SLABS, LEV, SPAN), F32)
    made = pl.pallas_call(
        step_kernel,
        out_shape=(
            jax.ShapeDtypeStruct((LEV * CX * 2, LANES), F32),
            jax.ShapeDtypeStruct((LEV, WIDTH), F32),
            jax.ShapeDtypeStruct((3, WIDTH, WIDTH), F32),
            jax.ShapeDtypeStruct((LEV, WIDTH), F32),
            jax.ShapeDtypeStruct((4, WIDTH), F32),
            jax.ShapeDtypeStruct((1, LEV), F32),
        ),
        in_specs=[ANY] * 10,
        out_specs=(ANY,) * 6,
        scratch_shapes=[
            pltpu.VMEM((LEV * CX * 2, LANES), F32),
            pltpu.VMEM((LEV * CX * 2, LANES), F32),
            pltpu.VMEM((CX, CY), F32),
            pltpu.VMEM((1, NCOL), jnp.int32),
            pltpu.VMEM((1, TILES * SUBS), jnp.int32),
            pltpu.VMEM((LEV, WIDTH), BF16),
            pltpu.VMEM((3, WIDTH, WIDTH), BF16),
            pltpu.VMEM((LEV, WIDTH), BF16),
            pltpu.VMEM((4, WIDTH), F32),
            pltpu.VMEM((1, LEV), F32),
            pltpu.VMEM((LEV * CX * 2, LANES), F32),
            pltpu.VMEM((LEV, WIDTH), F32),
            pltpu.VMEM((3, WIDTH, WIDTH), F32),
            pltpu.VMEM((LEV, WIDTH), F32),
            pltpu.VMEM((4, WIDTH), F32),
            pltpu.VMEM((1, LEV), F32),
            pltpu.SemaphoreType.DMA((10,)),
            pltpu.SemaphoreType.DMA((6,)),
            slabs,
            slabs,
            pltpu.VMEM((24, SPAN), F32),
            pltpu.VMEM((NCOL, LANES), F32),
            pltpu.VMEM((2, NCOL // LANES, LANES), jnp.int32),
            pltpu.SMEM((2, NCOL // LANES, LANES), jnp.int32),
        ]
        + both_ways((2, 2 * LEV + 2 * CX, CY), BF16)
        + both_ways((2, LEV + 2 * CX, LANES), BF16)
        + both_ways((4, 8, LANES), F32)
        + both_ways((2, 2 * LEV, CY), BF16)
        + both_ways((2, LEV, LANES), BF16)
        + both_ways((4, 8, LANES), F32)
        + [
            pltpu.VMEM((WIDTH, LEV), BF16),
            pltpu.VMEM((3, WIDTH, WIDTH), BF16),
            pltpu.VMEM((WIDTH, LEV), BF16),
            pltpu.VMEM((5, WIDTH, 1), F32),
            pltpu.VMEM((2, LANES, LANES), F32),
        ]
        + both_ways((SUBS, SHARE, LANES), BF16)
        + both_ways((SUBS, SHARE // 2, LANES), BF16)
        + [
            pltpu.VMEM((NCOL, LANES), F32),
            pltpu.VMEM((4, LANES, LANES), F32),
            pltpu.VMEM((4, LANES, LANES), F32),
            pltpu.VMEM((LANES, LANES), F32),
            pltpu.VMEM((GRAD_ROWS, 256), F32),
            pltpu.VMEM((PACKED_ROWS, LANES), BF16),
            pltpu.VMEM((PACKED_ROWS, LANES), F32),
        ]
        + both_ways((TILES, CHUNK, LANES), BF16)
        + [pltpu.SemaphoreType.DMA((2,))]
        + [pltpu.SemaphoreType.DMA((8,))] * 4
        + [pltpu.SemaphoreType.DMA((SUBS,))] * 4
        + [pltpu.SemaphoreType.DMA((TILES,))] * 4,
        compiler_params=pltpu.CompilerParams(
            collective_id=0, has_side_effects=True, vmem_limit_bytes=LIMIT
        ),
        name="step",
    )(
        tiled(initial),
        tiled(targets),
        diffusivity,
        column_order,
        send_counts,
        w_first[0],
        w_inner[0],
        w_last[0].T,
        b_inner[0],
        b_last,
    )
    result, step_first, step_inner, step_last_t, step_bias_inner, step_bias_last = pl.pallas_call(
        copy_kernel,
        out_shape=tuple(jax.ShapeDtypeStruct(one.shape, one.dtype) for one in made),
        in_specs=[ANY] * 6,
        out_specs=(ANY,) * 6,
        scratch_shapes=[pltpu.VMEM(one.shape, one.dtype) for one in made]
        + [pltpu.SemaphoreType.DMA((9,))] * 2,
        name="finish",
    )(*made)
    return (
        untiled(result),
        step_first[None],
        step_inner[None],
        step_last_t.T[None],
        step_bias_inner[None],
        step_bias_last,
    )


def solution(mesh):
    placed = (
        P(None, "tile", "sub"),
        P(None, "tile", "sub"),
        P("tile", "sub"),
        P(("tile", "sub"), None),
        P(("tile", "sub"), None),
        P("sub", None, None),
        P("sub", None, None, None),
        P("sub", None, None),
        P("sub", None, None),
        P("sub", None),
    )
    return jax.shard_map(
        per_device,
        mesh=mesh,
        in_specs=placed,
        out_specs=(
            P(None, "tile", "sub"),
            P("sub", None, None),
            P("sub", None, None, None),
            P("sub", None, None),
            P("sub", None, None),
            P("sub", None),
        ),
        check_vma=False,
    )
```

```python
import jax
import jax.numpy as jnp
from jax import lax
from jax.experimental import pallas as pl
from jax.experimental.pallas import tpu as pltpu
from jax.sharding import PartitionSpec as P

MESH = pl.DeviceIdType.MESH
F32 = jnp.float32
BF16 = jnp.bfloat16
LEV = 64
WIDTH = 192
CX = 16
CY = 256
NCOL = CX * CY
TILES = 8
SUBS = 16
SHARE = NCOL // SUBS
PARAMS = 136000
AUG = 16
LANES = 128
SPAN = CY + LANES
SLABS = CX + 4
CHUNK = 144
GRAD_ROWS = 768
UPPER = GRAD_ROWS // 2
PACKED_ROWS = CHUNK * TILES
LAST_BIAS = LEV + 2
GROUP = 4
FIRST_INNER = LEV + AUG
FIRST_LAST = FIRST_INNER + 3 * (WIDTH + AUG)
ANY = pl.BlockSpec(memory_space=pl.ANY)
LIMIT = 58 * 2**20


def wrapped(index, step, count):
    return lax.rem(index + step + count, count)


def remote(source, target, send_sem, recv_sem, peer):
    return pltpu.make_async_remote_copy(
        src_ref=source,
        dst_ref=target,
        send_sem=send_sem,
        recv_sem=recv_sem,
        device_id=peer,
        device_id_type=MESH,
    )


PAIRS = ((0, 0), (2, 0), (2, 1), (1, 0), (3, 0), (1, 1), (3, 1), (0, 1))


def crossing(j):
    late = jnp.minimum(j // 2, 1)
    return late * (1 - j % 2) + (1 - late) * (j % 2)


def partner(tile, sub, j, sign):
    turned = crossing(j)
    x = sum(jnp.where(j // 2 == k, pair[0], 0) for k, pair in enumerate(PAIRS))
    core = sum(jnp.where(j // 2 == k, pair[1], 0) for k, pair in enumerate(PAIRS))
    high = (sub // 8 + turned) % 2
    middle = (sub // 2 + sign * x + 4) % 4
    return (tile + 4 * turned) % TILES, high * 8 + middle * 2 + (sub + core) % 2


def place_of(sub, other):
    turned = (other // 8 + sub // 8) % 2
    x = (other // 2 - sub // 2 + 8) % 4
    core = (other + sub) % 2
    step = sum(
        jnp.where((x == pair[0]) & (core == pair[1]), k, 0) for k, pair in enumerate(PAIRS)
    )
    late = jnp.minimum(step, 1)
    return 2 * step + late * (1 - turned) + (1 - late) * turned


def tiled(block):
    return block.reshape(LEV, CX // 8, 8, 2, LANES).transpose(0, 1, 3, 2, 4).reshape(-1, LANES)


def untiled(rows):
    return rows.reshape(LEV, CX // 8, 2, 8, LANES).transpose(0, 1, 3, 2, 4).reshape(LEV, CX, CY)


def tiled_row(x, half):
    return (x // 8) * 16 + half * 8 + x % 8


def lanes(shape):
    return lax.broadcasted_iota(jnp.int32, shape, 1)


def sublanes(shape):
    return lax.broadcasted_iota(jnp.int32, shape, 0)


def dot(left, right, contract=(1, 0)):
    return lax.dot_general(
        left, right, (((contract[0],), (contract[1],)), ((), ())), preferred_element_type=F32
    )


def near_sum(value):
    return pltpu.roll(value, 1, 1) + pltpu.roll(value, SPAN - 1, 1)


def silu_and_slope(preact):
    sigmoid_value = 0.5 + 0.5 * jnp.tanh(0.5 * preact)
    active = preact * sigmoid_value
    return active.astype(BF16), sigmoid_value + active * (1.0 - sigmoid_value)


def find_routes(order, counts, sub, routes, tables, sems):
    count_row = counts[...]
    square = (TILES * SUBS, TILES * SUBS)
    earlier = lanes(square)

    def starts_and_shift(device):
        before = earlier < device
        same = earlier % SUBS == device % SUBS
        start = jnp.sum(jnp.where(before, count_row, 0), axis=1, keepdims=True)
        within = jnp.sum(jnp.where(before & same, count_row, 0), axis=1, keepdims=True)
        block = place_of(sub, device[:, 0:1] % SUBS)
        return start, block * SHARE + within - start

    device = sublanes(square)
    start, shift = starts_and_shift(device)
    _, shift_before = starts_and_shift(jnp.maximum(device - 1, 0))
    change = shift - jnp.where(device[:, 0:1] == 0, 0, shift_before)
    width = 512
    outward = jnp.zeros((32, 256), F32)
    homeward = jnp.zeros((32, 256), F32)

    def spread(where, what):
        high = (sublanes((32, width)) == where // LANES).astype(F32).astype(BF16)
        hit = sublanes((LANES, width)) == where % LANES
        values = jnp.concatenate(
            [jnp.where(hit, what // LANES, 0), jnp.where(hit, what % LANES, 0)], axis=0
        )
        return dot(high, values.astype(F32).astype(BF16), (1, 1))

    for first in range(0, NCOL, width):
        place = lanes((1, width)) + first
        slot = place + jnp.sum(jnp.where(start <= place, change, 0), axis=0, keepdims=True)
        column = order[:, first : first + width]
        outward = outward + spread(slot, column)
        homeward = homeward + spread(column, slot)
    for k, table in enumerate((outward, homeward)):
        whole = table.astype(jnp.int32)
        tables[k] = jnp.clip(whole[:, 0:LANES] * LANES + whole[:, LANES:], 0, NCOL - 1)
    for k in range(2):
        copy = pltpu.make_async_copy(tables.at[k], routes.at[k], sems.at[k])
        copy.start()
        copy.wait()


def step_kernel(
    initial_hbm, targets_hbm, diffusivity_hbm, order_hbm, counts_hbm,
    w_first_hbm, w_inner_hbm, w_last_hbm, b_inner_hbm, b_last_hbm,
    result_hbm, step_first_hbm, step_inner_hbm, step_last_hbm, step_bias_inner_hbm, step_bias_last_hbm,
    initial, targets, diffusivity, order, counts, w_first, w_inner, w_last_t, b_inner, b_last,
    result, step_first, step_inner, step_last_t, step_bias_inner, step_bias_last,
    load_sem, store_sem,
    field, middle, rates, columns, tables, routes,
    xs, xr, ys, yr, cs, cr, gxs, gxr, gys, gyr, gcs, gcr,
    wt_first, wt_inner, w_last, bias,
    stage, send, recv, answer, back, rows, grads_even, grads_odd, edges, total, wide, flat, parts, whole,
    table_sem, halo_sem, halo_in_sem, ghalo_sem, ghalo_in_sem,
    out_sem, in_sem, ret_sem, back_sem, part_sem, part_in_sem, whole_sem, whole_in_sem,
):
    tile, sub = lax.axis_index("tile"), lax.axis_index("sub")
    up, down = wrapped(tile, 1, TILES), wrapped(tile, -1, TILES)
    right, left = wrapped(sub, 1, SUBS), wrapped(sub, -1, SUBS)
    around = (
        (down, sub), (up, sub), (tile, left), (tile, right),
        (down, left), (down, right), (up, left), (up, right),
    )
    peers = (
        [partner(tile, sub, j, 1) for j in range(1, SUBS)]
        + [(wrapped(tile, j, TILES), sub) for j in range(1, TILES)]
        + list(around[2:])
    )
    loads = [
        pltpu.make_async_copy(source, target, load_sem.at[k])
        for k, (source, target) in enumerate(
            (
                (initial_hbm, initial), (diffusivity_hbm, diffusivity), (order_hbm, order),
                (counts_hbm, counts), (w_first_hbm, w_first), (w_inner_hbm, w_inner),
                (w_last_hbm, w_last_t), (b_inner_hbm, b_inner), (b_last_hbm, b_last),
                (targets_hbm, targets),
            )
        )
    ]
    for load in loads:
        load.start()
    barrier = pltpu.get_barrier_semaphore()
    for peer in peers:
        pl.semaphore_signal(barrier, inc=1, device_id=peer, device_id_type=MESH)
    stores = [
        pltpu.make_async_copy(source, target, store_sem.at[k])
        for k, (source, target) in enumerate(
            (
                (result, result_hbm), (step_first, step_first_hbm), (step_inner, step_inner_hbm),
                (step_last_t, step_last_hbm), (step_bias_inner, step_bias_inner_hbm),
                (step_bias_last, step_bias_last_hbm),
            )
        )
    ]

    def cells(ref, x):
        return jnp.concatenate(
            [ref[pl.ds(tiled_row(x, h), LEV, stride=2 * CX), :] for h in range(2)], axis=1
        )

    def halo(group, k, sends, receives, out_sems, in_sems):
        place = {"x": k, "y": 2 + k, "c": 4 + k}[group]
        other = (3 - k) if group == "c" else (1 - k)
        opposite = place - k + other
        return remote(
            sends.at[k], receives.at[other], out_sems.at[place], in_sems.at[opposite], around[place]
        )

    def strip(tile_of, side):
        pair = lanes((LEV, LANES)) // 2
        packed = jnp.zeros((LEV, LANES), F32)
        for x in range(CX):
            moved = tile_of(x, side)
            shift = (2 * x + 2 * side) % LANES
            if shift:
                moved = pltpu.roll(moved, shift, 1)
            packed = jnp.where(pair == x, moved, packed)
        return packed

    def edge_tile(x, side):
        return field[x + 2, :, side * LANES : (side + 1) * LANES]

    low = lanes((LEV, LANES)) < LEV

    def halo_tile(from_left, from_right, x):
        back_right = pltpu.roll(from_right, LANES - 2 * x, 1) if x else from_right
        return jnp.where(low, back_right, pltpu.roll(from_left, LANES - 2 - 2 * x, 1))

    def fill(x, carry):
        field[x + 2, :, 0:CY] = cells(initial, x)
        return carry

    loads[0].wait()
    loads[1].wait()
    for x in (0, 1, CX - 2, CX - 1):
        fill(x, 0)
    rate_high = diffusivity[...].astype(BF16)
    rate_parts = (rate_high, (diffusivity[...] - rate_high.astype(F32)).astype(BF16))
    same_lev = sublanes((LEV, LEV)) == lanes((LEV, LEV))
    for side in range(2):
        for k in range(2):
            edge = field[2 + (k if side == 0 else CX - 2 + k), :, 0:CY]
            xs[side, k * LEV : (k + 1) * LEV, :] = edge.astype(BF16)
        for k in range(2):
            xs[side, 2 * LEV + k * CX : 2 * LEV + (k + 1) * CX, :] = rate_parts[k]
    for corner in range(4):
        side, edge = corner // 2, corner % 2
        x = 0 if side == 0 else CX - 1
        y = edge * (CY - 1)
        cell = jnp.where(same_lev, field[x + 2, :, y : y + 1], 0.0)
        cs[corner, 0:1, 0:LEV] = jnp.sum(cell, axis=0, keepdims=True)
        cs[corner, 1:2, :] = diffusivity[x : x + 1, edge * LANES : (edge + 1) * LANES]
    pl.semaphore_wait(barrier, len(peers))
    copies = []
    for side in range(2):
        copies.append(halo("x", side, xs, xr, halo_sem, halo_in_sem))
        copies[-1].start()
    for corner in range(4):
        copies.append(halo("c", corner, cs, cr, halo_sem, halo_in_sem))
        copies[-1].start()
    lax.fori_loop(2, CX - 2, fill, 0)
    for side in range(2):
        ys[side, 0:LEV, :] = strip(edge_tile, side).astype(BF16)
        for k in range(2):
            part_rows = rate_parts[k][:, side * LANES : (side + 1) * LANES]
            ys[side, LEV + k * CX : LEV + (k + 1) * CX, :] = part_rows
        copies.append(halo("y", side, ys, yr, halo_sem, halo_in_sem))
        copies[-1].start()

    for load in loads[2:]:
        load.wait()
    find_routes(order, counts, sub, routes, tables, table_sem)
    for copy in copies:
        copy.wait_recv()
    def arrived_rates(message, first):
        high, rest = (message[first + k * CX : first + (k + 1) * CX, :].astype(F32) for k in range(2))
        return high + rest

    rates[0:2, 0:CY] = arrived_rates(xr.at[0], 2 * LEV)[CX - 2 :, :]
    rates[2 : CX + 2, 0:CY] = diffusivity[...]
    rates[CX + 2 : CX + 4, 0:CY] = arrived_rates(xr.at[1], 2 * LEV)[0:2, :]
    first_rows = lanes((CX, LANES)) < LEV
    rates[0:8, CY:] = jnp.zeros((8, LANES), F32)
    rates[16:24, CY:] = jnp.zeros((8, LANES), F32)
    rates[2 : CX + 2, CY:] = jnp.where(
        first_rows, arrived_rates(yr.at[1], LEV), arrived_rates(yr.at[0], LEV)
    )
    one_row = lanes((1, LANES)) < LEV
    rates[1:2, CY:] = jnp.where(one_row, cr[1, 1:2, :], cr[0, 1:2, :])
    rates[CX + 2 : CX + 3, CY:] = jnp.where(one_row, cr[3, 1:2, :], cr[2, 1:2, :])

    def spread_halo(x_in, y_in, c_in):
        for side in range(2):
            for k in range(2):
                slab = k if side == 0 else CX + 2 + k
                field[slab, :, 0:CY] = x_in[side, k * LEV : (k + 1) * LEV, :].astype(F32)
            outer = 0 if side == 0 else CX + 3
            field[outer, :, CY:] = jnp.zeros((LEV, LANES), F32)
            inner = 1 if side == 0 else CX + 2
            cell = [
                jnp.sum(jnp.where(same_lev, c_in[2 * side + k, 0:1, 0:LEV], 0.0), axis=1, keepdims=True)
                for k in range(2)
            ]
            field[inner, :, CY:] = jnp.where(low, cell[1], cell[0])
        from_left, from_right = y_in[0, 0:LEV, :].astype(F32), y_in[1, 0:LEV, :].astype(F32)
        for x in range(CX):
            field[x + 2, :, CY:] = halo_tile(from_left, from_right, x)

    spread_halo(xr, yr, cr)

    def diffused(ref, slab):
        now = ref[slab]
        near = ref[slab - 1] + ref[slab + 1] + near_sum(now)
        return now + rates[pl.ds(slab, 1), :] * (near - 4.0 * now)

    def forward_first(pair, carry):
        done = [diffused(field, 2 * pair + k) for k in (1, 2)]
        for k in (1, 2):
            middle[2 * pair + k] = done[k - 1]
        return carry

    lax.fori_loop(0, CX // 2 + 1, forward_first, 0)

    def forward_second(pair, carry):
        for x in (2 * pair, 2 * pair + 1):
            later = diffused(middle, x + 2)[:, 0:CY]
            both = jnp.concatenate([later, later - cells(targets, x)], axis=0)
            columns[pl.ds(pl.multiple_of(x * CY, CY), CY), :] = both.T
        return carry

    lax.fori_loop(0, CX // 2, forward_second, 0)

    def outgoing(j):
        return remote(send.at[j], recv.at[j], out_sem.at[j], in_sem.at[j], partner(tile, sub, j, 1))

    def returning(j):
        return remote(answer.at[j], back.at[j], ret_sem.at[j], back_sem.at[j], partner(tile, sub, j, -1))

    def gathered(table, line, source, target):
        for first in range(0, LANES, 16):
            taken = [source[pl.ds(routes[table, line, first + k], 1), :] for k in range(16)]
            for k in range(16):
                target[first + k : first + k + 1, :] = taken[k]

    def push(step, carry):
        j = lax.rem(step, SUBS)
        for half in range(2):
            gathered(0, 2 * j + half, columns, stage.at[half])
        send[j] = stage[...].reshape(SHARE, LANES).astype(BF16)

        @pl.when(j > 0)
        def _():
            outgoing(j).start()

        return carry

    lax.fori_loop(1, SUBS + 1, push, 0)
    recv[0] = send[0]

    same = sublanes((WIDTH, WIDTH)) == lanes((WIDTH, WIDTH))
    unit = same.astype(F32).astype(BF16)
    wt_first[...] = dot(unit, w_first[...], (1, 1)).astype(BF16)
    for k in range(3):
        wt_inner[k] = dot(unit, w_inner[k], (1, 1)).astype(BF16)
    w_last[...] = dot(unit, w_last_t[...], (1, 1)).astype(BF16)
    for k in range(4):
        bias[k] = jnp.sum(jnp.where(same, b_inner[k : k + 1, :], 0.0), axis=1, keepdims=True)
    bias[4, 0:LEV, :] = jnp.sum(jnp.where(same_lev, b_last[...], 0.0), axis=1, keepdims=True)
    total[...] = jnp.zeros_like(total)

    extra = (sublanes((AUG, SHARE)) == 0).astype(F32).astype(BF16)

    def with_ones(value):
        return jnp.concatenate([value, extra], axis=0)

    def some_blocks(turn, carry):
        @pl.when(turn > 0)
        def _():
            outgoing(GROUP * turn).wait_recv()

        for b in range(1, GROUP):
            outgoing(GROUP * turn + b).wait_recv()
        both = range(GROUP)
        turned = [recv[GROUP * turn + b].astype(F32).T for b in both]
        inputs = [turned[b][:LEV].astype(BF16) for b in both]
        current = inputs
        feeds, slopes = [inputs], []
        for k in range(4):
            weight = wt_first[...] if k == 0 else wt_inner[k - 1]
            outs = [silu_and_slope(dot(weight, current[b]) + bias[k]) for b in both]
            current = [outs[b][0] for b in both]
            feeds.append(current)
            slopes.append([outs[b][1] for b in both])
        residue = [
            turned[b][LEV:] + dot(w_last_t[...], current[b]) + bias[4, 0:LEV, :] for b in both
        ]
        error = [residue[b].astype(BF16) for b in both]
        total[FIRST_LAST:, 0 : WIDTH + AUG] += sum(
            dot(error[b], with_ones(current[b]), (1, 1)) for b in both
        )
        carried = [dot(w_last[...], error[b]) for b in both]
        for k in (3, 2, 1, 0):
            error = [(carried[b] * slopes[k][b]).astype(BF16) for b in both]
            row = FIRST_INNER + (k - 1) * (WIDTH + AUG) if k else 0
            high = (WIDTH if k else LEV) + AUG
            total[row : row + high, 0:WIDTH] += sum(
                dot(with_ones(feeds[k][b]), error[b], (1, 1)) for b in both
            )
            weight = w_inner[k - 1] if k else w_first[...]
            carried = [dot(weight, error[b]) for b in both]
        half = SHARE // 2
        for b in both:
            outcome = residue[b] + carried[b]
            packed = jnp.concatenate([outcome[:, :half], outcome[:, half:]], axis=0)
            answer[GROUP * turn + b] = packed.T.astype(BF16)

        @pl.when(turn > 0)
        def _():
            returning(GROUP * turn).start()

        for b in range(1, GROUP):
            returning(GROUP * turn + b).start()
        return carry

    lax.fori_loop(0, SUBS // GROUP, some_blocks, 0)

    last_bias = jnp.where(same_lev, total[FIRST_LAST:, WIDTH : WIDTH + 1], 0.0)
    total[LAST_BIAS : LAST_BIAS + 1, 0:LEV] = jnp.sum(last_bias, axis=0, keepdims=True)
    upper_low = lanes((UPPER, LANES)) < LEV
    wide[0:GRAD_ROWS, :] = total[:, 0:LANES].astype(BF16)
    wide[GRAD_ROWS:, :] = jnp.where(
        upper_low, total[0:UPPER, LANES:], pltpu.roll(total[UPPER:, LANES:], LEV, 1)
    ).astype(BF16)

    def part(j):
        owner = wrapped(tile, j, TILES)
        first = pl.multiple_of(owner * CHUNK, CHUNK)
        return remote(
            wide.at[pl.ds(first, CHUNK)], parts.at[j], part_sem.at[j], part_in_sem.at[j], (owner, sub)
        )

    def share_of(j):
        return remote(
            whole.at[0], whole.at[j], whole_sem.at[j], whole_in_sem.at[j], (wrapped(tile, j, TILES), sub)
        )

    for j in range(1, TILES):
        part(j).start()

    def unpack(j, source):
        block = source.astype(F32)
        first = pl.multiple_of(j * SHARE, SHARE)
        rows[pl.ds(first, SHARE // 2), :] = block
        rows[pl.ds(first + SHARE // 2, SHARE // 2), :] = pltpu.roll(block, LEV, 1)

    unpack(0, answer[0])

    def take(j, carry):
        returning(j).wait_recv()
        unpack(j, back[j])
        return carry

    lax.fori_loop(1, SUBS, take, 0)

    left_half = lanes((CY, LANES)) < LEV
    grads = (grads_even, grads_odd)

    def home(first_slabs):
        for held, x in zip(grads, first_slabs):
            for line in range(4):
                gathered(1, x * 2 + line, rows, held.at[line])
        for held, x in zip(grads, first_slabs):
            slab = [held[2 * k : 2 * k + 2].reshape(CY, LANES) for k in range(2)]
            turned = jnp.where(left_half, slab[0], pltpu.roll(slab[1], LEV, 1)).T
            for k in range(2):
                field[x + k + 2, :, 0:CY] = turned[k * LEV : (k + 1) * LEV]

    ghalos = []

    def home_row(line, k):
        return rows[pl.ds(routes[1, line, k], 1), :]

    for corner in range(4):
        line = (0 if corner < 2 else 2 * CX - 2) + corner % 2
        gcs[corner, 0:1, :] = home_row(line, (LANES - 1) * (corner % 2))
        ghalos.append(halo("c", corner, gcs, gcr, ghalo_sem, ghalo_in_sem))
        ghalos[-1].start()
    edges[2 * 2 * CX :, :] = jnp.zeros((LANES - 4 * CX, LANES), F32)
    for side in range(2):
        taken = [
            home_row(2 * x + side, (LANES - 2) * side + k) for x in range(CX) for k in range(2)
        ]
        for k in range(2 * CX):
            edges[2 * CX * side + k : 2 * CX * side + k + 1, :] = taken[k]
    turned_edges = edges[...].T[0:LEV, :]
    for side in range(2):
        moved = pltpu.roll(turned_edges, LANES - 2 * CX, 1) if side else turned_edges
        gys[side] = moved.astype(BF16)
        ghalos.append(halo("y", side, gys, gyr, ghalo_sem, ghalo_in_sem))
        ghalos[-1].start()

    home((0, CX - 2))
    for side in range(2):
        x = 0 if side == 0 else CX - 2
        for k in range(2):
            gxs[side, k * LEV : (k + 1) * LEV, :] = field[x + k + 2, :, 0:CY].astype(BF16)
        ghalos.append(halo("x", side, gxs, gxr, ghalo_sem, ghalo_in_sem))
        ghalos[-1].start()

    mine = pl.multiple_of(tile * CHUNK, CHUNK)
    summed = wide[pl.ds(mine, CHUNK), :].astype(F32)
    for j in range(1, TILES):
        part(j).wait_recv()
        summed = summed + parts[j].astype(F32)
    whole[0] = summed.astype(BF16)
    for j in range(1, TILES):
        share_of(j).start()

    def home_pairs(turn, carry):
        home((4 * turn + 2, 4 * turn + 4))
        return carry

    lax.fori_loop(0, CX // 4 - 1, home_pairs, 0)
    for copy in ghalos:
        copy.wait_recv()
    spread_halo(gxr, gyr, gcr)

    def adjoint(ref, slab):
        rate = [rates[pl.ds(slab + k, 1), :] for k in (-1, 0, 1)]
        now = ref[slab]
        flow = rate[1] * now
        near = rate[0] * ref[slab - 1] + rate[2] * ref[slab + 1] + near_sum(flow)
        return now + (near - 4.0 * flow)

    def adjoint_first(pair, carry):
        done = [adjoint(field, 2 * pair + k) for k in (1, 2)]
        for k in (1, 2):
            middle[2 * pair + k] = done[k - 1]
        return carry

    lax.fori_loop(0, CX // 2 + 1, adjoint_first, 0)

    def adjoint_second(pair, carry):
        done = [adjoint(middle, 2 * pair + k + 2) for k in range(2)]
        for k in range(2):
            for h in range(2):
                row = tiled_row(2 * pair + k, h)
                result[pl.ds(row, LEV, stride=2 * CX), :] = done[k][:, h * LANES : (h + 1) * LANES]
        return carry

    lax.fori_loop(0, CX // 2, adjoint_second, 0)

    stores[0].start()
    for j in range(1, TILES):
        share_of(j).wait_recv()
    for j in range(TILES):
        owner = wrapped(tile, -j, TILES)
        flat[pl.ds(pl.multiple_of(owner * CHUNK, CHUNK), CHUNK), :] = whole[j].astype(F32)
    everything = flat[...]
    total[:, 0:LANES] = flat[0:GRAD_ROWS, :]
    total[0:UPPER, LANES:] = flat[GRAD_ROWS:, :]
    total[UPPER:, LANES:] = pltpu.roll(flat[GRAD_ROWS:, :], LEV, 1)
    squares = jnp.sum(jnp.sum(everything * everything, axis=0, keepdims=True), axis=1, keepdims=True)
    factor = lax.rsqrt(squares / PARAMS + 1e-06)
    step_first[...] = total[0:LEV, 0:WIDTH] * factor
    step_bias_inner[0:1, :] = total[LEV : LEV + 1, 0:WIDTH] * factor
    for k in range(3):
        row = FIRST_INNER + k * (WIDTH + AUG)
        step_inner[k] = total[row : row + WIDTH, 0:WIDTH] * factor
        step_bias_inner[k + 1 : k + 2, :] = total[row + WIDTH : row + WIDTH + 1, 0:WIDTH] * factor
    step_last_t[...] = total[FIRST_LAST:, 0:WIDTH] * factor
    step_bias_last[...] = total[LAST_BIAS : LAST_BIAS + 1, 0:LEV] * factor
    for store in stores[1:]:
        store.start()


    def settle(j, carry):
        outgoing(j).wait_send()
        returning(j).wait_send()
        return carry

    lax.fori_loop(1, SUBS, settle, 0)
    for j in range(1, TILES):
        part(j).wait_send()
        share_of(j).wait_send()
    for copy in copies + ghalos:
        copy.wait_send()
    for store in stores:
        store.wait()


def copy_kernel(*refs):
    sources, targets, held = refs[0:6], refs[6:12], refs[12:18]
    in_sem, out_sem = refs[18:]
    piece = LEV * CX * 2 // 4
    places = [(0, pl.ds(k * piece, piece)) for k in range(4)] + [(k, slice(None)) for k in range(1, 6)]
    loads, stores = [], []
    for k, (which, rows) in enumerate(places):
        source, middle, target = (group[which].at[rows] for group in (sources, held, targets))
        loads.append(pltpu.make_async_copy(source, middle, in_sem.at[k]))
        stores.append(pltpu.make_async_copy(middle, target, out_sem.at[k]))
    for load in loads:
        load.start()
    for load, store in zip(loads, stores):
        load.wait()
        store.start()
    for store in stores:
        store.wait()


def both_ways(shape, kind):
    return [pltpu.VMEM(shape, kind), pltpu.VMEM(shape, kind)]


def per_device(
    initial, targets, diffusivity, column_order, send_counts, w_first, w_inner, w_last, b_inner, b_last
):
    slabs = pltpu.VMEM((SLABS, LEV, SPAN), F32)
    made = pl.pallas_call(
        step_kernel,
        out_shape=(
            jax.ShapeDtypeStruct((LEV * CX * 2, LANES), F32),
            jax.ShapeDtypeStruct((LEV, WIDTH), F32),
            jax.ShapeDtypeStruct((3, WIDTH, WIDTH), F32),
            jax.ShapeDtypeStruct((LEV, WIDTH), F32),
            jax.ShapeDtypeStruct((4, WIDTH), F32),
            jax.ShapeDtypeStruct((1, LEV), F32),
        ),
        in_specs=[ANY] * 10,
        out_specs=(ANY,) * 6,
        scratch_shapes=[
            pltpu.VMEM((LEV * CX * 2, LANES), F32),
            pltpu.VMEM((LEV * CX * 2, LANES), F32),
            pltpu.VMEM((CX, CY), F32),
            pltpu.VMEM((1, NCOL), jnp.int32),
            pltpu.VMEM((1, TILES * SUBS), jnp.int32),
            pltpu.VMEM((LEV, WIDTH), BF16),
            pltpu.VMEM((3, WIDTH, WIDTH), BF16),
            pltpu.VMEM((LEV, WIDTH), BF16),
            pltpu.VMEM((4, WIDTH), F32),
            pltpu.VMEM((1, LEV), F32),
            pltpu.VMEM((LEV * CX * 2, LANES), F32),
            pltpu.VMEM((LEV, WIDTH), F32),
            pltpu.VMEM((3, WIDTH, WIDTH), F32),
            pltpu.VMEM((LEV, WIDTH), F32),
            pltpu.VMEM((4, WIDTH), F32),
            pltpu.VMEM((1, LEV), F32),
            pltpu.SemaphoreType.DMA((10,)),
            pltpu.SemaphoreType.DMA((6,)),
            slabs,
            slabs,
            pltpu.VMEM((24, SPAN), F32),
            pltpu.VMEM((NCOL, LANES), F32),
            pltpu.VMEM((2, NCOL // LANES, LANES), jnp.int32),
            pltpu.SMEM((2, NCOL // LANES, LANES), jnp.int32),
        ]
        + both_ways((2, 2 * LEV + 2 * CX, CY), BF16)
        + both_ways((2, LEV + 2 * CX, LANES), BF16)
        + both_ways((4, 8, LANES), F32)
        + both_ways((2, 2 * LEV, CY), BF16)
        + both_ways((2, LEV, LANES), BF16)
        + both_ways((4, 8, LANES), F32)
        + [
            pltpu.VMEM((WIDTH, LEV), BF16),
            pltpu.VMEM((3, WIDTH, WIDTH), BF16),
            pltpu.VMEM((WIDTH, LEV), BF16),
            pltpu.VMEM((5, WIDTH, 1), F32),
            pltpu.VMEM((2, LANES, LANES), F32),
        ]
        + both_ways((SUBS, SHARE, LANES), BF16)
        + both_ways((SUBS, SHARE // 2, LANES), BF16)
        + [
            pltpu.VMEM((NCOL, LANES), F32),
            pltpu.VMEM((4, LANES, LANES), F32),
            pltpu.VMEM((4, LANES, LANES), F32),
            pltpu.VMEM((LANES, LANES), F32),
            pltpu.VMEM((GRAD_ROWS, 256), F32),
            pltpu.VMEM((PACKED_ROWS, LANES), BF16),
            pltpu.VMEM((PACKED_ROWS, LANES), F32),
        ]
        + both_ways((TILES, CHUNK, LANES), BF16)
        + [pltpu.SemaphoreType.DMA((2,))]
        + [pltpu.SemaphoreType.DMA((8,))] * 4
        + [pltpu.SemaphoreType.DMA((SUBS,))] * 4
        + [pltpu.SemaphoreType.DMA((TILES,))] * 4,
        compiler_params=pltpu.CompilerParams(
            collective_id=0, has_side_effects=True, vmem_limit_bytes=LIMIT
        ),
        name="step",
    )(
        tiled(initial),
        tiled(targets),
        diffusivity,
        column_order,
        send_counts,
        w_first[0],
        w_inner[0],
        w_last[0].T,
        b_inner[0],
        b_last,
    )
    result, step_first, step_inner, step_last_t, step_bias_inner, step_bias_last = pl.pallas_call(
        copy_kernel,
        out_shape=tuple(jax.ShapeDtypeStruct(one.shape, one.dtype) for one in made),
        in_specs=[ANY] * 6,
        out_specs=(ANY,) * 6,
        scratch_shapes=[pltpu.VMEM(one.shape, one.dtype) for one in made]
        + [pltpu.SemaphoreType.DMA((9,))] * 2,
        name="finish",
    )(*made)
    return (
        untiled(result),
        step_first[None],
        step_inner[None],
        step_last_t.T[None],
        step_bias_inner[None],
        step_bias_last,
    )


def solution(mesh):
    placed = (
        P(None, "tile", "sub"),
        P(None, "tile", "sub"),
        P("tile", "sub"),
        P(("tile", "sub"), None),
        P(("tile", "sub"), None),
        P("sub", None, None),
        P("sub", None, None, None),
        P("sub", None, None),
        P("sub", None, None),
        P("sub", None),
    )
    return jax.shard_map(
        per_device,
        mesh=mesh,
        in_specs=placed,
        out_specs=(
            P(None, "tile", "sub"),
            P("sub", None, None),
            P("sub", None, None, None),
            P("sub", None, None),
            P("sub", None, None),
            P("sub", None),
        ),
        check_vma=False,
    )
```

```python
import jax
import jax.numpy as jnp
from jax import lax
from jax.experimental import pallas as pl
from jax.experimental.pallas import tpu as pltpu
from jax.sharding import PartitionSpec as P

MESH = pl.DeviceIdType.MESH
F32 = jnp.float32
BF16 = jnp.bfloat16
LEV = 64
WIDTH = 192
CX = 16
CY = 256
NCOL = CX * CY
TILES = 8
SUBS = 16
SHARE = NCOL // SUBS
PARAMS = 136000
AUG = 16
LANES = 128
SPAN = CY + LANES
SLABS = CX + 4
CHUNK = 144
GRAD_ROWS = 768
UPPER = GRAD_ROWS // 2
PACKED_ROWS = CHUNK * TILES
LAST_BIAS = LEV + 2
GROUP = 4
FIRST_INNER = LEV + AUG
FIRST_LAST = FIRST_INNER + 3 * (WIDTH + AUG)
ANY = pl.BlockSpec(memory_space=pl.ANY)
LIMIT = 58 * 2**20


def wrapped(index, step, count):
    return lax.rem(index + step + count, count)


def remote(source, target, send_sem, recv_sem, peer):
    return pltpu.make_async_remote_copy(
        src_ref=source,
        dst_ref=target,
        send_sem=send_sem,
        recv_sem=recv_sem,
        device_id=peer,
        device_id_type=MESH,
    )


PAIRS = ((0, 0), (2, 0), (1, 0), (3, 0), (2, 1), (1, 1), (3, 1), (0, 1))


def crossing(j):
    late = jnp.minimum(j // 2, 1)
    return late * (1 - j % 2) + (1 - late) * (j % 2)


def partner(tile, sub, j, sign):
    turned = crossing(j)
    x = sum(jnp.where(j // 2 == k, pair[0], 0) for k, pair in enumerate(PAIRS))
    core = sum(jnp.where(j // 2 == k, pair[1], 0) for k, pair in enumerate(PAIRS))
    high = (sub // 8 + turned) % 2
    middle = (sub // 2 + sign * x + 4) % 4
    return (tile + 4 * turned) % TILES, high * 8 + middle * 2 + (sub + core) % 2


def place_of(sub, other):
    turned = (other // 8 + sub // 8) % 2
    x = (other // 2 - sub // 2 + 8) % 4
    core = (other + sub) % 2
    step = sum(
        jnp.where((x == pair[0]) & (core == pair[1]), k, 0) for k, pair in enumerate(PAIRS)
    )
    late = jnp.minimum(step, 1)
    return 2 * step + late * (1 - turned) + (1 - late) * turned


def tiled(block):
    return block.reshape(LEV, CX // 8, 8, 2, LANES).transpose(0, 1, 3, 2, 4).reshape(-1, LANES)


def untiled(rows):
    return rows.reshape(LEV, CX // 8, 2, 8, LANES).transpose(0, 1, 3, 2, 4).reshape(LEV, CX, CY)


def tiled_row(x, half):
    return (x // 8) * 16 + half * 8 + x % 8


def lanes(shape):
    return lax.broadcasted_iota(jnp.int32, shape, 1)


def sublanes(shape):
    return lax.broadcasted_iota(jnp.int32, shape, 0)


def dot(left, right, contract=(1, 0)):
    return lax.dot_general(
        left, right, (((contract[0],), (contract[1],)), ((), ())), preferred_element_type=F32
    )


def near_sum(value):
    return pltpu.roll(value, 1, 1) + pltpu.roll(value, SPAN - 1, 1)


def silu_and_slope(preact):
    sigmoid_value = 0.5 + 0.5 * jnp.tanh(0.5 * preact)
    active = preact * sigmoid_value
    return active.astype(BF16), sigmoid_value + active * (1.0 - sigmoid_value)


def find_routes(order, counts, sub, routes, tables, sems):
    count_row = counts[...]
    square = (TILES * SUBS, TILES * SUBS)
    earlier = lanes(square)

    def starts_and_shift(device):
        before = earlier < device
        same = earlier % SUBS == device % SUBS
        start = jnp.sum(jnp.where(before, count_row, 0), axis=1, keepdims=True)
        within = jnp.sum(jnp.where(before & same, count_row, 0), axis=1, keepdims=True)
        block = place_of(sub, device[:, 0:1] % SUBS)
        return start, block * SHARE + within - start

    device = sublanes(square)
    start, shift = starts_and_shift(device)
    _, shift_before = starts_and_shift(jnp.maximum(device - 1, 0))
    change = shift - jnp.where(device[:, 0:1] == 0, 0, shift_before)
    width = 512
    outward = jnp.zeros((32, 256), F32)
    homeward = jnp.zeros((32, 256), F32)

    def spread(where, what):
        high = (sublanes((32, width)) == where // LANES).astype(F32).astype(BF16)
        hit = sublanes((LANES, width)) == where % LANES
        values = jnp.concatenate(
            [jnp.where(hit, what // LANES, 0), jnp.where(hit, what % LANES, 0)], axis=0
        )
        return dot(high, values.astype(F32).astype(BF16), (1, 1))

    for first in range(0, NCOL, width):
        place = lanes((1, width)) + first
        slot = place + jnp.sum(jnp.where(start <= place, change, 0), axis=0, keepdims=True)
        column = order[:, first : first + width]
        outward = outward + spread(slot, column)
        homeward = homeward + spread(column, slot)
    for k, table in enumerate((outward, homeward)):
        whole = table.astype(jnp.int32)
        tables[k] = jnp.clip(whole[:, 0:LANES] * LANES + whole[:, LANES:], 0, NCOL - 1)
    for k in range(2):
        copy = pltpu.make_async_copy(tables.at[k], routes.at[k], sems.at[k])
        copy.start()
        copy.wait()


def step_kernel(
    initial_hbm, targets_hbm, diffusivity_hbm, order_hbm, counts_hbm,
    w_first_hbm, w_inner_hbm, w_last_hbm, b_inner_hbm, b_last_hbm,
    result_hbm, step_first_hbm, step_inner_hbm, step_last_hbm, step_bias_inner_hbm, step_bias_last_hbm,
    initial, targets, diffusivity, order, counts, w_first, w_inner, w_last_t, b_inner, b_last,
    result, step_first, step_inner, step_last_t, step_bias_inner, step_bias_last,
    load_sem, store_sem,
    field, middle, rates, columns, tables, routes,
    xs, xr, ys, yr, cs, cr, gxs, gxr, gys, gyr, gcs, gcr,
    wt_first, wt_inner, w_last, bias,
    stage, send, recv, answer, back, rows, grads_even, grads_odd, edges, total, wide, flat, parts, whole,
    table_sem, halo_sem, halo_in_sem, ghalo_sem, ghalo_in_sem,
    out_sem, in_sem, ret_sem, back_sem, part_sem, part_in_sem, whole_sem, whole_in_sem,
):
    tile, sub = lax.axis_index("tile"), lax.axis_index("sub")
    up, down = wrapped(tile, 1, TILES), wrapped(tile, -1, TILES)
    right, left = wrapped(sub, 1, SUBS), wrapped(sub, -1, SUBS)
    around = (
        (down, sub), (up, sub), (tile, left), (tile, right),
        (down, left), (down, right), (up, left), (up, right),
    )
    peers = (
        [partner(tile, sub, j, 1) for j in range(1, SUBS)]
        + [(wrapped(tile, j, TILES), sub) for j in range(1, TILES)]
        + list(around[2:])
    )
    loads = [
        pltpu.make_async_copy(source, target, load_sem.at[k])
        for k, (source, target) in enumerate(
            (
                (initial_hbm, initial), (diffusivity_hbm, diffusivity), (order_hbm, order),
                (counts_hbm, counts), (w_first_hbm, w_first), (w_inner_hbm, w_inner),
                (w_last_hbm, w_last_t), (b_inner_hbm, b_inner), (b_last_hbm, b_last),
                (targets_hbm, targets),
            )
        )
    ]
    for load in loads:
        load.start()
    barrier = pltpu.get_barrier_semaphore()
    for peer in peers:
        pl.semaphore_signal(barrier, inc=1, device_id=peer, device_id_type=MESH)
    stores = [
        pltpu.make_async_copy(source, target, store_sem.at[k])
        for k, (source, target) in enumerate(
            (
                (result, result_hbm), (step_first, step_first_hbm), (step_inner, step_inner_hbm),
                (step_last_t, step_last_hbm), (step_bias_inner, step_bias_inner_hbm),
                (step_bias_last, step_bias_last_hbm),
            )
        )
    ]

    def cells(ref, x):
        return jnp.concatenate(
            [ref[pl.ds(tiled_row(x, h), LEV, stride=2 * CX), :] for h in range(2)], axis=1
        )

    def halo(group, k, sends, receives, out_sems, in_sems):
        place = {"x": k, "y": 2 + k, "c": 4 + k}[group]
        other = (3 - k) if group == "c" else (1 - k)
        opposite = place - k + other
        return remote(
            sends.at[k], receives.at[other], out_sems.at[place], in_sems.at[opposite], around[place]
        )

    def strip(tile_of, side):
        pair = lanes((LEV, LANES)) // 2
        packed = jnp.zeros((LEV, LANES), F32)
        for x in range(CX):
            moved = tile_of(x, side)
            shift = (2 * x + 2 * side) % LANES
            if shift:
                moved = pltpu.roll(moved, shift, 1)
            packed = jnp.where(pair == x, moved, packed)
        return packed

    def edge_tile(x, side):
        return field[x + 2, :, side * LANES : (side + 1) * LANES]

    low = lanes((LEV, LANES)) < LEV

    def halo_tile(from_left, from_right, x):
        back_right = pltpu.roll(from_right, LANES - 2 * x, 1) if x else from_right
        return jnp.where(low, back_right, pltpu.roll(from_left, LANES - 2 - 2 * x, 1))

    def fill(x, carry):
        field[x + 2, :, 0:CY] = cells(initial, x)
        return carry

    loads[0].wait()
    loads[1].wait()
    for x in (0, 1, CX - 2, CX - 1):
        fill(x, 0)
    rate_high = diffusivity[...].astype(BF16)
    rate_parts = (rate_high, (diffusivity[...] - rate_high.astype(F32)).astype(BF16))
    same_lev = sublanes((LEV, LEV)) == lanes((LEV, LEV))
    for side in range(2):
        for k in range(2):
            edge = field[2 + (k if side == 0 else CX - 2 + k), :, 0:CY]
            xs[side, k * LEV : (k + 1) * LEV, :] = edge.astype(BF16)
        for k in range(2):
            xs[side, 2 * LEV + k * CX : 2 * LEV + (k + 1) * CX, :] = rate_parts[k]
    for corner in range(4):
        side, edge = corner // 2, corner % 2
        x = 0 if side == 0 else CX - 1
        y = edge * (CY - 1)
        cell = jnp.where(same_lev, field[x + 2, :, y : y + 1], 0.0)
        cs[corner, 0:1, 0:LEV] = jnp.sum(cell, axis=0, keepdims=True)
        cs[corner, 1:2, :] = diffusivity[x : x + 1, edge * LANES : (edge + 1) * LANES]
    pl.semaphore_wait(barrier, len(peers))
    copies = []
    for side in range(2):
        copies.append(halo("x", side, xs, xr, halo_sem, halo_in_sem))
        copies[-1].start()
    for corner in range(4):
        copies.append(halo("c", corner, cs, cr, halo_sem, halo_in_sem))
        copies[-1].start()
    lax.fori_loop(2, CX - 2, fill, 0)
    for side in range(2):
        ys[side, 0:LEV, :] = strip(edge_tile, side).astype(BF16)
        for k in range(2):
            part_rows = rate_parts[k][:, side * LANES : (side + 1) * LANES]
            ys[side, LEV + k * CX : LEV + (k + 1) * CX, :] = part_rows
        copies.append(halo("y", side, ys, yr, halo_sem, halo_in_sem))
        copies[-1].start()

    for load in loads[2:]:
        load.wait()
    find_routes(order, counts, sub, routes, tables, table_sem)
    for copy in copies:
        copy.wait_recv()
    def arrived_rates(message, first):
        high, rest = (message[first + k * CX : first + (k + 1) * CX, :].astype(F32) for k in range(2))
        return high + rest

    rates[0:2, 0:CY] = arrived_rates(xr.at[0], 2 * LEV)[CX - 2 :, :]
    rates[2 : CX + 2, 0:CY] = diffusivity[...]
    rates[CX + 2 : CX + 4, 0:CY] = arrived_rates(xr.at[1], 2 * LEV)[0:2, :]
    first_rows = lanes((CX, LANES)) < LEV
    rates[0:8, CY:] = jnp.zeros((8, LANES), F32)
    rates[16:24, CY:] = jnp.zeros((8, LANES), F32)
    rates[2 : CX + 2, CY:] = jnp.where(
        first_rows, arrived_rates(yr.at[1], LEV), arrived_rates(yr.at[0], LEV)
    )
    one_row = lanes((1, LANES)) < LEV
    rates[1:2, CY:] = jnp.where(one_row, cr[1, 1:2, :], cr[0, 1:2, :])
    rates[CX + 2 : CX + 3, CY:] = jnp.where(one_row, cr[3, 1:2, :], cr[2, 1:2, :])

    def spread_halo(x_in, y_in, c_in):
        for side in range(2):
            for k in range(2):
                slab = k if side == 0 else CX + 2 + k
                field[slab, :, 0:CY] = x_in[side, k * LEV : (k + 1) * LEV, :].astype(F32)
            outer = 0 if side == 0 else CX + 3
            field[outer, :, CY:] = jnp.zeros((LEV, LANES), F32)
            inner = 1 if side == 0 else CX + 2
            cell = [
                jnp.sum(jnp.where(same_lev, c_in[2 * side + k, 0:1, 0:LEV], 0.0), axis=1, keepdims=True)
                for k in range(2)
            ]
            field[inner, :, CY:] = jnp.where(low, cell[1], cell[0])
        from_left, from_right = y_in[0, 0:LEV, :].astype(F32), y_in[1, 0:LEV, :].astype(F32)
        for x in range(CX):
            field[x + 2, :, CY:] = halo_tile(from_left, from_right, x)

    spread_halo(xr, yr, cr)

    def diffused(ref, slab):
        now = ref[slab]
        near = ref[slab - 1] + ref[slab + 1] + near_sum(now)
        return now + rates[pl.ds(slab, 1), :] * (near - 4.0 * now)

    def forward_first(pair, carry):
        done = [diffused(field, 2 * pair + k) for k in (1, 2)]
        for k in (1, 2):
            middle[2 * pair + k] = done[k - 1]
        return carry

    lax.fori_loop(0, CX // 2 + 1, forward_first, 0)

    def forward_second(pair, carry):
        for x in (2 * pair, 2 * pair + 1):
            later = diffused(middle, x + 2)[:, 0:CY]
            both = jnp.concatenate([later, later - cells(targets, x)], axis=0)
            columns[pl.ds(pl.multiple_of(x * CY, CY), CY), :] = both.T
        return carry

    lax.fori_loop(0, CX // 2, forward_second, 0)

    def outgoing(j):
        return remote(send.at[j], recv.at[j], out_sem.at[j], in_sem.at[j], partner(tile, sub, j, 1))

    def returning(j):
        return remote(answer.at[j], back.at[j], ret_sem.at[j], back_sem.at[j], partner(tile, sub, j, -1))

    def gathered(table, line, source, target):
        for first in range(0, LANES, 16):
            taken = [source[pl.ds(routes[table, line, first + k], 1), :] for k in range(16)]
            for k in range(16):
                target[first + k : first + k + 1, :] = taken[k]

    def push(step, carry):
        j = lax.rem(step, SUBS)
        for half in range(2):
            gathered(0, 2 * j + half, columns, stage.at[half])
        send[j] = stage[...].reshape(SHARE, LANES).astype(BF16)

        @pl.when(j > 0)
        def _():
            outgoing(j).start()

        return carry

    lax.fori_loop(1, SUBS + 1, push, 0)
    recv[0] = send[0]

    same = sublanes((WIDTH, WIDTH)) == lanes((WIDTH, WIDTH))
    unit = same.astype(F32).astype(BF16)
    wt_first[...] = dot(unit, w_first[...], (1, 1)).astype(BF16)
    for k in range(3):
        wt_inner[k] = dot(unit, w_inner[k], (1, 1)).astype(BF16)
    w_last[...] = dot(unit, w_last_t[...], (1, 1)).astype(BF16)
    for k in range(4):
        bias[k] = jnp.sum(jnp.where(same, b_inner[k : k + 1, :], 0.0), axis=1, keepdims=True)
    bias[4, 0:LEV, :] = jnp.sum(jnp.where(same_lev, b_last[...], 0.0), axis=1, keepdims=True)
    total[...] = jnp.zeros_like(total)

    extra = (sublanes((AUG, SHARE)) == 0).astype(F32).astype(BF16)

    def with_ones(value):
        return jnp.concatenate([value, extra], axis=0)

    def some_blocks(turn, carry):
        @pl.when(turn > 0)
        def _():
            outgoing(GROUP * turn).wait_recv()

        for b in range(1, GROUP):
            outgoing(GROUP * turn + b).wait_recv()
        both = range(GROUP)
        turned = [recv[GROUP * turn + b].astype(F32).T for b in both]
        inputs = [turned[b][:LEV].astype(BF16) for b in both]
        current = inputs
        feeds, slopes = [inputs], []
        for k in range(4):
            weight = wt_first[...] if k == 0 else wt_inner[k - 1]
            outs = [silu_and_slope(dot(weight, current[b]) + bias[k]) for b in both]
            current = [outs[b][0] for b in both]
            feeds.append(current)
            slopes.append([outs[b][1] for b in both])
        residue = [
            turned[b][LEV:] + dot(w_last_t[...], current[b]) + bias[4, 0:LEV, :] for b in both
        ]
        error = [residue[b].astype(BF16) for b in both]
        total[FIRST_LAST:, 0 : WIDTH + AUG] += sum(
            dot(error[b], with_ones(current[b]), (1, 1)) for b in both
        )
        carried = [dot(w_last[...], error[b]) for b in both]
        for k in (3, 2, 1, 0):
            error = [(carried[b] * slopes[k][b]).astype(BF16) for b in both]
            row = FIRST_INNER + (k - 1) * (WIDTH + AUG) if k else 0
            high = (WIDTH if k else LEV) + AUG
            total[row : row + high, 0:WIDTH] += sum(
                dot(with_ones(feeds[k][b]), error[b], (1, 1)) for b in both
            )
            weight = w_inner[k - 1] if k else w_first[...]
            carried = [dot(weight, error[b]) for b in both]
        half = SHARE // 2
        for b in both:
            outcome = residue[b] + carried[b]
            packed = jnp.concatenate([outcome[:, :half], outcome[:, half:]], axis=0)
            answer[GROUP * turn + b] = packed.T.astype(BF16)

        @pl.when(turn > 0)
        def _():
            returning(GROUP * turn).start()

        for b in range(1, GROUP):
            returning(GROUP * turn + b).start()
        return carry

    lax.fori_loop(0, SUBS // GROUP, some_blocks, 0)

    last_bias = jnp.where(same_lev, total[FIRST_LAST:, WIDTH : WIDTH + 1], 0.0)
    total[LAST_BIAS : LAST_BIAS + 1, 0:LEV] = jnp.sum(last_bias, axis=0, keepdims=True)
    upper_low = lanes((UPPER, LANES)) < LEV
    wide[0:GRAD_ROWS, :] = total[:, 0:LANES].astype(BF16)
    wide[GRAD_ROWS:, :] = jnp.where(
        upper_low, total[0:UPPER, LANES:], pltpu.roll(total[UPPER:, LANES:], LEV, 1)
    ).astype(BF16)

    def part(j):
        owner = wrapped(tile, j, TILES)
        first = pl.multiple_of(owner * CHUNK, CHUNK)
        return remote(
            wide.at[pl.ds(first, CHUNK)], parts.at[j], part_sem.at[j], part_in_sem.at[j], (owner, sub)
        )

    def share_of(j):
        return remote(
            whole.at[0], whole.at[j], whole_sem.at[j], whole_in_sem.at[j], (wrapped(tile, j, TILES), sub)
        )

    for j in range(1, TILES):
        part(j).start()

    def unpack(j, source):
        block = source.astype(F32)
        first = pl.multiple_of(j * SHARE, SHARE)
        rows[pl.ds(first, SHARE // 2), :] = block
        rows[pl.ds(first + SHARE // 2, SHARE // 2), :] = pltpu.roll(block, LEV, 1)

    unpack(0, answer[0])

    def take(j, carry):
        returning(j).wait_recv()
        unpack(j, back[j])
        return carry

    lax.fori_loop(1, SUBS, take, 0)

    left_half = lanes((CY, LANES)) < LEV
    grads = (grads_even, grads_odd)

    def home(first_slabs):
        for held, x in zip(grads, first_slabs):
            for line in range(4):
                gathered(1, x * 2 + line, rows, held.at[line])
        for held, x in zip(grads, first_slabs):
            slab = [held[2 * k : 2 * k + 2].reshape(CY, LANES) for k in range(2)]
            turned = jnp.where(left_half, slab[0], pltpu.roll(slab[1], LEV, 1)).T
            for k in range(2):
                field[x + k + 2, :, 0:CY] = turned[k * LEV : (k + 1) * LEV]

    ghalos = []

    def home_row(line, k):
        return rows[pl.ds(routes[1, line, k], 1), :]

    for corner in range(4):
        line = (0 if corner < 2 else 2 * CX - 2) + corner % 2
        gcs[corner, 0:1, :] = home_row(line, (LANES - 1) * (corner % 2))
        ghalos.append(halo("c", corner, gcs, gcr, ghalo_sem, ghalo_in_sem))
        ghalos[-1].start()
    edges[2 * 2 * CX :, :] = jnp.zeros((LANES - 4 * CX, LANES), F32)
    for side in range(2):
        taken = [
            home_row(2 * x + side, (LANES - 2) * side + k) for x in range(CX) for k in range(2)
        ]
        for k in range(2 * CX):
            edges[2 * CX * side + k : 2 * CX * side + k + 1, :] = taken[k]
    turned_edges = edges[...].T[0:LEV, :]
    for side in range(2):
        moved = pltpu.roll(turned_edges, LANES - 2 * CX, 1) if side else turned_edges
        gys[side] = moved.astype(BF16)
        ghalos.append(halo("y", side, gys, gyr, ghalo_sem, ghalo_in_sem))
        ghalos[-1].start()

    home((0, CX - 2))
    for side in range(2):
        x = 0 if side == 0 else CX - 2
        for k in range(2):
            gxs[side, k * LEV : (k + 1) * LEV, :] = field[x + k + 2, :, 0:CY].astype(BF16)
        ghalos.append(halo("x", side, gxs, gxr, ghalo_sem, ghalo_in_sem))
        ghalos[-1].start()

    mine = pl.multiple_of(tile * CHUNK, CHUNK)
    summed = wide[pl.ds(mine, CHUNK), :].astype(F32)
    for j in range(1, TILES):
        part(j).wait_recv()
        summed = summed + parts[j].astype(F32)
    whole[0] = summed.astype(BF16)
    for j in range(1, TILES):
        share_of(j).start()

    def home_pairs(turn, carry):
        home((4 * turn + 2, 4 * turn + 4))
        return carry

    lax.fori_loop(0, CX // 4 - 1, home_pairs, 0)
    for copy in ghalos:
        copy.wait_recv()
    spread_halo(gxr, gyr, gcr)

    def adjoint(ref, slab):
        rate = [rates[pl.ds(slab + k, 1), :] for k in (-1, 0, 1)]
        now = ref[slab]
        flow = rate[1] * now
        near = rate[0] * ref[slab - 1] + rate[2] * ref[slab + 1] + near_sum(flow)
        return now + (near - 4.0 * flow)

    def adjoint_first(pair, carry):
        done = [adjoint(field, 2 * pair + k) for k in (1, 2)]
        for k in (1, 2):
            middle[2 * pair + k] = done[k - 1]
        return carry

    lax.fori_loop(0, CX // 2 + 1, adjoint_first, 0)

    def adjoint_second(pair, carry):
        done = [adjoint(middle, 2 * pair + k + 2) for k in range(2)]
        for k in range(2):
            for h in range(2):
                row = tiled_row(2 * pair + k, h)
                result[pl.ds(row, LEV, stride=2 * CX), :] = done[k][:, h * LANES : (h + 1) * LANES]
        return carry

    lax.fori_loop(0, CX // 2, adjoint_second, 0)

    stores[0].start()
    for j in range(1, TILES):
        share_of(j).wait_recv()
    for j in range(TILES):
        owner = wrapped(tile, -j, TILES)
        flat[pl.ds(pl.multiple_of(owner * CHUNK, CHUNK), CHUNK), :] = whole[j].astype(F32)
    everything = flat[...]
    total[:, 0:LANES] = flat[0:GRAD_ROWS, :]
    total[0:UPPER, LANES:] = flat[GRAD_ROWS:, :]
    total[UPPER:, LANES:] = pltpu.roll(flat[GRAD_ROWS:, :], LEV, 1)
    squares = jnp.sum(jnp.sum(everything * everything, axis=0, keepdims=True), axis=1, keepdims=True)
    factor = lax.rsqrt(squares / PARAMS + 1e-06)
    step_first[...] = total[0:LEV, 0:WIDTH] * factor
    step_bias_inner[0:1, :] = total[LEV : LEV + 1, 0:WIDTH] * factor
    for k in range(3):
        row = FIRST_INNER + k * (WIDTH + AUG)
        step_inner[k] = total[row : row + WIDTH, 0:WIDTH] * factor
        step_bias_inner[k + 1 : k + 2, :] = total[row + WIDTH : row + WIDTH + 1, 0:WIDTH] * factor
    step_last_t[...] = total[FIRST_LAST:, 0:WIDTH] * factor
    step_bias_last[...] = total[LAST_BIAS : LAST_BIAS + 1, 0:LEV] * factor
    for store in stores[1:]:
        store.start()


    def settle(j, carry):
        outgoing(j).wait_send()
        returning(j).wait_send()
        return carry

    lax.fori_loop(1, SUBS, settle, 0)
    for j in range(1, TILES):
        part(j).wait_send()
        share_of(j).wait_send()
    for copy in copies + ghalos:
        copy.wait_send()
    for store in stores:
        store.wait()


def copy_kernel(*refs):
    sources, targets, held = refs[0:6], refs[6:12], refs[12:18]
    in_sem, out_sem = refs[18:]
    piece = LEV * CX * 2 // 4
    places = [(0, pl.ds(k * piece, piece)) for k in range(4)] + [(k, slice(None)) for k in range(1, 6)]
    loads, stores = [], []
    for k, (which, rows) in enumerate(places):
        source, middle, target = (group[which].at[rows] for group in (sources, held, targets))
        loads.append(pltpu.make_async_copy(source, middle, in_sem.at[k]))
        stores.append(pltpu.make_async_copy(middle, target, out_sem.at[k]))
    for load in loads:
        load.start()
    for load, store in zip(loads, stores):
        load.wait()
        store.start()
    for store in stores:
        store.wait()


def both_ways(shape, kind):
    return [pltpu.VMEM(shape, kind), pltpu.VMEM(shape, kind)]


def per_device(
    initial, targets, diffusivity, column_order, send_counts, w_first, w_inner, w_last, b_inner, b_last
):
    slabs = pltpu.VMEM((SLABS, LEV, SPAN), F32)
    made = pl.pallas_call(
        step_kernel,
        out_shape=(
            jax.ShapeDtypeStruct((LEV * CX * 2, LANES), F32),
            jax.ShapeDtypeStruct((LEV, WIDTH), F32),
            jax.ShapeDtypeStruct((3, WIDTH, WIDTH), F32),
            jax.ShapeDtypeStruct((LEV, WIDTH), F32),
            jax.ShapeDtypeStruct((4, WIDTH), F32),
            jax.ShapeDtypeStruct((1, LEV), F32),
        ),
        in_specs=[ANY] * 10,
        out_specs=(ANY,) * 6,
        scratch_shapes=[
            pltpu.VMEM((LEV * CX * 2, LANES), F32),
            pltpu.VMEM((LEV * CX * 2, LANES), F32),
            pltpu.VMEM((CX, CY), F32),
            pltpu.VMEM((1, NCOL), jnp.int32),
            pltpu.VMEM((1, TILES * SUBS), jnp.int32),
            pltpu.VMEM((LEV, WIDTH), BF16),
            pltpu.VMEM((3, WIDTH, WIDTH), BF16),
            pltpu.VMEM((LEV, WIDTH), BF16),
            pltpu.VMEM((4, WIDTH), F32),
            pltpu.VMEM((1, LEV), F32),
            pltpu.VMEM((LEV * CX * 2, LANES), F32),
            pltpu.VMEM((LEV, WIDTH), F32),
            pltpu.VMEM((3, WIDTH, WIDTH), F32),
            pltpu.VMEM((LEV, WIDTH), F32),
            pltpu.VMEM((4, WIDTH), F32),
            pltpu.VMEM((1, LEV), F32),
            pltpu.SemaphoreType.DMA((10,)),
            pltpu.SemaphoreType.DMA((6,)),
            slabs,
            slabs,
            pltpu.VMEM((24, SPAN), F32),
            pltpu.VMEM((NCOL, LANES), F32),
            pltpu.VMEM((2, NCOL // LANES, LANES), jnp.int32),
            pltpu.SMEM((2, NCOL // LANES, LANES), jnp.int32),
        ]
        + both_ways((2, 2 * LEV + 2 * CX, CY), BF16)
        + both_ways((2, LEV + 2 * CX, LANES), BF16)
        + both_ways((4, 8, LANES), F32)
        + both_ways((2, 2 * LEV, CY), BF16)
        + both_ways((2, LEV, LANES), BF16)
        + both_ways((4, 8, LANES), F32)
        + [
            pltpu.VMEM((WIDTH, LEV), BF16),
            pltpu.VMEM((3, WIDTH, WIDTH), BF16),
            pltpu.VMEM((WIDTH, LEV), BF16),
            pltpu.VMEM((5, WIDTH, 1), F32),
            pltpu.VMEM((2, LANES, LANES), F32),
        ]
        + both_ways((SUBS, SHARE, LANES), BF16)
        + both_ways((SUBS, SHARE // 2, LANES), BF16)
        + [
            pltpu.VMEM((NCOL, LANES), F32),
            pltpu.VMEM((4, LANES, LANES), F32),
            pltpu.VMEM((4, LANES, LANES), F32),
            pltpu.VMEM((LANES, LANES), F32),
            pltpu.VMEM((GRAD_ROWS, 256), F32),
            pltpu.VMEM((PACKED_ROWS, LANES), BF16),
            pltpu.VMEM((PACKED_ROWS, LANES), F32),
        ]
        + both_ways((TILES, CHUNK, LANES), BF16)
        + [pltpu.SemaphoreType.DMA((2,))]
        + [pltpu.SemaphoreType.DMA((8,))] * 4
        + [pltpu.SemaphoreType.DMA((SUBS,))] * 4
        + [pltpu.SemaphoreType.DMA((TILES,))] * 4,
        compiler_params=pltpu.CompilerParams(
            collective_id=0, has_side_effects=True, vmem_limit_bytes=LIMIT
        ),
        name="step",
    )(
        tiled(initial),
        tiled(targets),
        diffusivity,
        column_order,
        send_counts,
        w_first[0],
        w_inner[0],
        w_last[0].T,
        b_inner[0],
        b_last,
    )
    result, step_first, step_inner, step_last_t, step_bias_inner, step_bias_last = pl.pallas_call(
        copy_kernel,
        out_shape=tuple(jax.ShapeDtypeStruct(one.shape, one.dtype) for one in made),
        in_specs=[ANY] * 6,
        out_specs=(ANY,) * 6,
        scratch_shapes=[pltpu.VMEM(one.shape, one.dtype) for one in made]
        + [pltpu.SemaphoreType.DMA((9,))] * 2,
        name="finish",
    )(*made)
    return (
        untiled(result),
        step_first[None],
        step_inner[None],
        step_last_t.T[None],
        step_bias_inner[None],
        step_bias_last,
    )


def solution(mesh):
    placed = (
        P(None, "tile", "sub"),
        P(None, "tile", "sub"),
        P("tile", "sub"),
        P(("tile", "sub"), None),
        P(("tile", "sub"), None),
        P("sub", None, None),
        P("sub", None, None, None),
        P("sub", None, None),
        P("sub", None, None),
        P("sub", None),
    )
    return jax.shard_map(
        per_device,
        mesh=mesh,
        in_specs=placed,
        out_specs=(
            P(None, "tile", "sub"),
            P("sub", None, None),
            P("sub", None, None, None),
            P("sub", None, None),
            P("sub", None, None),
            P("sub", None),
        ),
        check_vma=False,
    )
```
